128 devices in a mesh: wide: 16 (over x_lo, y, core), narrow: 8 (over x_hi, z).
Axes of the slice: x: 4 (x_hi: 2, x_lo: 2; x = x_hi * 2 + x_lo), y: 4, z: 4, core: 2. Of those that a mesh axis runs over, the one named last changes fastest.
Arguments:
- tokens: bfloat16 [65536, 768], P(('wide', 'narrow')), may hold values from -6 to 6
- seq_lengths: int32 [128, 4], P(('wide', 'narrow')), may hold values from 0 to 512, as said below
- ln1_gain: bfloat16 [768], P(('wide', 'narrow')), may hold values from 0.25 to 1.75
- ln1_bias: bfloat16 [768], P(('wide', 'narrow')), may hold values from -3 to 3
- qkv_weight: bfloat16 [768, 2304], P(('wide', 'narrow')), may hold values from -0.21875 to 0.21875
- out_weight: bfloat16 [768, 768], P(('wide', 'narrow')), may hold values from -0.4375 to 0.4375
- ln2_gain: bfloat16 [768], P(('wide', 'narrow')), may hold values from 0.25 to 1.75
- ln2_bias: bfloat16 [768], P(('wide', 'narrow')), may hold values from -3 to 3
- up_weight: bfloat16 [768, 3072], P(None, ('wide', 'narrow')), may hold values from -0.21875 to 0.21875
- down_weight: bfloat16 [3072, 768], P(('wide', 'narrow')), may hold values from -0.109375 to 0.109375
- cotangent: bfloat16 [65536, 768], P(('wide', 'narrow')), may hold values from -6 to 6
Outputs:
- output: bfloat16 [65536, 768], P(('wide', 'narrow'))
- tokens_grad: bfloat16 [65536, 768], P(('wide', 'narrow'))
- ln1_gain_grad: float32 [768], P(('wide', 'narrow'))
- ln1_bias_grad: float32 [768], P(('wide', 'narrow'))
- qkv_grad: float32 [768, 2304], P(('wide', 'narrow'))
- out_grad: float32 [768, 768], P(('wide', 'narrow'))
- ln2_gain_grad: float32 [768], P(('wide', 'narrow'))
- ln2_bias_grad: float32 [768], P(('wide', 'narrow'))
- up_grad: float32 [768, 3072], P(None, ('wide', 'narrow'))
- down_grad: float32 [3072, 768], P(('wide', 'narrow'))
The draws below stay inside these ranges and needn't reach their ends.
Inputs may be any that keep to these rules, and one draw needn't show every extreme that they name: `seq_lengths`: each device's row is either 512, 0, 0, 0 or two to four entries 128 followed by zeros; both kinds occur in every draw.
All inputs are finite; a program needn't handle non-finite values.
Results may differ from the reference program's by a relative error of at most 0.018.
Values may be sent and summed in bfloat16 or wider, within the bound.
No kernel may reach another device: no remote copies, remote signals or barrier semaphores. Data moves between devices by JAX's collectives and lax.ppermute only.
A program may use at most 128 MiB of HBM per device.

```python
import jax
import jax.numpy as jnp
from jax import lax

D = 768
HEADS = 12
HEAD_DIM = 64
FF = 3072
TOK_DEV = 512
SLOTS = 4
SHORT = 128
TOKENS = 65536
DEVICES = 128


def draw_seq_lengths(key, part):
    key = jax.random.fold_in(key, 11)
    key_count, key_kind, key_pick, key_step = jax.random.split(key, 4)
    count = jax.random.randint(key_count, (DEVICES, 1), 2, 5)
    kind = jax.random.randint(key_kind, (DEVICES, 1), 0, 4)
    long_pick = jax.random.randint(key_pick, (), 0, DEVICES)
    short_pick = (long_pick + jax.random.randint(key_step, (), 1, DEVICES)) % DEVICES
    device_rows = jnp.arange(DEVICES)[:, None]
    kind = jnp.where(device_rows == long_pick, 1, jnp.where(device_rows == short_pick, 0, kind))
    slot_index = jnp.arange(SLOTS)[None, :]
    short_row = jnp.where(slot_index < count, SHORT, 0)
    long_row = jnp.where(slot_index == 0, TOK_DEV, 0)
    return jnp.where(kind > 0, long_row, short_row).astype(jnp.int32)


def block_levels(key, extent, pieces, least, top_value):
    level = 1.0
    for position, shards_of in pieces:
        steps = jax.random.uniform(jax.random.fold_in(jax.random.fold_in(key, 6), position), (shards_of,), jnp.float32, least / len(pieces), top_value / len(pieces))
        level = level * jnp.repeat(jnp.exp(steps), extent[position] // shards_of).reshape((-1,) + (1,) * (len(extent) - 1 - position))
    return level


def normal_values(rng, shape, scale, most, shards=(), kind=jnp.bfloat16):
    gain = block_levels(rng, shape, shards, -0.22, 0.18) if shards else 1.0
    values = jax.random.normal(rng, shape, jnp.float32) * scale * gain
    return jnp.minimum(jnp.maximum(values, -most), most).astype(kind)


def setup_inputs(seed: int = 0) -> dict:
    seeds = jax.random.split(jax.random.key(seed), 12)
    tokens = normal_values(seeds[0], (TOKENS, D), 1.0, 6.0, ((0, 128),))
    seq_lengths = draw_seq_lengths(jax.random.fold_in(seeds[11], 71), 0)
    ln1_gain = jnp.clip(1.0 + 0.15 * jax.random.normal(seeds[2], (D,), jnp.float32), 0.25, 1.75).astype(jnp.bfloat16)
    ln1_bias = normal_values(seeds[3], (D,), 0.5, 3.0, ((0, 128),))
    qkv_weight = normal_values(seeds[4], (D, 3 * D), D ** -0.5, 0.21875, ((0, 128),))
    out_weight = normal_values(seeds[5], (D, D), (D // 4) ** -0.5, 0.4375, ((0, 128),))
    ln2_gain = jnp.clip(1.0 + 0.15 * jax.random.normal(seeds[6], (D,), jnp.float32), 0.25, 1.75).astype(jnp.bfloat16)
    ln2_bias = normal_values(seeds[7], (D,), 0.5, 3.0, ((0, 128),))
    up_weight = normal_values(seeds[8], (D, FF), D ** -0.5, 0.21875, ((1, 128),))
    down_weight = normal_values(seeds[9], (FF, D), FF ** -0.5, 0.109375, ((0, 128),))
    cotangent = normal_values(seeds[10], (TOKENS, D), 1.0, 6.0, ((0, 128),))
    return dict(tokens=tokens, seq_lengths=seq_lengths, ln1_gain=ln1_gain, ln1_bias=ln1_bias, qkv_weight=qkv_weight, out_weight=out_weight, ln2_gain=ln2_gain, ln2_bias=ln2_bias, up_weight=up_weight, down_weight=down_weight, cotangent=cotangent)


EPS = 1e-05
SHARP = 4.0
NEG = -1e+30
HIGH = lax.Precision.HIGHEST

@jax.custom_vjp
def low(v):
    return lax.optimization_barrier(v.astype(jnp.bfloat16)).astype(jnp.float32)

@jax.custom_vjp
def low_back(v):
    return v

def low_keep(v):
    return (low(v), None)

def low_pass(kept, grad):
    return (grad,)

def back_keep(v):
    return (v, None)

def back_low(kept, grad):
    return (low(grad),)
low.defvjp(low_keep, low_pass)
low_back.defvjp(back_keep, back_low)

def layout_masks(row_lengths, row_count):
    positions = jnp.arange(row_count, dtype=jnp.int32)
    group_ends = jnp.cumsum(row_lengths).astype(jnp.int32)
    segment = lax.optimization_barrier(jnp.sum((positions[:, None] >= group_ends[None, :]).astype(jnp.int32), axis=1)).astype(jnp.int32)
    first_row = jnp.concatenate([jnp.ones((1,), dtype=bool), segment[1:] != segment[:-1]])
    same_group = segment[:, None] == segment[None, :]
    allowed = same_group & (positions[None, :] <= positions[:, None])
    chosen = same_group & (positions[None, :] < positions[:, None]) & jnp.logical_not(first_row)[None, :]
    return (allowed, chosen)

def norm_rows(values, gain_row, bias_row):
    row_mean = lax.optimization_barrier(jnp.mean(values, axis=-1, keepdims=True))
    centered = values - row_mean
    variance = lax.optimization_barrier(jnp.mean(centered * centered, axis=-1, keepdims=True))
    return centered * lax.rsqrt(variance + EPS) * gain_row + bias_row

def attend_block(block_pair):
    qkv_block, row_lengths = block_pair
    row_count = qkv_block.shape[0]
    allowed, chosen = layout_masks(row_lengths, row_count)
    queries = qkv_block[:, :D].reshape(row_count, HEADS, HEAD_DIM)
    keys_all = qkv_block[:, D:2 * D].reshape(row_count, HEADS, HEAD_DIM)
    values = qkv_block[:, 2 * D:].reshape(row_count, HEADS, HEAD_DIM)
    logits = jnp.einsum('ihc,jhc->hij', queries, keys_all, precision=HIGH) * HEAD_DIM ** (-0.5)
    logits = low_back(logits)
    selected = jnp.where(chosen, jax.nn.softplus(SHARP * logits[0]) / SHARP, 0.0)
    running = jnp.cumsum(selected, axis=0)
    penalty = jnp.concatenate([jnp.zeros((1, row_count), jnp.float32), running[:-1]], axis=0)
    shifted = jnp.where(allowed[None], logits - penalty[None], NEG)
    row_top = lax.optimization_barrier(jnp.max(shifted, axis=-1, keepdims=True))
    exponent = jnp.exp(shifted - row_top)
    weights_soft = exponent / lax.optimization_barrier(jnp.sum(exponent, axis=-1, keepdims=True))
    mixed = jnp.einsum('hij,jhc->ihc', low(weights_soft), values, precision=HIGH)
    return low_back(low(mixed.reshape(row_count, D)))

def layer(inputs, seq_lengths, gain_one, bias_one, qkv_full, out_full, gain_two, bias_two, up_full, down_full):
    h_one = low(norm_rows(inputs, gain_one, bias_one))
    qkv = low_back(low(jnp.dot(h_one, qkv_full, precision=HIGH)))
    blocks = qkv.reshape(DEVICES, TOK_DEV, 3 * D)
    mixed = lax.map(jax.checkpoint(attend_block), (blocks, seq_lengths)).reshape(TOKENS, D)
    branch = low_back(jnp.dot(mixed, out_full, precision=HIGH))
    middle = inputs + branch
    h_two = low(norm_rows(middle, gain_two, bias_two))
    up_value = low_back(jnp.dot(h_two, up_full, precision=HIGH))
    activated = low(jax.nn.gelu(up_value, approximate=True))
    down_value = low_back(jnp.dot(activated, down_full, precision=HIGH))
    return middle + down_value

def reference(tokens, seq_lengths, ln1_gain, ln1_bias, qkv_weight, out_weight, ln2_gain, ln2_bias, up_weight, down_weight, cotangent):

    def forward(inputs, gain_one, bias_one, qkv_full, out_full, gain_two, bias_two, up_full, down_full):
        return layer(inputs, seq_lengths, gain_one, bias_one, qkv_full, out_full, gain_two, bias_two, up_full, down_full)
    result, pullback = jax.vjp(forward, tokens.astype(jnp.float32), ln1_gain.astype(jnp.float32), ln1_bias.astype(jnp.float32), qkv_weight.astype(jnp.float32), out_weight.astype(jnp.float32), ln2_gain.astype(jnp.float32), ln2_bias.astype(jnp.float32), up_weight.astype(jnp.float32), down_weight.astype(jnp.float32))
    totals = lax.optimization_barrier(jnp.sum(seq_lengths, axis=1)).astype(jnp.int32)
    live_rows = (jnp.arange(TOK_DEV, dtype=jnp.int32)[None, :] < totals[:, None]).reshape(TOKENS)
    grads = pullback(cotangent.astype(jnp.float32) * live_rows[:, None].astype(jnp.float32))
    return (result.astype(jnp.bfloat16), grads[0].astype(jnp.bfloat16), grads[1], grads[2], grads[3], grads[4], grads[5], grads[6], grads[7], grads[8])
```

```python
import itertools

import jax
import jax.numpy as jnp
from jax import lax
from jax.experimental import pallas as pl
from jax.experimental.pallas import tpu as pltpu
from jax.sharding import PartitionSpec as P

BF = jnp.bfloat16
F32 = jnp.float32
I32 = jnp.int32
AXES = ("wide", "narrow")
D = 768
ROWS = 512
FF = 3072
OWN = 6
SLOT = 8
PEERS = 64
HALF = PEERS * SLOT
EPS = 1e-05
FAR = 1e30
TANH_SCALE = 0.7978845608028654
TANH_CUBE = 0.044715
MIB = 1 << 20


def device_number(x, y, z, core):
    return ((x & 1) * 8 + y * 2 + core) * 8 + (x >> 1) * 4 + z


def peer_groups(dims):
    sizes = dict(x=4, y=4, z=4, c=2)
    rest = [name for name in "xyzc" if name not in dims]
    groups = []
    for fixed in itertools.product(*[range(sizes[name]) for name in rest]):
        members = []
        for moving in itertools.product(*[range(sizes[name]) for name in dims]):
            at = dict(zip(rest, fixed))
            at.update(zip(dims, moving))
            members.append(device_number(at["x"], at["y"], at["z"], at["c"]))
        groups.append(members)
    return groups


def core_pairs():
    return [
        (device_number(x, y, z, c), device_number(x, y, z, 1 - c))
        for x, y, z, c in itertools.product(range(4), range(4), range(4), range(2))
    ]


def dot_nn(left, right):
    return lax.dot_general(left, right, (((1,), (0,)), ((), ())), preferred_element_type=F32)


def dot_nt(left, right):
    return lax.dot_general(left, right, (((1,), (1,)), ((), ())), preferred_element_type=F32)


def dot_tn(left, right):
    return lax.dot_general(left, right, (((0,), (0,)), ((), ())), preferred_element_type=F32)


def iota(shape, dim):
    return lax.broadcasted_iota(I32, shape, dim)


def one_hot(mask):
    return jnp.where(mask, 1.0, 0.0).astype(BF)


def split_low(values):
    high = values.astype(BF)
    return high, (values - high.astype(F32)).astype(BF)


def owner(group, core):
    z = group >> 4
    y = (group >> 2) & 3
    x = group & 3
    return ((x & 1) << 6) + (y << 4) + (core << 3) + ((x >> 1) << 2) + z


def sixth(number):
    return (number * 43691) >> 18


def place_matrix(core):
    slot = iota((1, HALF), 1)
    inner = slot & 7
    feature = jnp.where(inner < OWN, owner(slot >> 3, core) * OWN + inner, -1)
    return one_hot(iota((D, HALF), 0) == feature)


def vector_lanes(which):
    feature = iota((1, D), 1)
    lane = which * OWN + feature - OWN * sixth(feature)
    return iota((128, D), 0) == lane


def owned_features(core):
    return owner(iota((PEERS, 1), 0), core) == sixth(iota((1, D), 1))


def unpack_vectors(weights, core, count):
    pick = one_hot(iota((PEERS, HALF), 1) == iota((PEERS, HALF), 0) * SLOT + OWN)
    packed = dot_nn(pick, weights).astype(BF)
    mine = owned_features(core)
    return [
        jnp.sum(
            jnp.where(mine, dot_nn(packed, one_hot(vector_lanes(which))), 0.0),
            axis=0,
            keepdims=True,
        )
        for which in range(count)
    ]


def pack_vectors(vectors, core):
    mine = owned_features(core)
    total = jnp.zeros((PEERS, 128), F32)
    for which, vector in enumerate(vectors):
        spread = jnp.where(mine, vector, 0.0).astype(BF)
        total = total + dot_nt(spread, one_hot(vector_lanes(which)))
    put = one_hot(iota((HALF, PEERS), 0) == iota((HALF, PEERS), 1) * SLOT + OWN)
    return dot_nn(put, total.astype(BF))


def norm_stats(values):
    center = values - jnp.mean(values, axis=-1, keepdims=True)
    inverse = lax.rsqrt(jnp.mean(center * center, axis=-1, keepdims=True) + EPS)
    return center * inverse, inverse


def norm_pull(gradient, unit, inverse, gain):
    scaled = gradient * gain
    return inverse * (
        scaled
        - jnp.mean(scaled, axis=-1, keepdims=True)
        - unit * jnp.mean(scaled * unit, axis=-1, keepdims=True)
    )


def group_ends(lens_ref):
    ends = []
    total = 0
    for slot in range(4):
        total = total + lens_ref[0, slot]
        ends.append(total)
    return ends


def segments(positions, ends):
    return sum((positions >= end).astype(I32) for end in ends)


VM = pl.BlockSpec(memory_space=pltpu.VMEM)
SM = pl.BlockSpec(memory_space=pltpu.SMEM)
ANY = pl.BlockSpec(memory_space=pl.ANY)


def params(limit=56):
    return pltpu.CompilerParams(vmem_limit_bytes=limit * MIB)


def pack_kernel(
    g1_ref, b1_ref, qkv_ref, out_ref, g2_ref, b2_ref, up_ref, down_ref, early_ref, late_ref, es, ls
):
    es[...] = jnp.zeros_like(es)
    ls[...] = jnp.zeros_like(ls)
    qkv = qkv_ref[...].astype(F32)
    for part in range(3):
        es[SLOT * part : SLOT * part + OWN, :] = qkv[:, part * D : part * D + D]
    es[OWN : OWN + 1, 0:OWN] = g1_ref[...].astype(F32)
    es[OWN : OWN + 1, OWN : 2 * OWN] = b1_ref[...].astype(F32)
    up = up_ref[...].astype(F32).T
    down = down_ref[...].astype(F32)
    ls[0:16, :] = up[0:16]
    ls[16:32, :] = down[0:16]
    ls[32:40, :] = up[16:24]
    ls[40:48, :] = down[16:24]
    ls[48 : 48 + OWN, :] = out_ref[...].astype(F32)
    ls[48 + OWN : 49 + OWN, 0:OWN] = g2_ref[...].astype(F32)
    ls[48 + OWN : 49 + OWN, OWN : 2 * OWN] = b2_ref[...].astype(F32)
    early_ref[...] = es[...].astype(BF)
    late_ref[...] = ls[...].astype(BF)


def pack(g1, b1, qkv, out, g2, b2, up, down):
    return pl.pallas_call(
        pack_kernel,
        out_shape=(
            jax.ShapeDtypeStruct((24, D), BF),
            jax.ShapeDtypeStruct((64, D), BF),
        ),
        in_specs=[VM] * 8,
        out_specs=(VM, VM),
        scratch_shapes=[pltpu.VMEM((24, D), F32), pltpu.VMEM((64, D), F32)],
        compiler_params=params(),
        name="pack",
    )(g1[None], b1[None], qkv, out, g2[None], b2[None], up, down)


def project_kernel(core_ref, x_ref, own_ref, oth_ref, h_ref, qkv_ref, w_ref, ln_ref, hs):
    core = core_ref[0, 0]
    gain = jnp.zeros((1, D), F32)
    bias = jnp.zeros((1, D), F32)
    for half, source in enumerate((own_ref, oth_ref)):

        @pl.loop(0, 4)
        def _(block):
            slab = source[pl.ds(block * 16, 16)].astype(F32)
            for part in range(3):
                rows = slab[:, SLOT * part : SLOT * part + SLOT, :].reshape(128, D)
                w_ref[half, part, pl.ds(pl.multiple_of(block * 128, 128), 128), :] = rows.astype(BF)

        side = core if half == 0 else 1 - core
        found = unpack_vectors(w_ref[half, 0, :, 0:128], side, 2)
        gain = gain + found[0]
        bias = bias + found[1]
    ln_ref[...] = jnp.zeros_like(ln_ref)
    ln_ref[0:1, :] = gain

    @pl.loop(0, 4)
    def _(block):
        rows = pl.ds(pl.multiple_of(block * 128, 128), 128)
        unit, _ = norm_stats(x_ref[rows, :].astype(F32))
        hs[rows, :] = (unit * gain + bias).astype(BF)

    for half in range(2):
        side = core if half == 0 else 1 - core
        h_ref[half] = dot_nn(hs[...], place_matrix(side)).astype(BF)
    for part in range(3):
        total = dot_nn(h_ref[0], w_ref[0, part]) + dot_nn(h_ref[1], w_ref[1, part])
        qkv_ref[:, part * D : part * D + D] = total.astype(BF)


def project(core, x, own, oth):
    return pl.pallas_call(
        project_kernel,
        out_shape=(
            jax.ShapeDtypeStruct((2, ROWS, HALF), BF),
            jax.ShapeDtypeStruct((ROWS, 3 * D), BF),
            jax.ShapeDtypeStruct((2, 3, HALF, D), BF),
            jax.ShapeDtypeStruct((8, D), F32),
        ),
        in_specs=[SM, VM, VM, VM],
        out_specs=(VM, VM, VM, VM),
        scratch_shapes=[pltpu.VMEM((ROWS, D), BF)],
        compiler_params=params(),
        name="project",
    )(core, x, own, oth)


def softplus4(logits):
    sharp = 4.0 * logits
    return 0.25 * (jnp.maximum(sharp, 0.0) + jnp.log(1.0 + jnp.exp(-jnp.abs(sharp))))


def block_masks(block, ends):
    count = (block + 1) * 128
    row = iota((128, 1), 0) + block * 128
    column = iota((1, count), 1)
    same = segments(row, ends) == segments(column, ends)
    first = column == 0
    for end in ends:
        first = first | (column == end)
    allowed = same & (column <= row)
    chosen = same & (column < row) & jnp.logical_not(first)
    return allowed, chosen


def attend_kernel(lens_ref, qkv_ref, attn_ref, pen_ref, lse_ref, carry):
    ends = group_ends(lens_ref)
    left = iota((1, 128), 1) < 64
    zero = jnp.zeros((), BF)
    q0 = jnp.where(left, qkv_ref[:, 0:128], zero) * jnp.asarray(0.125, BF)
    k0 = qkv_ref[:, D : D + 128]
    lower = one_hot(iota((128, 128), 0) > iota((128, 128), 1))
    carry[...] = jnp.zeros_like(carry)
    for block in range(4):
        count = (block + 1) * 128
        rows = slice(block * 128, count)
        allowed, chosen = block_masks(block, ends)
        chosen_values = jnp.where(chosen, softplus4(dot_nt(q0[rows], k0[:count])), 0.0)
        high, low = split_low(chosen_values)
        penalty = dot_nn(lower, high) + dot_nn(lower, low) + carry[0:1, :count]
        carry[0:1, :count] = carry[0:1, :count] + jnp.sum(chosen_values, axis=0, keepdims=True)
        pen_ref[rows, :count] = jnp.where(allowed, penalty, FAR)

    @pl.loop(0, 6)
    def _(pair):
        lanes = pl.ds(pl.multiple_of(pair * 128, 128), 128)
        q = qkv_ref[:, lanes] * jnp.asarray(0.125, BF)
        k = qkv_ref[:, pl.ds(pl.multiple_of(pair * 128 + D, 128), 128)]
        v = qkv_ref[:, pl.ds(pl.multiple_of(pair * 128 + 2 * D, 128), 128)]
        sides = (jnp.where(left, q, zero), jnp.where(left, zero, q))
        for block in range(4):
            count = (block + 1) * 128
            rows = slice(block * 128, count)
            mixed = []
            totals = []
            for side in sides:
                shifted = dot_nt(side[rows], k[:count]) - pen_ref[rows, :count]
                top = jnp.max(shifted, axis=-1, keepdims=True)
                exponent = jnp.exp(shifted - top)
                total = jnp.sum(exponent, axis=-1, keepdims=True)
                mixed.append(dot_nn((exponent * (1.0 / total)).astype(BF), v[:count]))
                totals.append(top + jnp.log(total))
            attn_ref[rows, lanes] = jnp.where(left, mixed[0], mixed[1]).astype(BF)
            lse_ref[pair, rows, :] = jnp.where(left, totals[0], totals[1])


def attend(lens, qkv):
    return pl.pallas_call(
        attend_kernel,
        out_shape=(
            jax.ShapeDtypeStruct((ROWS, D), BF),
            jax.ShapeDtypeStruct((ROWS, ROWS), F32),
            jax.ShapeDtypeStruct((6, ROWS, 128), F32),
        ),
        in_specs=[SM, VM],
        out_specs=(VM, VM, VM),
        scratch_shapes=[pltpu.VMEM((8, ROWS), F32)],
        compiler_params=params(),
        name="attend",
    )(lens, qkv)


def attend_back_kernel(
    lens_ref, qkv_ref, up_ref, pen_ref, lse_ref, dqkv_ref, total, kept, dk_acc, dv_acc, carry
):
    ends = group_ends(lens_ref)
    left = iota((1, 128), 1) < 64
    zero = jnp.zeros((), BF)
    scale = jnp.asarray(0.125, BF)
    total[...] = jnp.zeros_like(total)

    def pair_parts(pair):
        lanes = pl.ds(pl.multiple_of(pair * 128, 128), 128)
        q = qkv_ref[:, lanes] * scale
        k = qkv_ref[:, pl.ds(pl.multiple_of(pair * 128 + D, 128), 128)]
        v = qkv_ref[:, pl.ds(pl.multiple_of(pair * 128 + 2 * D, 128), 128)]
        return q, k, v, up_ref[:, lanes]

    def one_side(values, side):
        return jnp.where(left, values, zero) if side == 0 else jnp.where(left, zero, values)

    def score_gradient(qs, k, us, v, block, log_total):
        count = (block + 1) * 128
        rows = slice(block * 128, count)
        shifted = dot_nt(qs[rows], k[:count]) - pen_ref[rows, :count]
        soft = jnp.exp(shifted - log_total)
        gradient = dot_nt(us[rows], v[:count])
        inner = jnp.sum(gradient * soft, axis=-1, keepdims=True)
        return soft.astype(BF), soft * (gradient - inner)

    def run_pair(pair, skip_first):
        q, k, v, u = pair_parts(pair)
        dk_acc[...] = jnp.zeros_like(dk_acc)
        dv_acc[...] = jnp.zeros_like(dv_acc)
        lanes = pl.ds(pl.multiple_of(pair * 128, 128), 128)
        for block in range(4):
            count = (block + 1) * 128
            rows = slice(block * 128, count)
            log_totals = lse_ref[pair, rows, :]
            dq = []
            for side in range(2):
                qs, us = one_side(q, side), one_side(u, side)
                soft, dz = score_gradient(
                    qs, k, us, v, block, log_totals[:, side * 64 : side * 64 + 1]
                )
                total[rows, :count] = total[rows, :count] + dz
                dv_acc[:count, :] = dv_acc[:count, :] + dot_tn(soft, us[rows])
                if side == 0 and skip_first:
                    kept[rows, :count] = dz
                    dq.append(jnp.zeros((128, 128), F32))
                else:
                    low = dz.astype(BF)
                    dq.append(dot_nn(low, k[:count]))
                    dk_acc[:count, :] = dk_acc[:count, :] + dot_tn(low, qs[rows])
            dqkv_ref[rows, lanes] = (jnp.where(left, dq[0], dq[1]) * 0.125).astype(BF)
        dqkv_ref[:, pl.ds(pl.multiple_of(pair * 128 + D, 128), 128)] = dk_acc[...].astype(BF)
        dqkv_ref[:, pl.ds(pl.multiple_of(pair * 128 + 2 * D, 128), 128)] = dv_acc[...].astype(BF)

    @pl.loop(1, 6)
    def _(pair):
        run_pair(pair, False)

    run_pair(0, True)
    q, k, _, _ = pair_parts(0)
    qs = one_side(q, 0)
    upper = one_hot(iota((128, 128), 1) > iota((128, 128), 0))
    carry[...] = jnp.zeros_like(carry)
    for block in (3, 2, 1, 0):
        count = (block + 1) * 128
        rows = slice(block * 128, count)
        _, chosen = block_masks(block, ends)
        dz = total[rows, :count]
        high, low = split_low(dz)
        selected = -(dot_nn(upper, high) + dot_nn(upper, low) + carry[0:1, :count])
        carry[0:1, :count] = carry[0:1, :count] + jnp.sum(dz, axis=0, keepdims=True)
        sharp = 4.0 * dot_nt(qs[rows], k[:count])
        slope = 1.0 / (1.0 + jnp.exp(-sharp))
        low = (kept[rows, :count] + jnp.where(chosen, slope * selected, 0.0)).astype(BF)
        dq = dot_nn(low, k[:count]) * 0.125
        dqkv_ref[rows, 0:128] = jnp.where(left, dq, dqkv_ref[rows, 0:128].astype(F32)).astype(BF)
        dk_acc[:count, :] = dk_acc[:count, :] + dot_tn(low, qs[rows])
    dqkv_ref[:, D : D + 128] = dk_acc[...].astype(BF)


def attend_back(lens, qkv, upstream, pen, lse):
    return pl.pallas_call(
        attend_back_kernel,
        out_shape=jax.ShapeDtypeStruct((ROWS, 3 * D), BF),
        in_specs=[SM, VM, VM, VM, VM],
        out_specs=VM,
        scratch_shapes=[
            pltpu.VMEM((ROWS, ROWS), F32),
            pltpu.VMEM((ROWS, ROWS), F32),
            pltpu.VMEM((ROWS, 128), F32),
            pltpu.VMEM((ROWS, 128), F32),
            pltpu.VMEM((8, ROWS), F32),
        ],
        compiler_params=params(),
        name="attend_back",
    )(lens, qkv, upstream, pen, lse)


def feed_kernel(
    core_ref, lens_ref, x_ref, attn_ref, cot_ref, own_ref, oth_ref,
    y_ref, dx_ref, dattn_ref, lng_ref, ga_own, gb_own, go_own, ga_oth, gb_oth, go_oth,
    up_s, down_s, mid_s, out_s, gup_s, gdown_s, gmid_s, mid_f, wo_s, ap_s, h_s, dy_s, unit_s, acc_s, dh_s,
    sems, out_sems,
):
    core = core_ref[0, 0]
    sources = (own_ref, oth_ref)
    loads = {}

    def load(key, source, target, slot):
        loads[key] = pltpu.make_async_copy(source, target, sems.at[slot])
        loads[key].start()

    for half in range(2):
        load(("out", half), sources[half].at[:, 48:64, :], out_s.at[half], half)
    for half in range(2):
        for part in range(2):
            chunk = half * 3 + part
            devices = pl.ds(part * 32, 32)
            load(("up", chunk), sources[half].at[devices, 0:16, :], up_s.at[chunk], 2 + chunk)
            load(("down", chunk), sources[half].at[devices, 16:32, :], down_s.at[chunk], 8 + chunk)
        load(("mid", half), sources[half].at[:, 32:48, :], mid_s.at[half], 14 + half)

    gain = jnp.zeros((1, D), F32)
    bias = jnp.zeros((1, D), F32)
    for half in range(2):
        side = core if half == 0 else 1 - core
        loads["out", half].wait()
        rows = out_s[half].astype(F32)[:, 0:SLOT, :].reshape(HALF, D)
        wo_s[half] = rows.astype(BF)
        found = unpack_vectors(wo_s[half, :, 0:128], side, 2)
        gain = gain + found[0]
        bias = bias + found[1]
        ap_s[half] = dot_nn(attn_ref[...], place_matrix(side)).astype(BF)
    acc_s[...] = dot_nn(ap_s[0], wo_s[0]) + dot_nn(ap_s[1], wo_s[1])
    ends = group_ends(lens_ref)

    @pl.loop(0, 4)
    def _(block):
        rows = pl.ds(pl.multiple_of(block * 128, 128), 128)
        middle = x_ref[rows, :].astype(F32) + acc_s[rows, :]
        acc_s[rows, :] = middle
        unit, _ = norm_stats(middle)
        unit_s[rows, :] = unit
        h_s[rows, :] = (unit * gain + bias).astype(BF)
        live = (iota((128, 1), 0) + block * 128) < ends[3]
        dy_s[rows, :] = jnp.where(live, cot_ref[rows, :].astype(F32), 0.0).astype(BF)

    dh_s[...] = jnp.zeros_like(dh_s)
    for half in range(2):
        for part in range(2):
            loads["up", half * 3 + part].wait()
            loads["down", half * 3 + part].wait()
        loads["mid", half].wait()
        mid = mid_s[half].astype(F32)
        up_s[half * 3 + 2] = mid[:, 0:8, :].reshape(32, 16, D).astype(BF)
        down_s[half * 3 + 2] = mid[:, 8:16, :].reshape(32, 16, D).astype(BF)

    @pl.loop(0, 6)
    def _(chunk):
        up = up_s[chunk].reshape(ROWS, D)
        down = down_s[chunk].reshape(ROWS, D)
        value = dot_nt(h_s[...], up)
        square = value * value
        bend = jnp.tanh(TANH_SCALE * (value + TANH_CUBE * (value * square)))
        act = (0.5 * value * (1.0 + bend)).astype(BF)
        slope = 0.5 * (1.0 + bend) + (0.5 * TANH_SCALE) * value * (1.0 - bend * bend) * (
            1.0 + 3.0 * TANH_CUBE * square
        )
        pulled = (dot_nt(dy_s[...], down) * slope).astype(BF)
        acc_s[...] = acc_s[...] + dot_nn(act, down)
        dh_s[...] = dh_s[...] + dot_nn(pulled, up)
        gdown_s[chunk] = dot_tn(act, dy_s[...]).astype(BF).reshape(32, 16, D)
        gup_s[chunk] = dot_tn(pulled, h_s[...]).astype(BF).reshape(32, 16, D)

    stores = []

    def store(source, target, slot):
        copy = pltpu.make_async_copy(source, target, out_sems.at[slot])
        copy.start()
        stores.append(copy)

    for half, (big, small) in enumerate(((ga_own, gb_own), (ga_oth, gb_oth))):
        for part in range(2):
            chunk = half * 3 + part
            devices = pl.ds(part * 32, 32)
            store(gup_s.at[chunk], big.at[devices, 0:16, :], half * 5 + part * 2)
            store(gdown_s.at[chunk], big.at[devices, 16:32, :], half * 5 + part * 2 + 1)
        mid_f[:, 0:8, :] = gup_s[half * 3 + 2].astype(F32).reshape(PEERS, 8, D)
        mid_f[:, 8:16, :] = gdown_s[half * 3 + 2].astype(F32).reshape(PEERS, 8, D)
        gmid_s[half] = mid_f[...].astype(BF)
        store(gmid_s.at[half], small, half * 5 + 4)

    lng_ref[...] = jnp.zeros_like(lng_ref)

    @pl.loop(0, 4)
    def _(block):
        rows = pl.ds(pl.multiple_of(block * 128, 128), 128)
        y_ref[rows, :] = acc_s[rows, :].astype(BF)
        unit = unit_s[rows, :]
        gradient = dh_s[rows, :]
        lng_ref[0:1, :] = lng_ref[0:1, :] + jnp.sum(gradient * unit, axis=0, keepdims=True)
        lng_ref[1:2, :] = lng_ref[1:2, :] + jnp.sum(gradient, axis=0, keepdims=True)

    middle_rows = dot_nn(ap_s[0], wo_s[0]) + dot_nn(ap_s[1], wo_s[1])
    acc_s[...] = middle_rows

    @pl.loop(0, 4)
    def _(block):
        rows = pl.ds(pl.multiple_of(block * 128, 128), 128)
        _, inverse = norm_stats(x_ref[rows, :].astype(F32) + acc_s[rows, :])
        moved = dy_s[rows, :].astype(F32) + norm_pull(dh_s[rows, :], unit_s[rows, :], inverse, gain)
        dx_ref[rows, :] = moved
        h_s[rows, :] = moved.astype(BF)

    total = jnp.zeros((ROWS, D), F32)
    for half, target in enumerate((go_own, go_oth)):
        side = core if half == 0 else 1 - core
        target[...] = dot_tn(ap_s[half], h_s[...]).reshape(PEERS, SLOT, D).astype(BF)
        total = total + dot_nt(dot_nt(h_s[...], wo_s[half]).astype(BF), place_matrix(side))
    dattn_ref[...] = total.astype(BF)
    for copy in stores:
        copy.wait()


def feed(core, lens, x, attn, cot, own, oth):
    big = jax.ShapeDtypeStruct((PEERS, 32, D), BF)
    small = jax.ShapeDtypeStruct((PEERS, 16, D), BF)
    outer = jax.ShapeDtypeStruct((PEERS, SLOT, D), BF)
    return pl.pallas_call(
        feed_kernel,
        out_shape=(
            jax.ShapeDtypeStruct((ROWS, D), BF),
            jax.ShapeDtypeStruct((ROWS, D), F32),
            jax.ShapeDtypeStruct((ROWS, D), BF),
            jax.ShapeDtypeStruct((8, D), F32),
            big, small, outer, big, small, outer,
        ),
        in_specs=[SM, SM, VM, VM, VM, ANY, ANY],
        out_specs=(VM, VM, VM, VM, ANY, ANY, VM, ANY, ANY, VM),
        scratch_shapes=[
            pltpu.VMEM((6, 32, 16, D), BF),
            pltpu.VMEM((6, 32, 16, D), BF),
            pltpu.VMEM((2, PEERS, 16, D), BF),
            pltpu.VMEM((2, PEERS, 16, D), BF),
            pltpu.VMEM((6, 32, 16, D), BF),
            pltpu.VMEM((6, 32, 16, D), BF),
            pltpu.VMEM((2, PEERS, 16, D), BF),
            pltpu.VMEM((PEERS, 16, D), F32),
            pltpu.VMEM((2, HALF, D), BF),
            pltpu.VMEM((2, ROWS, HALF), BF),
            pltpu.VMEM((ROWS, D), BF),
            pltpu.VMEM((ROWS, D), BF),
            pltpu.VMEM((ROWS, D), F32),
            pltpu.VMEM((ROWS, D), F32),
            pltpu.VMEM((ROWS, D), F32),
            pltpu.SemaphoreType.DMA((16,)),
            pltpu.SemaphoreType.DMA((10,)),
        ],
        compiler_params=params(),
        name="feed",
    )(core, lens, x, attn, cot, own, oth)


def project_back_kernel(
    core_ref, x_ref, dx_ref, h_ref, w_ref, dqkv_ref, ln_ref, lng_ref, dtok_ref, own_ref, oth_ref, dh_s, vec_s
):
    core = core_ref[0, 0]
    total = jnp.zeros((ROWS, D), F32)
    for half in range(2):
        side = core if half == 0 else 1 - core
        parts = dot_nt(dqkv_ref[:, 0:D], w_ref[half, 0])
        parts = parts + dot_nt(dqkv_ref[:, D : 2 * D], w_ref[half, 1])
        parts = parts + dot_nt(dqkv_ref[:, 2 * D : 3 * D], w_ref[half, 2])
        high, low = split_low(parts)
        place = place_matrix(side)
        total = total + dot_nt(high, place) + dot_nt(low, place)
    dh_s[...] = total
    vec_s[...] = jnp.zeros_like(vec_s)
    gain = ln_ref[0:1, :]

    @pl.loop(0, 4)
    def _(block):
        rows = pl.ds(pl.multiple_of(block * 128, 128), 128)
        unit, inverse = norm_stats(x_ref[rows, :].astype(F32))
        gradient = dh_s[rows, :]
        vec_s[0:1, :] = vec_s[0:1, :] + jnp.sum(gradient * unit, axis=0, keepdims=True)
        vec_s[1:2, :] = vec_s[1:2, :] + jnp.sum(gradient, axis=0, keepdims=True)
        moved = dx_ref[rows, :] + norm_pull(gradient, unit, inverse, gain)
        dtok_ref[rows, :] = moved.astype(BF)

    vectors = [vec_s[0:1, :], vec_s[1:2, :], lng_ref[0:1, :], lng_ref[1:2, :]]
    for half, target in enumerate((own_ref, oth_ref)):
        side = core if half == 0 else 1 - core
        pads = pack_vectors(vectors, side)
        pieces = []
        for part in range(3):
            piece = dot_tn(h_ref[half], dqkv_ref[:, part * D : part * D + D])
            if part == 0:
                piece = jnp.concatenate([piece[:, 0:128] + pads, piece[:, 128:]], axis=1)
            pieces.append(piece.reshape(PEERS, SLOT, D))
        target[...] = jnp.concatenate(pieces, axis=1).astype(BF)


def project_back(core, x, dx, h, w, dqkv, ln, lng):
    slab = jax.ShapeDtypeStruct((PEERS, 24, D), BF)
    return pl.pallas_call(
        project_back_kernel,
        out_shape=(jax.ShapeDtypeStruct((ROWS, D), BF), slab, slab),
        in_specs=[SM] + [VM] * 7,
        out_specs=(VM, VM, VM),
        scratch_shapes=[pltpu.VMEM((ROWS, D), F32), pltpu.VMEM((8, D), F32)],
        compiler_params=params(),
        name="project_back",
    )(core, x, dx, h, w, dqkv, ln, lng)


def join_kernel(a0, b0, c0, a1, b1, c1, out_ref):
    pieces = [
        left[...].astype(F32) + right[...].astype(F32)
        for left, right in ((a0, a1), (b0, b1), (c0, c1))
    ]
    out_ref[...] = jnp.concatenate(pieces, axis=1).astype(BF)


def join(own, received):
    sizes = (32, 16, SLOT)
    specs = [pl.BlockSpec((8, size, D), lambda i: (i, 0, 0)) for size in sizes]
    return pl.pallas_call(
        join_kernel,
        grid=(8,),
        out_shape=jax.ShapeDtypeStruct((PEERS, 56, D), BF),
        in_specs=specs + specs,
        out_specs=pl.BlockSpec((8, 56, D), lambda i: (i, 0, 0)),
        compiler_params=params(),
        name="join",
    )(*own, *received)


def finish_kernel(early_ref, qkv_ref, g1_ref, b1_ref, g2_ref, b2_ref):
    total = jnp.sum(early_ref[...].astype(F32), axis=0)
    for part in range(3):
        qkv_ref[:, part * D : part * D + D] = total[SLOT * part : SLOT * part + OWN, :]
    for which, target in enumerate((g1_ref, b1_ref, g2_ref, b2_ref)):
        target[...] = total[OWN : OWN + 1, which * OWN : which * OWN + OWN]


def finish(early):
    vector = jax.ShapeDtypeStruct((1, OWN), F32)
    return pl.pallas_call(
        finish_kernel,
        out_shape=(jax.ShapeDtypeStruct((OWN, 3 * D), F32), vector, vector, vector, vector),
        in_specs=[VM],
        out_specs=(VM,) * 5,
        compiler_params=params(),
        name="finish",
    )(early)


def unpack_kernel(late_ref, up_ref, down_ref, out_ref, down_s):
    late = late_ref[...].astype(F32)
    up_ref[...] = jnp.concatenate([late[0:16], late[32:40]], axis=0).T
    down_ref[...] = jnp.concatenate([late[16:32], late[40:48]], axis=0)
    out_ref[...] = late[48 : 48 + OWN]


def unpack(late):
    return pl.pallas_call(
        unpack_kernel,
        out_shape=(
            jax.ShapeDtypeStruct((D, 24), F32),
            jax.ShapeDtypeStruct((24, D), F32),
            jax.ShapeDtypeStruct((OWN, D), F32),
        ),
        in_specs=[VM],
        out_specs=(VM,) * 3,
        scratch_shapes=[pltpu.VMEM((8, D), F32)],
        compiler_params=params(),
        name="unpack",
    )(late)


def on_device(
    tokens,
    seq_lengths,
    ln1_gain,
    ln1_bias,
    qkv_weight,
    out_weight,
    ln2_gain,
    ln2_bias,
    up_weight,
    down_weight,
    cotangent,
):
    core = (lax.axis_index("wide") & 1).astype(I32).reshape(1, 1)
    everyone = peer_groups("zyx")
    pairs = core_pairs()
    early, late = pack(
        ln1_gain, ln1_bias, qkv_weight, out_weight, ln2_gain, ln2_bias, up_weight, down_weight
    )
    late_own = lax.all_gather(late, AXES, axis_index_groups=everyone)
    early_own = lax.all_to_all(
        jnp.broadcast_to(early, (PEERS, 24, D)), AXES, 0, 0, axis_index_groups=everyone, tiled=True
    )
    early_oth = lax.ppermute(early_own, AXES, pairs)
    h_slots, qkv, weights, ln_rows = project(core, tokens, early_own, early_oth)
    attn, penalty, log_totals = attend(seq_lengths, qkv)
    late_oth = lax.ppermute(late_own, AXES, pairs)
    output, dx, dattn, ln_grads, *slabs = feed(
        core, seq_lengths, tokens, attn, cotangent, late_own, late_oth
    )
    received = [lax.ppermute(slab, AXES, pairs) for slab in slabs[3:]]
    joined = join(slabs[:3], received).reshape(PEERS * 56, D)
    for dim in "zyx":
        joined = lax.psum_scatter(
            joined, AXES, scatter_dimension=0, axis_index_groups=peer_groups(dim), tiled=True
        )
    dqkv = attend_back(seq_lengths, qkv, dattn, penalty, log_totals)
    dtokens, tail_own, tail_oth = project_back(
        core, tokens, dx, h_slots, weights, dqkv, ln_rows, ln_grads
    )
    tail_received = lax.ppermute(tail_oth, AXES, pairs)
    tail = (tail_own.astype(F32) + tail_received.astype(F32)).astype(BF)
    tail = lax.all_to_all(tail, AXES, 0, 0, axis_index_groups=everyone, tiled=True)
    qkv_grad, g1_grad, b1_grad, g2_grad, b2_grad = finish(tail)
    up_grad, down_grad, out_grad = unpack(joined)
    return (
        output,
        dtokens,
        g1_grad.reshape(OWN),
        b1_grad.reshape(OWN),
        qkv_grad,
        out_grad,
        g2_grad.reshape(OWN),
        b2_grad.reshape(OWN),
        up_grad,
        down_grad,
    )


def solution(mesh):
    rows = P(AXES, None)
    flat = P(AXES)
    columns = P(None, AXES)
    return jax.shard_map(
        on_device,
        mesh=mesh,
        in_specs=(rows, rows, flat, flat, rows, rows, flat, flat, columns, rows, rows),
        out_specs=(rows, rows, flat, flat, rows, rows, flat, flat, columns, rows),
        check_vma=False,
    )
```

```python
import itertools

import jax
import jax.numpy as jnp
from jax import lax
from jax.experimental import pallas as pl
from jax.experimental.pallas import tpu as pltpu
from jax.sharding import PartitionSpec as P

BF = jnp.bfloat16
F32 = jnp.float32
I32 = jnp.int32
AXES = ("wide", "narrow")
D = 768
ROWS = 512
FF = 3072
OWN = 6
PEERS = 64
HALF = PEERS * OWN
BLOCKS = 6
OUTER = 3 * OWN * BLOCKS
GATHERED = OUTER + OWN * BLOCKS
EARLY = 152
LATE = 48
WHOLE = 336
TAIL = 112
STEP = TAIL + 1
WIDE = 128 * 8
EPS = 1e-05
FAR = 1e30
TANH_SCALE = 0.7978845608028654
TANH_CUBE = 0.044715
MIB = 1 << 20


def device_number(x, y, z, core):
    return ((x & 1) * 8 + y * 2 + core) * 8 + (x >> 1) * 4 + z


def peer_groups(dims):
    sizes = dict(x=4, y=4, z=4, c=2)
    rest = [name for name in "xyzc" if name not in dims]
    groups = []
    for fixed in itertools.product(*[range(sizes[name]) for name in rest]):
        members = []
        for moving in itertools.product(*[range(sizes[name]) for name in dims]):
            at = dict(zip(rest, fixed))
            at.update(zip(dims, moving))
            members.append(device_number(at["x"], at["y"], at["z"], at["c"]))
        groups.append(members)
    return groups


def core_pairs():
    return [
        (device_number(x, y, z, c), device_number(x, y, z, 1 - c))
        for x, y, z, c in itertools.product(range(4), range(4), range(4), range(2))
    ]


def dot_nn(left, right):
    return lax.dot_general(left, right, (((1,), (0,)), ((), ())), preferred_element_type=F32)


def dot_nt(left, right):
    return lax.dot_general(left, right, (((1,), (1,)), ((), ())), preferred_element_type=F32)


def dot_tn(left, right):
    return lax.dot_general(left, right, (((0,), (0,)), ((), ())), preferred_element_type=F32)


def iota(shape, dim):
    return lax.broadcasted_iota(I32, shape, dim)


def one_hot(mask):
    return jnp.where(mask, 1.0, 0.0).astype(BF)


def split_low(values):
    high = values.astype(BF)
    return high, (values - high.astype(F32)).astype(BF)


def owner(group, core, spot):
    y = group >> 4
    x = (group >> 2) & 3
    z = (spot[1] - (group & 3)) & 3
    return ((x & 1) << 6) + (y << 4) + (core << 3) + ((x >> 1) << 2) + z


def sixth(number):
    return (number * 43691) >> 18


def place_matrix(spot):
    slot = iota((1, D), 1)
    other = (slot >= HALF).astype(I32)
    inner = slot - HALF * other
    side = spot[0] + other - 2 * spot[0] * other
    feature = owner(inner & (PEERS - 1), side, spot) * OWN + (inner >> 6)
    return one_hot(iota((D, D), 0) == feature)


def place_transposed(spot):
    slot = iota((D, 1), 0)
    other = (slot >= HALF).astype(I32)
    inner = slot - HALF * other
    side = spot[0] + other - 2 * spot[0] * other
    feature = owner(inner & (PEERS - 1), side, spot) * OWN + (inner >> 6)
    return one_hot(iota((D, D), 1) == feature)


def late_owner(group):
    z = group >> 5
    c = (group >> 4) & 1
    y = (group >> 2) & 3
    x = group & 3
    return ((x & 1) << 6) + (y << 4) + (c << 3) + ((x >> 1) << 2) + z


def place_late():
    slot = iota((1, WIDE), 1)
    inner = slot & 7
    feature = jnp.where(inner < OWN, late_owner(slot >> 3) * OWN + inner, -1)
    return one_hot(iota((D, WIDE), 0) == feature)


def vector_lanes(which):
    feature = iota((1, D), 1)
    lane = which * OWN + feature - OWN * sixth(feature)
    return one_hot(iota((128, D), 0) == lane)


def owned_features(core, spot):
    return owner(iota((PEERS, 1), 0), core, spot) == sixth(iota((1, D), 1))


def unpack_vector(packed, mine, which):
    spread = dot_nn(packed.astype(BF), vector_lanes(which))
    return jnp.sum(jnp.where(mine, spread, 0.0), axis=0, keepdims=True)


def pack_vectors(vectors, core, spot):
    mine = owned_features(core, spot)
    total = jnp.zeros((PEERS, 128), F32)
    for which, vector in enumerate(vectors):
        spread = jnp.where(mine, vector, 0.0).astype(BF)
        total = total + dot_nt(spread, vector_lanes(which))
    return total


def norm_stats(values):
    center = values - jnp.mean(values, axis=-1, keepdims=True)
    inverse = lax.rsqrt(jnp.mean(center * center, axis=-1, keepdims=True) + EPS)
    return center * inverse, inverse


def norm_pull(gradient, unit, inverse, gain):
    scaled = gradient * gain
    return inverse * (
        scaled
        - jnp.mean(scaled, axis=-1, keepdims=True)
        - unit * jnp.mean(scaled * unit, axis=-1, keepdims=True)
    )


def group_ends(lens_ref):
    ends = []
    total = 0
    for slot in range(4):
        total = total + lens_ref[0, slot]
        ends.append(total)
    return ends


def segments(positions, ends):
    return sum((positions >= end).astype(I32) for end in ends)


VM = pl.BlockSpec(memory_space=pltpu.VMEM)
SM = pl.BlockSpec(memory_space=pltpu.SMEM)
ANY = pl.BlockSpec(memory_space=pl.ANY)
OUT_WEIGHT = pl.BlockSpec((D, D), lambda i: (0, 3), memory_space=pltpu.VMEM)


def params(limit=60):
    return pltpu.CompilerParams(vmem_limit_bytes=limit * MIB)


def pack_kernel(
    g1_ref, b1_ref, qkv_ref, out_ref, g2_ref, b2_ref, up_ref, down_ref, early_ref, late_ref, es
):
    es[...] = jnp.zeros_like(es)
    qkv = qkv_ref[...].astype(F32)
    out = out_ref[...].astype(F32)
    for pair in range(BLOCKS):
        for part in range(3):
            start = (pair * 3 + part) * OWN
            es[start : start + OWN, :] = qkv[:, part * D + pair * 128 : part * D + pair * 128 + 128]
        start = OUTER + pair * OWN
        es[start : start + OWN, :] = out[:, pair * 128 : pair * 128 + 128]
    for which, ref in enumerate((g1_ref, b1_ref, g2_ref, b2_ref)):
        es[GATHERED : GATHERED + 1, which * OWN : which * OWN + OWN] = ref[...].astype(F32)
    early_ref[...] = es[...].astype(BF)
    up = up_ref[...].astype(F32)
    down = down_ref[...].astype(F32)
    late_ref[...] = jnp.concatenate([up[0:16], down[0:16], up[16:24], down[16:24]], axis=0).astype(BF)


def pack(g1, b1, qkv, out, g2, b2, up, down):
    return pl.pallas_call(
        pack_kernel,
        out_shape=(
            jax.ShapeDtypeStruct((EARLY, 128), BF),
            jax.ShapeDtypeStruct((LATE, D), BF),
        ),
        in_specs=[VM] * 8,
        out_specs=(VM, VM),
        scratch_shapes=[pltpu.VMEM((EARLY, 128), F32)],
        compiler_params=params(),
        name="pack",
    )(g1[None], b1[None], qkv, out, g2[None], b2[None], up, down)


def project_kernel(spot_ref, x_ref, own_ref, oth_ref, ht_ref, qkv_ref, w_ref, ln_ref, hs, rows_s):
    spot = (spot_ref[0, 0], spot_ref[0, 1])
    core = spot[0]
    vectors = [jnp.zeros((1, D), F32) for _ in range(4)]
    for half, source in enumerate((own_ref, oth_ref)):
        side = core if half == 0 else 1 - core

        @pl.loop(0, 8)
        def _(block):
            start = pl.multiple_of(block * (8 * EARLY), 8 * EARLY)
            values = source[pl.ds(block * 8, 8)].astype(F32)
            rows_s[pl.ds(start, 8 * EARLY), :] = values.reshape(8 * EARLY, 128)

        for block in range(4 * BLOCKS):
            for row in range(OWN):
                to = half * HALF + row * PEERS
                w_ref[to : to + PEERS, block * 128 : block * 128 + 128] = rows_s[
                    pl.ds(block * OWN + row, PEERS, stride=EARLY), :
                ].astype(BF)
        packed = rows_s[pl.ds(GATHERED, PEERS, stride=EARLY), :]
        mine = owned_features(side, spot)
        vectors = [
            vector + unpack_vector(packed, mine, which) for which, vector in enumerate(vectors)
        ]
    for which, vector in enumerate(vectors):
        ln_ref[which : which + 1, :] = vector
    ln_ref[4:8, :] = jnp.zeros((4, D), F32)

    @pl.loop(0, 4)
    def _(block):
        rows = pl.ds(pl.multiple_of(block * 128, 128), 128)
        unit, _ = norm_stats(x_ref[rows, :].astype(F32))
        hs[rows, :] = (unit * ln_ref[0:1, :] + ln_ref[1:2, :]).astype(BF)

    placed = dot_nn(hs[...], place_matrix(spot)).astype(BF)
    for part in range(3):
        columns = slice(part * D, part * D + D)
        qkv_ref[:, columns] = dot_nn(placed, w_ref[:, columns]).astype(BF)
    ht_ref[...] = dot_nt(place_transposed(spot), hs[...]).astype(BF)


def project(spot, x, own, oth):
    return pl.pallas_call(
        project_kernel,
        out_shape=(
            jax.ShapeDtypeStruct((D, ROWS), BF),
            jax.ShapeDtypeStruct((ROWS, 3 * D), BF),
            jax.ShapeDtypeStruct((D, 4 * D), BF),
            jax.ShapeDtypeStruct((8, D), F32),
        ),
        in_specs=[SM, VM, VM, VM],
        out_specs=(VM, VM, VM, VM),
        scratch_shapes=[pltpu.VMEM((ROWS, D), BF), pltpu.VMEM((PEERS * EARLY, 128), F32)],
        compiler_params=params(),
        name="project",
    )(spot, x, own, oth)


def softplus4(logits):
    sharp = 4.0 * logits
    return 0.25 * (jnp.maximum(sharp, 0.0) + jnp.log(1.0 + jnp.exp(-jnp.abs(sharp))))


def block_masks(block, ends):
    count = (block + 1) * 128
    query = iota((1, 128), 1) + block * 128
    key = iota((count, 1), 0)
    same = segments(key, ends) == segments(query, ends)
    first = key == 0
    for end in ends:
        first = first | (key == end)
    allowed = same & (key <= query)
    chosen = same & (key < query) & jnp.logical_not(first)
    return allowed, chosen


def twice(values):
    return jnp.concatenate([values, values], axis=1)


def side_by_side(values):
    left = iota((1, 128), 1) < 64
    zero = jnp.zeros((), BF)
    return jnp.concatenate([jnp.where(left, values, zero), jnp.where(left, zero, values)], axis=0)


def own_halves(values):
    return jnp.concatenate([values[0:64, 0:128], values[64:128, 128:256]], axis=0)


def lanes_of(pair, part):
    return pl.ds(pl.multiple_of(pair * 384 + part * 128, 128), 128)


def attend_kernel(
    spot_ref, lens_ref, x_ref, qkv_ref, wo_ref, ln_ref, mixed_ref, middle_ref, h_ref, pen_ref, lse_ref, attn_s, carry
):
    ends = group_ends(lens_ref)
    scale = jnp.asarray(0.125, BF)
    row, column = iota((128, 256), 0), iota((128, 256), 1)
    before = one_hot((row < column) | (column >= 128))
    carry[...] = jnp.zeros_like(carry)
    k0 = qkv_ref[:, 128:256]
    for block in range(4):
        count = (block + 1) * 128
        rows = slice(block * 128, count)
        q0 = side_by_side(qkv_ref[rows, 0:128] * scale)[0:128]
        allowed, chosen = block_masks(block, ends)
        picked = jnp.where(chosen, softplus4(dot_nt(k0[:count], q0)), 0.0)
        high, low = split_low(picked)
        sums = dot_nn(high, before) + dot_nn(low, before)
        pen_ref[:count, rows] = jnp.where(allowed, sums[:, 0:128] + carry[:count, :], FAR)
        carry[:count, :] = carry[:count, :] + sums[:, 128:256]

    @pl.loop(0, 6)
    def _(pair):
        lanes = pl.ds(pl.multiple_of(pair * 128, 128), 128)
        k = qkv_ref[:, lanes_of(pair, 1)]
        v = qkv_ref[:, lanes_of(pair, 2)]
        for block in range(4):
            count = (block + 1) * 128
            rows = slice(block * 128, count)
            q = side_by_side(qkv_ref[rows, lanes_of(pair, 0)] * scale)
            shifted = dot_nt(k[:count], q) - twice(pen_ref[:count, rows])
            top = jnp.max(shifted, axis=0, keepdims=True)
            exponent = jnp.exp(shifted - top)
            total = jnp.sum(exponent, axis=0, keepdims=True)
            mixed = dot_tn(v[:count], exponent.astype(BF)) * (1.0 / total)
            attn_s[lanes, rows] = own_halves(mixed).astype(BF)
            log_total = top + jnp.log(total)
            lse_ref[pair, 0:1, rows] = log_total[:, 0:128]
            lse_ref[pair, 1:2, rows] = log_total[:, 128:256]

    mixed_ref[...] = dot_tn(attn_s[...], place_late()).astype(BF)
    mixed = dot_tn(attn_s[...], place_matrix((spot_ref[0, 0], spot_ref[0, 1]))).astype(BF)
    middle_ref[...] = dot_nn(mixed, wo_ref[...])

    @pl.loop(0, 4)
    def _(block):
        rows = pl.ds(pl.multiple_of(block * 128, 128), 128)
        middle = x_ref[rows, :].astype(F32) + middle_ref[rows, :]
        middle_ref[rows, :] = middle
        unit, _ = norm_stats(middle)
        h_ref[rows, :] = (unit * ln_ref[2:3, :] + ln_ref[3:4, :]).astype(BF)


def attend(spot, lens, x, qkv, weights, ln):
    return pl.pallas_call(
        attend_kernel,
        grid=(1,),
        out_shape=(
            jax.ShapeDtypeStruct((ROWS, WIDE), BF),
            jax.ShapeDtypeStruct((ROWS, D), F32),
            jax.ShapeDtypeStruct((ROWS, D), BF),
            jax.ShapeDtypeStruct((ROWS, ROWS), F32),
            jax.ShapeDtypeStruct((6, 8, ROWS), F32),
        ),
        in_specs=[SM, SM, VM, VM, OUT_WEIGHT, VM],
        out_specs=(VM,) * 5,
        scratch_shapes=[pltpu.VMEM((D, ROWS), BF), pltpu.VMEM((ROWS, 128), F32)],
        compiler_params=params(),
        name="attend",
    )(spot, lens, x, qkv, weights, ln)


def back_pair(pair, qkv, up, pen, lse, total, grads, kept, dk_acc, dv_acc):
    scale = jnp.asarray(0.125, BF)
    k = qkv[:, lanes_of(pair, 1)]
    v = qkv[:, lanes_of(pair, 2)]
    dv_acc[...] = jnp.zeros_like(dv_acc)
    dk_acc[...] = jnp.zeros_like(dk_acc)
    for block in range(4):
        count = (block + 1) * 128
        rows = slice(block * 128, count)
        q = side_by_side(qkv[rows, lanes_of(pair, 0)] * scale)
        u = side_by_side(up[rows, pl.ds(pl.multiple_of(pair * 128, 128), 128)])
        log_total = jnp.concatenate([lse[pair, 0:1, rows], lse[pair, 1:2, rows]], axis=1)
        soft = jnp.exp(dot_nt(k[:count], q) - twice(pen[:count, rows]) - log_total)
        pulled = dot_nt(v[:count], u)
        inner = jnp.sum(pulled * soft, axis=0, keepdims=True)
        dz = soft * (pulled - inner)
        total[:count, rows] = total[:count, rows] + (dz[:, 0:128] + dz[:, 128:256])
        dv_acc[:count, :] = dv_acc[:count, :] + dot_nn(soft.astype(BF), u)
        if kept is not None:
            kept[block, :count, :] = dz
        else:
            low = dz.astype(BF)
            dk_acc[:count, :] = dk_acc[:count, :] + dot_nn(low, q)
            dq = (own_halves(dot_tn(k[:count], low)) * 0.125).T
            grads[rows, lanes_of(pair, 0)] = dq.astype(BF)
    grads[:, lanes_of(pair, 2)] = dv_acc[...].astype(BF)
    if kept is None:
        grads[:, lanes_of(pair, 1)] = dk_acc[...].astype(BF)


def back_first(ends, qkv, total, grads, kept, dk_acc, carry):
    scale = jnp.asarray(0.125, BF)
    k = qkv[:, 128:256]
    row, column = iota((128, 256), 0), iota((128, 256), 1)
    after = one_hot((row > column) | (column >= 128))
    carry[...] = jnp.zeros_like(carry)
    for block in (3, 2, 1, 0):
        count = (block + 1) * 128
        rows = slice(block * 128, count)
        q = side_by_side(qkv[rows, 0:128] * scale)
        _, chosen = block_masks(block, ends)
        high, low = split_low(total[:count, rows])
        sums = dot_nn(high, after) + dot_nn(low, after)
        picked = sums[:, 0:128] + carry[:count, :]
        carry[:count, :] = carry[:count, :] + sums[:, 128:256]
        slope = 1.0 / (1.0 + jnp.exp(-4.0 * dot_nt(k[:count], q[0:128])))
        first = kept[block, :count, 0:128] - jnp.where(chosen, slope * picked, 0.0)
        low = jnp.concatenate([first, kept[block, :count, 128:256]], axis=1).astype(BF)
        dk_acc[:count, :] = dk_acc[:count, :] + dot_nn(low, q)
        grads[rows, 0:128] = (own_halves(dot_tn(k[:count], low)) * 0.125).T.astype(BF)
    grads[:, 128:256] = dk_acc[...].astype(BF)


def put_rows(rows_s, piece, start):
    for row in range(OWN):
        rows_s[pl.ds(start + row, PEERS, stride=STEP), :] = piece[
            row * PEERS : row * PEERS + PEERS
        ]


def back_kernel(
    spot_ref, lens_ref, x_ref, up, vec_ref,
    qkv_hbm, pen_hbm, lse_hbm, w_hbm, ht_hbm,
    oth_ref, own_ref, dh_one_ref,
    qkv, pen, lse, w, ht,
    total, kept, grads, dk_acc, dv_acc, carry, dh_s, vec_s, rows_s, slab_s, sems, out_sems,
):
    spot = (spot_ref[0, 0], spot_ref[0, 1])
    core = spot[0]
    ends = group_ends(lens_ref)
    loads = [
        pltpu.make_async_copy(source, target, sems.at[number])
        for number, (source, target) in enumerate(
            ((qkv_hbm, qkv), (pen_hbm, pen), (lse_hbm, lse), (w_hbm.at[:, 0 : 3 * D], w), (ht_hbm, ht))
        )
    ]
    for load in loads:
        load.start()
    total[...] = jnp.zeros_like(total)
    vec_s[...] = vec_ref[...]
    for load in loads[0:3]:
        load.wait()

    @pl.loop(1, 6)
    def _(pair):
        back_pair(pair, qkv, up, pen, lse, total, grads, None, dk_acc, dv_acc)

    back_pair(0, qkv, up, pen, lse, total, grads, kept, dk_acc, dv_acc)
    back_first(ends, qkv, total, grads, kept, dk_acc, carry)
    for load in loads[3:]:
        load.wait()
    high, low = split_low(dot_nt(grads[...], w[...]))
    place = place_matrix(spot)
    dh_s[...] = dot_nt(high, place) + dot_nt(low, place)

    @pl.loop(0, 4)
    def _(block):
        rows = pl.ds(pl.multiple_of(block * 128, 128), 128)
        unit, _ = norm_stats(x_ref[rows, :].astype(F32))
        gradient = dh_s[rows, :]
        vec_s[0:1, :] = vec_s[0:1, :] + jnp.sum(gradient * unit, axis=0, keepdims=True)
        vec_s[1:2, :] = vec_s[1:2, :] + jnp.sum(gradient, axis=0, keepdims=True)

    store_dh = pltpu.make_async_copy(dh_s, dh_one_ref, out_sems.at[2])
    store_dh.start()
    vectors = [vec_s[which : which + 1, :] for which in range(4)]
    stores = [store_dh]
    for half, target in ((1, oth_ref), (0, own_ref)):
        side = core if half == 0 else 1 - core
        slots = slice(half * HALF, half * HALF + HALF)
        for part in range(3):
            piece = dot_nn(ht[slots, :], grads[:, part * D : part * D + D])
            for block in range(BLOCKS):
                start = (part * BLOCKS + block) * OWN
                put_rows(rows_s, piece[:, block * 128 : block * 128 + 128], start)
        rows_s[pl.ds(OUTER, PEERS, stride=STEP), :] = pack_vectors(vectors, side, spot)

        @pl.loop(0, 8)
        def _(block):
            for peer in range(8):
                start = (block * 8 + peer) * STEP
                slab_s[half, block * 8 + peer] = rows_s[pl.ds(start, TAIL), :].astype(BF)

        store = pltpu.make_async_copy(slab_s.at[half], target, out_sems.at[half])
        store.start()
        stores.append(store)
    for store in stores:
        store.wait()


def back(spot, lens, x, up, vec, qkv, pen, lse, weights, ht):
    slab = jax.ShapeDtypeStruct((PEERS, TAIL, 128), BF)
    return pl.pallas_call(
        back_kernel,
        out_shape=(slab, slab, jax.ShapeDtypeStruct((ROWS, D), F32)),
        in_specs=[SM, SM] + [VM] * 3 + [ANY] * 5,
        out_specs=(ANY,) * 3,
        scratch_shapes=[
            pltpu.VMEM((ROWS, 3 * D), BF),
            pltpu.VMEM((ROWS, ROWS), F32),
            pltpu.VMEM((6, 8, ROWS), F32),
            pltpu.VMEM((D, 3 * D), BF),
            pltpu.VMEM((D, ROWS), BF),
            pltpu.VMEM((ROWS, ROWS), F32),
            pltpu.VMEM((4, ROWS, 256), F32),
            pltpu.VMEM((ROWS, 3 * D), BF),
            pltpu.VMEM((ROWS, 128), F32),
            pltpu.VMEM((ROWS, 128), F32),
            pltpu.VMEM((ROWS, 128), F32),
            pltpu.VMEM((ROWS, D), F32),
            pltpu.VMEM((8, D), F32),
            pltpu.VMEM((PEERS * STEP, 128), F32),
            pltpu.VMEM((2, PEERS, TAIL, 128), BF),
            pltpu.SemaphoreType.DMA((5,)),
            pltpu.SemaphoreType.DMA((3,)),
        ],
        compiler_params=params(),
        name="back",
    )(spot, lens, x, up, vec, qkv, pen, lse, weights, ht)


def feed_kernel(
    spot_ref, lens_ref, middle_ref, h_ref, mixed_ref, wo_ref, ln_ref, cot_ref, late_ref,
    y_ref, grad_ref, dx_ref, up_ref, vec_ref,
    up_s, down_s, mid_s, gup_s, gdown_s, gout_s, dy_s, h_s, acc_s, dh_ref, sems, out_sems,
):
    def load_up(chunk):
        devices = pl.ds(chunk * 32, 32)
        return pltpu.make_async_copy(late_ref.at[devices, 0:16, :], up_s.at[chunk], sems.at[chunk])

    def load_down(chunk):
        devices = pl.ds(chunk * 32, 32)
        return pltpu.make_async_copy(
            late_ref.at[devices, 16:32, :], down_s.at[chunk], sems.at[4 + chunk]
        )

    def load_mid(half):
        devices = pl.ds(half * 64, 64)
        return pltpu.make_async_copy(
            late_ref.at[devices, 32:48, :], mid_s.at[half], sems.at[8 + half]
        )

    def store_big(chunk, block):
        devices = pl.ds(chunk * 32, 32)
        lanes = slice(block * 128, block * 128 + 128)
        return [
            pltpu.make_async_copy(
                grads.at[chunk, :, :, lanes],
                grad_ref.at[devices, block * 48 + offset : block * 48 + offset + 16, :],
                out_sems.at[chunk],
            )
            for grads, offset in ((gup_s, 0), (gdown_s, 16))
        ]

    def store_mid(half, block):
        devices = pl.ds(half * 64, 64)
        lanes = slice(block * 128, block * 128 + 128)
        return pltpu.make_async_copy(
            mid_s.at[half, :, :, lanes],
            grad_ref.at[devices, block * 48 + 32 : block * 48 + 48, :],
            out_sems.at[4 + half],
        )

    for chunk in range(4):
        load_up(chunk).start()
        load_down(chunk).start()
    for half in range(2):
        load_mid(half).start()
    ends = group_ends(lens_ref)
    gain = ln_ref[2:3, :]
    vec_ref[...] = jnp.zeros_like(vec_ref)

    @pl.loop(0, 4)
    def _(block):
        rows = pl.ds(pl.multiple_of(block * 128, 128), 128)
        acc_s[rows, :] = middle_ref[rows, :]
        live = (iota((128, 1), 0) + block * 128) < ends[3]
        dy_s[rows, :] = jnp.where(live, cot_ref[rows, :].astype(F32), 0.0).astype(BF)
        dh_ref[rows, :] = jnp.zeros((128, D), F32)

    def both_ways(up, down):
        value = dot_nt(h_ref[...], up)
        square = value * value
        bend = jnp.tanh(TANH_SCALE * (value + TANH_CUBE * (value * square)))
        act = (0.5 * value * (1.0 + bend)).astype(BF)
        slope = 0.5 * (1.0 + bend) + (0.5 * TANH_SCALE) * value * (1.0 - bend * bend) * (
            1.0 + 3.0 * TANH_CUBE * square
        )
        pulled = (dot_nt(dy_s[...], down) * slope).astype(BF)
        acc_s[...] = acc_s[...] + dot_nn(act, down)
        dh_ref[...] = dh_ref[...] + dot_nn(pulled, up)
        return dot_tn(pulled, h_ref[...]), dot_tn(act, dy_s[...])

    @pl.loop(0, 4)
    def _(chunk):
        load_up(chunk).wait()
        load_down(chunk).wait()
        up_grad, down_grad = both_ways(
            up_s[chunk].reshape(ROWS, D), down_s[chunk].reshape(ROWS, D)
        )
        gup_s[chunk] = up_grad.astype(BF).reshape(32, 16, D)
        gdown_s[chunk] = down_grad.astype(BF).reshape(32, 16, D)
        for block in range(BLOCKS):
            for copy in store_big(chunk, block):
                copy.start()

    @pl.loop(0, 2)
    def _(half):
        load_mid(half).wait()
        mid = mid_s[half].astype(F32)
        up_grad, down_grad = both_ways(
            mid[:, 0:8, :].reshape(ROWS, D).astype(BF), mid[:, 8:16, :].reshape(ROWS, D).astype(BF)
        )
        joined = jnp.concatenate(
            [up_grad.reshape(PEERS, 8, D), down_grad.reshape(PEERS, 8, D)], axis=1
        )
        mid_s[half] = joined.astype(BF)
        for block in range(BLOCKS):
            store_mid(half, block).start()

    @pl.loop(0, 4)
    def _(block):
        rows = pl.ds(pl.multiple_of(block * 128, 128), 128)
        y_ref[rows, :] = acc_s[rows, :].astype(BF)
        unit, inverse = norm_stats(middle_ref[rows, :])
        gradient = dh_ref[rows, :]
        vec_ref[2:3, :] = vec_ref[2:3, :] + jnp.sum(gradient * unit, axis=0, keepdims=True)
        vec_ref[3:4, :] = vec_ref[3:4, :] + jnp.sum(gradient, axis=0, keepdims=True)
        live = (iota((128, 1), 0) + block * 128) < ends[3]
        dy = jnp.where(live, cot_ref[rows, :].astype(F32), 0.0)
        moved = dy + norm_pull(gradient, unit, inverse, gain)
        dx_ref[rows, :] = moved
        h_s[rows, :] = moved.astype(BF)

    outer = dot_tn(mixed_ref[...], h_s[...])
    stores = []
    for block in range(0, BLOCKS, 2):
        pieces = [
            outer[:, at * 128 : at * 128 + 128].reshape(128, 8, 128) for at in (block, block + 1)
        ]
        gout_s[block // 2] = jnp.concatenate(pieces, axis=1).astype(BF)
        start = 288 + block * 8
        store = pltpu.make_async_copy(
            gout_s.at[block // 2], grad_ref.at[:, start : start + 16, :], out_sems.at[6 + block // 2]
        )
        store.start()
        stores.append(store)
    placed = dot_nt(h_s[...], wo_ref[...]).astype(BF)
    up_ref[...] = dot_nt(placed, place_matrix((spot_ref[0, 0], spot_ref[0, 1]))).astype(BF)
    for block in range(BLOCKS):
        for chunk in range(4):
            for copy in store_big(chunk, block):
                copy.wait()
        for half in range(2):
            store_mid(half, block).wait()
    for store in stores:
        store.wait()


def feed(spot, lens, middle, h, mixed, weights, ln, cot, late):
    return pl.pallas_call(
        feed_kernel,
        grid=(1,),
        out_shape=(
            jax.ShapeDtypeStruct((ROWS, D), BF),
            jax.ShapeDtypeStruct((128, WHOLE, 128), BF),
            jax.ShapeDtypeStruct((ROWS, D), F32),
            jax.ShapeDtypeStruct((ROWS, D), BF),
            jax.ShapeDtypeStruct((8, D), F32),
        ),
        in_specs=[SM, SM, VM, VM, VM, OUT_WEIGHT, VM, VM, ANY],
        out_specs=(VM, ANY, VM, VM, VM),
        scratch_shapes=[
            pltpu.VMEM((4, 32, 16, D), BF),
            pltpu.VMEM((4, 32, 16, D), BF),
            pltpu.VMEM((2, PEERS, 16, D), BF),
            pltpu.VMEM((4, 32, 16, D), BF),
            pltpu.VMEM((4, 32, 16, D), BF),
            pltpu.VMEM((3, 128, 16, 128), BF),
            pltpu.VMEM((ROWS, D), BF),
            pltpu.VMEM((ROWS, D), BF),
            pltpu.VMEM((ROWS, D), F32),
            pltpu.VMEM((ROWS, D), F32),
            pltpu.SemaphoreType.DMA((10,)),
            pltpu.SemaphoreType.DMA((9,)),
        ],
        compiler_params=params(),
        name="feed",
    )(spot, lens, middle, h, mixed, weights, ln, cot, late)


def norm_back_kernel(x_ref, dx_ref, dh_ref, ln_ref, dtok_ref):
    @pl.loop(0, 4)
    def _(block):
        rows = pl.ds(pl.multiple_of(block * 128, 128), 128)
        unit, inverse = norm_stats(x_ref[rows, :].astype(F32))
        moved = dx_ref[rows, :] + norm_pull(dh_ref[rows, :], unit, inverse, ln_ref[0:1, :])
        dtok_ref[rows, :] = moved.astype(BF)


def norm_back(x, dx, dh, ln):
    return pl.pallas_call(
        norm_back_kernel,
        out_shape=jax.ShapeDtypeStruct((ROWS, D), BF),
        in_specs=[VM] * 4,
        out_specs=VM,
        compiler_params=params(),
        name="norm_back",
    )(x, dx, dh, ln)


def finish_kernel(*refs):
    slabs, (qkv_ref, g1_ref, b1_ref, g2_ref, b2_ref), sum_s = refs[0:4], refs[4:9], refs[9]
    sum_s[...] = sum(slab[...].astype(F32) for slab in slabs)
    for pair in range(BLOCKS):
        for part in range(3):
            start = (pair * 3 + part) * OWN
            at = part * D + pair * 128
            qkv_ref[:, at : at + 128] = sum_s[start : start + OWN, :]
    for which, target in enumerate((g1_ref, b1_ref, g2_ref, b2_ref)):
        target[...] = sum_s[OUTER : OUTER + 1, which * OWN : which * OWN + OWN]


def finish(slabs):
    vector = jax.ShapeDtypeStruct((1, OWN), F32)
    return pl.pallas_call(
        finish_kernel,
        out_shape=(
            jax.ShapeDtypeStruct((OWN, 3 * D), F32),
            vector, vector, vector, vector,
        ),
        in_specs=[VM] * 4,
        out_specs=(VM,) * 5,
        scratch_shapes=[pltpu.VMEM((TAIL, 128), F32)],
        compiler_params=params(),
        name="finish",
    )(*slabs)


def unpack_kernel(late_ref, up_ref, down_ref, out_ref, sum_s):
    sum_s[...] = jnp.sum(late_ref[...].astype(F32), axis=0)
    for block in range(BLOCKS):
        lanes = slice(block * 128, block * 128 + 128)
        row = block * 48
        up_ref[0:16, lanes] = sum_s[row : row + 16, :]
        down_ref[0:16, lanes] = sum_s[row + 16 : row + 32, :]
        up_ref[16:24, lanes] = sum_s[row + 32 : row + 40, :]
        down_ref[16:24, lanes] = sum_s[row + 40 : row + 48, :]
        row = BLOCKS * 48 + block * 8
        out_ref[:, lanes] = sum_s[row : row + OWN, :]


def unpack(late):
    shard = jax.ShapeDtypeStruct((24, D), F32)
    return pl.pallas_call(
        unpack_kernel,
        out_shape=(shard, shard, jax.ShapeDtypeStruct((OWN, D), F32)),
        in_specs=[VM],
        out_specs=(VM, VM, VM),
        scratch_shapes=[pltpu.VMEM((WHOLE, 128), F32)],
        compiler_params=params(),
        name="unpack",
    )(late)


def fold_kernel(slabs_ref, *sums):
    for back, target in enumerate(sums):
        rows = slice(back * TAIL, back * TAIL + TAIL)
        target[...] = jnp.sum(slabs_ref[:, rows, :].astype(F32), axis=0).astype(BF)


def fold(slabs):
    piece = jax.ShapeDtypeStruct((TAIL, 128), BF)
    return pl.pallas_call(
        fold_kernel,
        out_shape=(piece,) * 4,
        in_specs=[VM],
        out_specs=(VM,) * 4,
        compiler_params=params(),
        name="fold",
    )(slabs)


def exchange(slabs, dims):
    return lax.all_to_all(slabs, AXES, 0, 0, axis_index_groups=peer_groups(dims), tiled=True)


def along_z(ahead):
    return [
        (device_number(x, y, z, c), device_number(x, y, (z + ahead) % 4, c))
        for x, y, z, c in itertools.product(range(4), range(4), range(4), range(2))
    ]


def copies_of_peers(own):
    ring = [own] + [lax.ppermute(own, AXES, along_z(ahead)) for ahead in (1, 2, 3)]
    ring = jnp.concatenate(ring, axis=0)
    return exchange(jnp.broadcast_to(ring, (16, *ring.shape)), "yx").reshape(PEERS, *own.shape)


def sum_over_peers(own, other):
    received = lax.ppermute(other, AXES, core_pairs())
    slab = (own.astype(F32) + received.astype(F32)).astype(BF)
    pieces = fold(exchange(slab.reshape(16, 4 * TAIL, 128), "yx"))
    return [pieces[0]] + [
        lax.ppermute(piece, AXES, along_z(-back)) for back, piece in enumerate(pieces) if back
    ]


def on_device(
    tokens,
    seq_lengths,
    ln1_gain,
    ln1_bias,
    qkv_weight,
    out_weight,
    ln2_gain,
    ln2_bias,
    up_weight,
    down_weight,
    cotangent,
):
    spot = jnp.stack([lax.axis_index("wide") & 1, lax.axis_index("narrow") & 3])
    spot = spot.astype(I32).reshape(1, 2)
    early, late = pack(
        ln1_gain, ln1_bias, qkv_weight, out_weight, ln2_gain, ln2_bias, up_weight.T, down_weight
    )
    late = lax.all_gather(late, AXES, axis_index_groups=peer_groups("zcyx"))
    early_own = copies_of_peers(early)
    early_oth = lax.ppermute(early_own, AXES, core_pairs())
    ht, qkv, weights, norms = project(spot, tokens, early_own, early_oth)
    mixed, middle, h_two, penalty, log_totals = attend(
        spot, seq_lengths, tokens, qkv, weights, norms
    )
    output, late_grad, dx, upstream, vectors = feed(
        spot, seq_lengths, middle, h_two, mixed, weights, norms, cotangent, late
    )
    late_grad = lax.psum_scatter(
        late_grad.reshape(128 * WHOLE, 128),
        AXES,
        scatter_dimension=0,
        axis_index_groups=peer_groups("zc"),
        tiled=True,
    )
    oth, own, dh_one = back(
        spot, seq_lengths, tokens, upstream, vectors, qkv, penalty, log_totals, weights, ht
    )
    tail = sum_over_peers(own, oth)
    dtokens = norm_back(tokens, dx, dh_one, norms)
    late_grad = exchange(late_grad.reshape(16, WHOLE, 128), "yx")
    qkv_grad, g1_grad, b1_grad, g2_grad, b2_grad = finish(tail)
    up_grad, down_grad, out_grad = unpack(late_grad)
    return (
        output,
        dtokens,
        g1_grad.reshape(OWN),
        b1_grad.reshape(OWN),
        qkv_grad,
        out_grad,
        g2_grad.reshape(OWN),
        b2_grad.reshape(OWN),
        up_grad.T,
        down_grad,
    )


def solution(mesh):
    rows = P(AXES, None)
    flat = P(AXES)
    columns = P(None, AXES)
    return jax.shard_map(
        on_device,
        mesh=mesh,
        in_specs=(rows, rows, flat, flat, rows, rows, flat, flat, columns, rows, rows),
        out_specs=(rows, rows, flat, flat, rows, rows, flat, flat, columns, rows),
        check_vma=False,
    )
```

```python
import functools
import itertools

import jax
import jax.numpy as jnp
from jax import lax
from jax.experimental import pallas as pl
from jax.experimental.pallas import tpu as pltpu
from jax.sharding import PartitionSpec as P

BF = jnp.bfloat16
F32 = jnp.float32
I32 = jnp.int32
AXES = ("wide", "narrow")
D = 768
ROWS = 512
FF = 3072
OWN = 6
PEERS = 64
HALF = PEERS * OWN
BLOCKS = 6
OUTER = 3 * OWN * BLOCKS
GATHERED = OUTER + OWN * BLOCKS
EARLY = 152
LATE = 48
WHOLE = 336
TAIL = 112
STEP = TAIL + 1
WIDE = 128 * 8
EPS = 1e-05
FAR = 1e30
TANH_SCALE = 0.7978845608028654
TANH_CUBE = 0.044715
MIB = 1 << 20


def device_number(x, y, z, core):
    return ((x & 1) * 8 + y * 2 + core) * 8 + (x >> 1) * 4 + z


def peer_groups(dims):
    sizes = dict(x=4, y=4, z=4, c=2)
    rest = [name for name in "xyzc" if name not in dims]
    groups = []
    for fixed in itertools.product(*[range(sizes[name]) for name in rest]):
        members = []
        for moving in itertools.product(*[range(sizes[name]) for name in dims]):
            at = dict(zip(rest, fixed))
            at.update(zip(dims, moving))
            members.append(device_number(at["x"], at["y"], at["z"], at["c"]))
        groups.append(members)
    return groups


def core_pairs():
    return [
        (device_number(x, y, z, c), device_number(x, y, z, 1 - c))
        for x, y, z, c in itertools.product(range(4), range(4), range(4), range(2))
    ]


def dot_nn(left, right):
    return lax.dot_general(left, right, (((1,), (0,)), ((), ())), preferred_element_type=F32)


def dot_nt(left, right):
    return lax.dot_general(left, right, (((1,), (1,)), ((), ())), preferred_element_type=F32)


def dot_tn(left, right):
    return lax.dot_general(left, right, (((0,), (0,)), ((), ())), preferred_element_type=F32)


def iota(shape, dim):
    return lax.broadcasted_iota(I32, shape, dim)


def one_hot(mask):
    return jnp.where(mask, 1.0, 0.0).astype(BF)


def split_low(values):
    high = values.astype(BF)
    return high, (values - high.astype(F32)).astype(BF)


def owner(group, core, spot):
    y = (spot[3] - (group >> 4)) & 3
    x = (spot[2] - (group >> 2)) & 3
    z = (spot[1] - group) & 3
    return ((x & 1) << 6) + (y << 4) + (core << 3) + ((x >> 1) << 2) + z


def sixth(number):
    return (number * 43691) >> 18


def place_matrix(spot):
    slot = iota((1, D), 1)
    other = (slot >= HALF).astype(I32)
    inner = slot - HALF * other
    side = spot[0] + other - 2 * spot[0] * other
    feature = owner(inner & (PEERS - 1), side, spot) * OWN + (inner >> 6)
    return one_hot(iota((D, D), 0) == feature)


def place_transposed(spot):
    slot = iota((D, 1), 0)
    other = (slot >= HALF).astype(I32)
    inner = slot - HALF * other
    side = spot[0] + other - 2 * spot[0] * other
    feature = owner(inner & (PEERS - 1), side, spot) * OWN + (inner >> 6)
    return one_hot(iota((D, D), 1) == feature)


def late_owner(group):
    y = group >> 5
    c = (group >> 4) & 1
    z = (group >> 2) & 3
    x = group & 3
    return ((x & 1) << 6) + (y << 4) + (c << 3) + ((x >> 1) << 2) + z


def place_late():
    slot = iota((1, WIDE), 1)
    inner = slot & 7
    feature = jnp.where(inner < OWN, late_owner(slot >> 3) * OWN + inner, -1)
    return one_hot(iota((D, WIDE), 0) == feature)


def vector_lanes(which):
    feature = iota((1, D), 1)
    lane = which * OWN + feature - OWN * sixth(feature)
    return one_hot(iota((128, D), 0) == lane)


def owned_features(core, spot):
    return owner(iota((PEERS, 1), 0), core, spot) == sixth(iota((1, D), 1))


def unpack_vector(packed, mine, which):
    spread = dot_nn(packed.astype(BF), vector_lanes(which))
    return jnp.sum(jnp.where(mine, spread, 0.0), axis=0, keepdims=True)


def pack_vectors(vectors, core, spot):
    mine = owned_features(core, spot)
    total = jnp.zeros((PEERS, 128), F32)
    for which, vector in enumerate(vectors):
        spread = jnp.where(mine, vector, 0.0).astype(BF)
        total = total + dot_nt(spread, vector_lanes(which))
    return total


def norm_stats(values):
    center = values - jnp.mean(values, axis=-1, keepdims=True)
    inverse = lax.rsqrt(jnp.mean(center * center, axis=-1, keepdims=True) + EPS)
    return center * inverse, inverse


def norm_pull(gradient, unit, inverse, gain):
    scaled = gradient * gain
    return inverse * (
        scaled
        - jnp.mean(scaled, axis=-1, keepdims=True)
        - unit * jnp.mean(scaled * unit, axis=-1, keepdims=True)
    )


def group_ends(lens_ref):
    ends = []
    total = 0
    for slot in range(4):
        total = total + lens_ref[0, slot]
        ends.append(total)
    return ends


def segments(positions, ends):
    return sum((positions >= end).astype(I32) for end in ends)


VM = pl.BlockSpec(memory_space=pltpu.VMEM)
SM = pl.BlockSpec(memory_space=pltpu.SMEM)
ANY = pl.BlockSpec(memory_space=pl.ANY)


def params(limit=60):
    return pltpu.CompilerParams(vmem_limit_bytes=limit * MIB)


def pack_kernel(
    g1_ref, b1_ref, qkv_ref, out_ref, g2_ref, b2_ref, up_ref, down_ref, early_ref, late_ref, es
):
    es[...] = jnp.zeros_like(es)
    qkv = qkv_ref[...].astype(F32)
    out = out_ref[...].astype(F32)
    for pair in range(BLOCKS):
        for part in range(3):
            start = (pair * 3 + part) * OWN
            es[start : start + OWN, :] = qkv[:, part * D + pair * 128 : part * D + pair * 128 + 128]
        start = OUTER + pair * OWN
        es[start : start + OWN, :] = out[:, pair * 128 : pair * 128 + 128]
    for which, ref in enumerate((g1_ref, b1_ref, g2_ref, b2_ref)):
        es[GATHERED : GATHERED + 1, which * OWN : which * OWN + OWN] = ref[...].astype(F32)
    early_ref[...] = es[...].astype(BF)
    up = up_ref[...].astype(F32)
    down = down_ref[...].astype(F32)
    late_ref[...] = jnp.concatenate([up[0:16], down[0:16], up[16:24], down[16:24]], axis=0).astype(BF)


def pack(g1, b1, qkv, out, g2, b2, up, down):
    return pl.pallas_call(
        pack_kernel,
        out_shape=(
            jax.ShapeDtypeStruct((EARLY, 128), BF),
            jax.ShapeDtypeStruct((LATE, D), BF),
        ),
        in_specs=[VM] * 8,
        out_specs=(VM, VM),
        scratch_shapes=[pltpu.VMEM((EARLY, 128), F32)],
        compiler_params=params(),
        name="pack",
    )(g1[None], b1[None], qkv, out, g2[None], b2[None], up, down)


def softplus4(logits):
    sharp = 4.0 * logits
    return 0.25 * (jnp.maximum(sharp, 0.0) + jnp.log(1.0 + jnp.exp(-jnp.abs(sharp))))


def block_masks(block, ends):
    count = (block + 1) * 128
    query = iota((1, 128), 1) + block * 128
    key = iota((count, 1), 0)
    same = segments(key, ends) == segments(query, ends)
    first = key == 0
    for end in ends:
        first = first | (key == end)
    allowed = same & (key <= query)
    chosen = same & (key < query) & jnp.logical_not(first)
    return allowed, chosen


def twice(values):
    return jnp.concatenate([values, values], axis=1)


def side_by_side(values):
    left = iota((1, 128), 1) < 64
    zero = jnp.zeros((), BF)
    return jnp.concatenate([jnp.where(left, values, zero), jnp.where(left, zero, values)], axis=0)


def own_halves(values):
    return jnp.concatenate([values[0:64, 0:128], values[64:128, 128:256]], axis=0)


def lanes_of(pair, part):
    return pl.ds(pl.multiple_of(pair * 384 + part * 128, 128), 128)


def front_kernel(
    spot_ref, lens_ref, x_ref, own_ref, oth_ref,
    ht_ref, qkv_ref, w_ref, ln_ref, mixed_ref, middle_ref, h_ref, pen_ref, lse_ref,
    rows_s, w, h_s, qkv, pen, attn_s, carry, sems,
):
    spot = tuple(spot_ref[0, at] for at in range(4))
    core = spot[0]
    vectors = [jnp.zeros((1, D), F32) for _ in range(4)]
    for half, source in enumerate((own_ref, oth_ref)):
        side = core if half == 0 else 1 - core

        @pl.loop(0, 8)
        def _(block):
            for peer in range(8):
                start = (block * 8 + peer) * (EARLY + 1)
                rows_s[pl.ds(start, EARLY), :] = source[block * 8 + peer].astype(F32)

        for block in range(4 * BLOCKS):
            for row in range(OWN):
                to = half * HALF + row * PEERS
                w[to : to + PEERS, block * 128 : block * 128 + 128] = rows_s[
                    pl.ds(block * OWN + row, PEERS, stride=EARLY + 1), :
                ].astype(BF)
        packed = rows_s[pl.ds(GATHERED, PEERS, stride=EARLY + 1), :]
        mine = owned_features(side, spot)
        vectors = [
            vector + unpack_vector(packed, mine, which) for which, vector in enumerate(vectors)
        ]
    store_w = pltpu.make_async_copy(w, w_ref, sems.at[0])
    store_w.start()
    for which, vector in enumerate(vectors):
        ln_ref[which : which + 1, :] = vector
    ln_ref[4:8, :] = jnp.zeros((4, D), F32)

    @pl.loop(0, 4)
    def _(block):
        rows = pl.ds(pl.multiple_of(block * 128, 128), 128)
        unit, _ = norm_stats(x_ref[rows, :].astype(F32))
        h_s[rows, :] = (unit * ln_ref[0:1, :] + ln_ref[1:2, :]).astype(BF)

    place = place_matrix(spot)
    placed = dot_nn(h_s[...], place).astype(BF)
    for part in range(3):
        columns = slice(part * D, part * D + D)
        qkv[:, columns] = dot_nn(placed, w[:, columns]).astype(BF)
    store_qkv = pltpu.make_async_copy(qkv, qkv_ref, sems.at[1])
    store_qkv.start()

    ends = group_ends(lens_ref)
    scale = jnp.asarray(0.125, BF)
    row, column = iota((128, 256), 0), iota((128, 256), 1)
    before = one_hot((row < column) | (column >= 128))
    carry[...] = jnp.zeros_like(carry)
    k0 = qkv[:, 128:256]
    for block in range(4):
        count = (block + 1) * 128
        rows = slice(block * 128, count)
        q0 = side_by_side(qkv[rows, 0:128] * scale)[0:128]
        allowed, chosen = block_masks(block, ends)
        picked = jnp.where(chosen, softplus4(dot_nt(k0[:count], q0)), 0.0)
        high, low = split_low(picked)
        sums = dot_nn(high, before) + dot_nn(low, before)
        pen[:count, rows] = jnp.where(allowed, sums[:, 0:128] + carry[:count, :], FAR)
        carry[:count, :] = carry[:count, :] + sums[:, 128:256]
    store_pen = pltpu.make_async_copy(pen, pen_ref, sems.at[2])
    store_pen.start()

    @pl.loop(0, 3)
    def _(turn):
        for block in range(4):
            count = (block + 1) * 128
            rows = slice(block * 128, count)
            penalty = twice(pen[:count, rows])
            for pair in (2 * turn, 2 * turn + 1):
                k = qkv[:count, lanes_of(pair, 1)]
                v = qkv[:count, lanes_of(pair, 2)]
                q = side_by_side(qkv[rows, lanes_of(pair, 0)] * scale)
                shifted = dot_nt(k, q) - penalty
                top = jnp.max(shifted, axis=0, keepdims=True)
                exponent = jnp.exp(shifted - top)
                total = jnp.sum(exponent, axis=0, keepdims=True)
                mixed = dot_tn(v, exponent.astype(BF)) * (1.0 / total)
                lanes = pl.ds(pl.multiple_of(pair * 128, 128), 128)
                attn_s[lanes, rows] = own_halves(mixed).astype(BF)
                log_total = top + jnp.log(total)
                lse_ref[pair, 0:1, rows] = log_total[:, 0:128]
                lse_ref[pair, 1:2, rows] = log_total[:, 128:256]

    mixed = dot_tn(attn_s[...], place).astype(BF)
    middle_ref[...] = dot_nn(mixed, w[:, 3 * D : 4 * D])

    @pl.loop(0, 4)
    def _(block):
        rows = pl.ds(pl.multiple_of(block * 128, 128), 128)
        middle = x_ref[rows, :].astype(F32) + middle_ref[rows, :]
        middle_ref[rows, :] = middle
        unit, _ = norm_stats(middle)
        h_ref[rows, :] = (unit * ln_ref[2:3, :] + ln_ref[3:4, :]).astype(BF)

    mixed_ref[...] = dot_tn(attn_s[...], place_late()).astype(BF)
    ht_ref[...] = dot_nt(place_transposed(spot), h_s[...]).astype(BF)
    for store in (store_w, store_qkv, store_pen):
        store.wait()


def front(spot, lens, x, own, oth):
    return pl.pallas_call(
        front_kernel,
        out_shape=(
            jax.ShapeDtypeStruct((D, ROWS), BF),
            jax.ShapeDtypeStruct((ROWS, 3 * D), BF),
            jax.ShapeDtypeStruct((D, 4 * D), BF),
            jax.ShapeDtypeStruct((8, D), F32),
            jax.ShapeDtypeStruct((ROWS, WIDE), BF),
            jax.ShapeDtypeStruct((ROWS, D), F32),
            jax.ShapeDtypeStruct((ROWS, D), BF),
            jax.ShapeDtypeStruct((ROWS, ROWS), F32),
            jax.ShapeDtypeStruct((6, 8, ROWS), F32),
        ),
        in_specs=[SM, SM, VM, VM, VM],
        out_specs=(VM, ANY, ANY, VM, VM, VM, VM, ANY, VM),
        scratch_shapes=[
            pltpu.VMEM((PEERS * (EARLY + 1), 128), F32),
            pltpu.VMEM((D, 4 * D), BF),
            pltpu.VMEM((ROWS, D), BF),
            pltpu.VMEM((ROWS, 3 * D), BF),
            pltpu.VMEM((ROWS, ROWS), F32),
            pltpu.VMEM((D, ROWS), BF),
            pltpu.VMEM((ROWS, 128), F32),
            pltpu.SemaphoreType.DMA((3,)),
        ],
        compiler_params=params(),
        name="front",
    )(spot, lens, x, own, oth)


def add_blocks(sums, values):
    for at in range(values.shape[0] // 128):
        part = values[at * 128 : at * 128 + 128]
        if at < len(sums):
            sums[at] = sums[at] + part
        else:
            sums.append(part)


def back_pairs(pairs, qkv, up, pen, lse, total, grads, kept):
    scale = jnp.asarray(0.125, BF)
    dk = [[] for _ in pairs]
    dv = [[] for _ in pairs]
    for block in range(4):
        count = (block + 1) * 128
        rows = slice(block * 128, count)
        penalty = twice(pen[:count, rows])
        gathered = total[:count, rows]
        for at, pair in enumerate(pairs):
            k = qkv[:count, lanes_of(pair, 1)]
            v = qkv[:count, lanes_of(pair, 2)]
            q = side_by_side(qkv[rows, lanes_of(pair, 0)] * scale)
            u = side_by_side(up[rows, pl.ds(pl.multiple_of(pair * 128, 128), 128)])
            log_total = jnp.concatenate([lse[pair, 0:1, rows], lse[pair, 1:2, rows]], axis=1)
            soft = jnp.exp(dot_nt(k, q) - penalty - log_total)
            pulled = dot_nt(v, u)
            inner = jnp.sum(pulled * soft, axis=0, keepdims=True)
            dz = soft * (pulled - inner)
            gathered = gathered + (dz[:, 0:128] + dz[:, 128:256])
            add_blocks(dv[at], dot_nn(soft.astype(BF), u))
            if kept is not None and at == 0:
                kept[block, :count, :] = dz
            else:
                low = dz.astype(BF)
                add_blocks(dk[at], dot_nn(low, q))
                dq = (own_halves(dot_tn(k, low)) * 0.125).T
                grads[rows, lanes_of(pair, 0)] = dq.astype(BF)
        total[:count, rows] = gathered
    for at, pair in enumerate(pairs):
        grads[:, lanes_of(pair, 2)] = jnp.concatenate(dv[at], axis=0).astype(BF)
        if dk[at]:
            grads[:, lanes_of(pair, 1)] = jnp.concatenate(dk[at], axis=0).astype(BF)


def back_first(ends, qkv, total, grads, kept):
    scale = jnp.asarray(0.125, BF)
    row, column = iota((128, 256), 0), iota((128, 256), 1)
    after = one_hot((row > column) | (column >= 128))
    carry = jnp.zeros((ROWS, 128), F32)
    dk = []
    for block in (3, 2, 1, 0):
        count = (block + 1) * 128
        rows = slice(block * 128, count)
        k = qkv[:count, 128:256]
        q = side_by_side(qkv[rows, 0:128] * scale)
        _, chosen = block_masks(block, ends)
        high, low = split_low(total[:count, rows])
        sums = dot_nn(high, after) + dot_nn(low, after)
        picked = sums[:, 0:128] + carry[:count]
        carry = carry[:count] + sums[:, 128:256]
        slope = 1.0 / (1.0 + jnp.exp(-4.0 * dot_nt(k, q[0:128])))
        first = kept[block, :count, 0:128] - jnp.where(chosen, slope * picked, 0.0)
        low = jnp.concatenate([first, kept[block, :count, 128:256]], axis=1).astype(BF)
        add_blocks(dk, dot_nn(low, q))
        grads[rows, 0:128] = (own_halves(dot_tn(k, low)) * 0.125).T.astype(BF)
    grads[:, 128:256] = jnp.concatenate(dk, axis=0).astype(BF)


def put_rows(rows_s, piece, start):
    for row in range(OWN):
        rows_s[pl.ds(start + row, PEERS, stride=STEP), :] = piece[
            row * PEERS : row * PEERS + PEERS
        ]


def back_kernel(
    spot_ref, lens_ref, dx_ref, vec_ref,
    qkv_hbm, pen_hbm, lse_hbm, w_hbm, ht_hbm, x_hbm,
    oth_ref, own_ref, dh_one_ref,
    qkv, pen, lse, w, ht, x_ref, up,
    total, kept, grads, dh_s, vec_s, rows_s, slab_s, sems, out_sems,
):
    spot = tuple(spot_ref[0, at] for at in range(4))
    core = spot[0]
    ends = group_ends(lens_ref)
    loads = [
        pltpu.make_async_copy(source, target, sems.at[number])
        for number, (source, target) in enumerate(
            (
                (w_hbm, w),
                (qkv_hbm, qkv),
                (pen_hbm, pen),
                (lse_hbm, lse),
                (ht_hbm, ht),
                (x_hbm, x_ref),
            )
        )
    ]
    for load in loads:
        load.start()
    total[...] = jnp.zeros_like(total)
    vec_s[...] = vec_ref[...]
    place = place_matrix(spot)
    loads[0].wait()
    placed = dot_nt(dx_ref[...].astype(BF), w[:, 3 * D : 4 * D]).astype(BF)
    up[...] = dot_nt(placed, place).astype(BF)
    for load in loads[1:4]:
        load.wait()

    @pl.loop(0, 2)
    def _(turn):
        back_pairs((2 * turn + 2, 2 * turn + 3), qkv, up, pen, lse, total, grads, None)

    back_pairs((0, 1), qkv, up, pen, lse, total, grads, kept)
    back_first(ends, qkv, total, grads, kept)
    for load in loads[4:]:
        load.wait()
    placed = dot_nt(grads[...], w[:, 0 : 3 * D]).astype(BF)
    dh_s[...] = dot_nt(placed, place)

    @pl.loop(0, 4)
    def _(block):
        rows = pl.ds(pl.multiple_of(block * 128, 128), 128)
        unit, _ = norm_stats(x_ref[rows, :].astype(F32))
        gradient = dh_s[rows, :]
        vec_s[0:1, :] = vec_s[0:1, :] + jnp.sum(gradient * unit, axis=0, keepdims=True)
        vec_s[1:2, :] = vec_s[1:2, :] + jnp.sum(gradient, axis=0, keepdims=True)

    store_dh = pltpu.make_async_copy(dh_s, dh_one_ref, out_sems.at[2])
    store_dh.start()
    vectors = [vec_s[which : which + 1, :] for which in range(4)]
    stores = [store_dh]
    for half, target in ((1, oth_ref), (0, own_ref)):
        side = core if half == 0 else 1 - core
        slots = slice(half * HALF, half * HALF + HALF)
        for part in range(3):
            piece = dot_nn(ht[slots, :], grads[:, part * D : part * D + D])
            for block in range(BLOCKS):
                start = (part * BLOCKS + block) * OWN
                put_rows(rows_s, piece[:, block * 128 : block * 128 + 128], start)
        rows_s[pl.ds(OUTER, PEERS, stride=STEP), :] = pack_vectors(vectors, side, spot)

        @pl.loop(0, 8)
        def _(block):
            for peer in range(8):
                group = block * 8 + peer
                z, x = (spot[1] - group) & 3, (spot[2] - (group >> 2)) & 3
                to = z * 16 + x * 4 + (group >> 4)
                slab_s[half, to] = rows_s[pl.ds(group * STEP, TAIL), :].astype(BF)

        store = pltpu.make_async_copy(slab_s.at[half], target, out_sems.at[half])
        store.start()
        stores.append(store)
    for store in stores:
        store.wait()


def back(spot, lens, dx, vec, qkv, pen, lse, weights, ht, x):
    slab = jax.ShapeDtypeStruct((PEERS, TAIL, 128), BF)
    return pl.pallas_call(
        back_kernel,
        out_shape=(slab, slab, jax.ShapeDtypeStruct((ROWS, D), F32)),
        in_specs=[SM, SM, VM, VM] + [ANY] * 6,
        out_specs=(ANY,) * 3,
        scratch_shapes=[
            pltpu.VMEM((ROWS, 3 * D), BF),
            pltpu.VMEM((ROWS, ROWS), F32),
            pltpu.VMEM((6, 8, ROWS), F32),
            pltpu.VMEM((D, 4 * D), BF),
            pltpu.VMEM((D, ROWS), BF),
            pltpu.VMEM((ROWS, D), BF),
            pltpu.VMEM((ROWS, D), BF),
            pltpu.VMEM((ROWS, ROWS), F32),
            pltpu.VMEM((4, ROWS, 256), F32),
            pltpu.VMEM((ROWS, 3 * D), BF),
            pltpu.VMEM((ROWS, D), F32),
            pltpu.VMEM((8, D), F32),
            pltpu.VMEM((PEERS * STEP, 128), F32),
            pltpu.VMEM((2, PEERS, TAIL, 128), BF),
            pltpu.SemaphoreType.DMA((6,)),
            pltpu.SemaphoreType.DMA((3,)),
        ],
        compiler_params=params(),
        name="back",
    )(spot, lens, dx, vec, qkv, pen, lse, weights, ht, x)


def feed_kernel(
    lens_ref, middle_ref, h_ref, ln_ref, cot_ref, mixed_hbm, late_ref,
    y_ref, grad_ref, dx_ref, vec_ref,
    up_s, down_s, mid_s, gup_s, gdown_s, gout_s, mixed_s, dy_s, h_s, y_s, dx_s, acc_s, dh_ref, sems, out_sems,
):
    def load_up(chunk):
        devices = pl.ds(chunk * 32, 32)
        return pltpu.make_async_copy(late_ref.at[devices, 0:16, :], up_s.at[chunk], sems.at[chunk])

    def load_down(chunk):
        devices = pl.ds(chunk * 32, 32)
        return pltpu.make_async_copy(
            late_ref.at[devices, 16:32, :], down_s.at[chunk], sems.at[4 + chunk]
        )

    def load_mid(half):
        devices = pl.ds(half * 64, 64)
        return pltpu.make_async_copy(
            late_ref.at[devices, 32:48, :], mid_s.at[half], sems.at[8 + half]
        )

    def store_big(chunk, block):
        devices = pl.ds(chunk * 32, 32)
        lanes = slice(block * 128, block * 128 + 128)
        return [
            pltpu.make_async_copy(
                grads.at[chunk, :, :, lanes],
                grad_ref.at[devices, block * 48 + offset : block * 48 + offset + 16, :],
                out_sems.at[chunk],
            )
            for grads, offset in ((gup_s, 0), (gdown_s, 16))
        ]

    def store_mid(half, block):
        devices = pl.ds(half * 64, 64)
        lanes = slice(block * 128, block * 128 + 128)
        return pltpu.make_async_copy(
            mid_s.at[half, :, :, lanes],
            grad_ref.at[devices, block * 48 + 32 : block * 48 + 48, :],
            out_sems.at[4 + half],
        )

    for chunk in range(4):
        load_up(chunk).start()
        load_down(chunk).start()
    for half in range(2):
        load_mid(half).start()
    load_mixed = pltpu.make_async_copy(mixed_hbm, mixed_s, sems.at[10])
    load_mixed.start()
    ends = group_ends(lens_ref)
    gain = ln_ref[2:3, :]
    vec_ref[...] = jnp.zeros_like(vec_ref)

    @pl.loop(0, 4)
    def _(block):
        rows = pl.ds(pl.multiple_of(block * 128, 128), 128)
        acc_s[rows, :] = middle_ref[rows, :]
        live = (iota((128, 1), 0) + block * 128) < ends[3]
        dy_s[rows, :] = jnp.where(live, cot_ref[rows, :].astype(F32), 0.0).astype(BF)
        dh_ref[rows, :] = jnp.zeros((128, D), F32)

    def both_ways(up, down):
        value = dot_nt(h_ref[...], up)
        square = value * value
        bend = jnp.tanh(TANH_SCALE * (value + TANH_CUBE * (value * square)))
        act = (0.5 * value * (1.0 + bend)).astype(BF)
        slope = 0.5 * (1.0 + bend) + (0.5 * TANH_SCALE) * value * (1.0 - bend * bend) * (
            1.0 + 3.0 * TANH_CUBE * square
        )
        pulled = (dot_nt(dy_s[...], down) * slope).astype(BF)
        acc_s[...] = acc_s[...] + dot_nn(act, down)
        dh_ref[...] = dh_ref[...] + dot_nn(pulled, up)
        return dot_tn(pulled, h_ref[...]), dot_tn(act, dy_s[...])

    @pl.loop(0, 4)
    def _(chunk):
        load_up(chunk).wait()
        load_down(chunk).wait()
        up_grad, down_grad = both_ways(
            up_s[chunk].reshape(ROWS, D), down_s[chunk].reshape(ROWS, D)
        )
        gup_s[chunk] = up_grad.astype(BF).reshape(32, 16, D)
        gdown_s[chunk] = down_grad.astype(BF).reshape(32, 16, D)
        for block in range(BLOCKS):
            for copy in store_big(chunk, block):
                copy.start()

    @pl.loop(0, 2)
    def _(half):
        load_mid(half).wait()
        mid = mid_s[half].astype(F32)
        up_grad, down_grad = both_ways(
            mid[:, 0:8, :].reshape(ROWS, D).astype(BF), mid[:, 8:16, :].reshape(ROWS, D).astype(BF)
        )
        joined = jnp.concatenate(
            [up_grad.reshape(PEERS, 8, D), down_grad.reshape(PEERS, 8, D)], axis=1
        )
        mid_s[half] = joined.astype(BF)
        for block in range(BLOCKS):
            store_mid(half, block).start()

    @pl.loop(0, 4)
    def _(block):
        rows = pl.ds(pl.multiple_of(block * 128, 128), 128)
        y_s[rows, :] = acc_s[rows, :].astype(BF)
        unit, inverse = norm_stats(middle_ref[rows, :])
        gradient = dh_ref[rows, :]
        vec_ref[2:3, :] = vec_ref[2:3, :] + jnp.sum(gradient * unit, axis=0, keepdims=True)
        vec_ref[3:4, :] = vec_ref[3:4, :] + jnp.sum(gradient, axis=0, keepdims=True)
        live = (iota((128, 1), 0) + block * 128) < ends[3]
        dy = jnp.where(live, cot_ref[rows, :].astype(F32), 0.0)
        moved = dy + norm_pull(gradient, unit, inverse, gain)
        dx_s[rows, :] = moved
        h_s[rows, :] = moved.astype(BF)

    store_y = pltpu.make_async_copy(y_s, y_ref, out_sems.at[9])
    store_y.start()
    store_dx = pltpu.make_async_copy(dx_s, dx_ref, out_sems.at[10])
    store_dx.start()
    load_mixed.wait()
    outer = dot_tn(mixed_s[...], h_s[...])
    stores = []
    for block in range(0, BLOCKS, 2):
        pieces = [
            outer[:, at * 128 : at * 128 + 128].reshape(128, 8, 128) for at in (block, block + 1)
        ]
        gout_s[block // 2] = jnp.concatenate(pieces, axis=1).astype(BF)
        start = 288 + block * 8
        store = pltpu.make_async_copy(
            gout_s.at[block // 2], grad_ref.at[:, start : start + 16, :], out_sems.at[6 + block // 2]
        )
        store.start()
        stores.append(store)
    for block in range(BLOCKS):
        for chunk in range(4):
            for copy in store_big(chunk, block):
                copy.wait()
        for half in range(2):
            store_mid(half, block).wait()
    for store in (store_y, store_dx, *stores):
        store.wait()


def feed(lens, middle, h, ln, cot, mixed, late):
    return pl.pallas_call(
        feed_kernel,
        out_shape=(
            jax.ShapeDtypeStruct((ROWS, D), BF),
            jax.ShapeDtypeStruct((128, WHOLE, 128), BF),
            jax.ShapeDtypeStruct((ROWS, D), F32),
            jax.ShapeDtypeStruct((8, D), F32),
        ),
        in_specs=[SM, VM, VM, VM, VM, ANY, ANY],
        out_specs=(ANY, ANY, ANY, VM),
        scratch_shapes=[
            pltpu.VMEM((4, 32, 16, D), BF),
            pltpu.VMEM((4, 32, 16, D), BF),
            pltpu.VMEM((2, PEERS, 16, D), BF),
            pltpu.VMEM((4, 32, 16, D), BF),
            pltpu.VMEM((4, 32, 16, D), BF),
            pltpu.VMEM((3, 128, 16, 128), BF),
            pltpu.VMEM((ROWS, WIDE), BF),
            pltpu.VMEM((ROWS, D), BF),
            pltpu.VMEM((ROWS, D), BF),
            pltpu.VMEM((ROWS, D), BF),
            pltpu.VMEM((ROWS, D), F32),
            pltpu.VMEM((ROWS, D), F32),
            pltpu.VMEM((ROWS, D), F32),
            pltpu.SemaphoreType.DMA((11,)),
            pltpu.SemaphoreType.DMA((11,)),
        ],
        compiler_params=params(),
        name="feed",
    )(lens, middle, h, ln, cot, mixed, late)


def norm_back_kernel(x_ref, dx_ref, dh_ref, ln_ref, dtok_ref):
    @pl.loop(0, 4)
    def _(block):
        rows = pl.ds(pl.multiple_of(block * 128, 128), 128)
        unit, inverse = norm_stats(x_ref[rows, :].astype(F32))
        moved = dx_ref[rows, :] + norm_pull(dh_ref[rows, :], unit, inverse, ln_ref[0:1, :])
        dtok_ref[rows, :] = moved.astype(BF)


def norm_back(x, dx, dh, ln):
    return pl.pallas_call(
        norm_back_kernel,
        out_shape=jax.ShapeDtypeStruct((ROWS, D), BF),
        in_specs=[VM] * 4,
        out_specs=VM,
        compiler_params=params(),
        name="norm_back",
    )(x, dx, dh, ln)


def finish_kernel(*refs):
    slabs, (qkv_ref, g1_ref, b1_ref, g2_ref, b2_ref), sum_s = refs[0:4], refs[4:9], refs[9]
    sum_s[...] = sum(slab[...].astype(F32) for slab in slabs)
    for pair in range(BLOCKS):
        for part in range(3):
            start = (pair * 3 + part) * OWN
            at = part * D + pair * 128
            qkv_ref[:, at : at + 128] = sum_s[start : start + OWN, :]
    for which, target in enumerate((g1_ref, b1_ref, g2_ref, b2_ref)):
        target[...] = sum_s[OUTER : OUTER + 1, which * OWN : which * OWN + OWN]


def finish(slabs):
    vector = jax.ShapeDtypeStruct((1, OWN), F32)
    return pl.pallas_call(
        finish_kernel,
        out_shape=(
            jax.ShapeDtypeStruct((OWN, 3 * D), F32),
            vector, vector, vector, vector,
        ),
        in_specs=[VM] * 4,
        out_specs=(VM,) * 5,
        scratch_shapes=[pltpu.VMEM((TAIL, 128), F32)],
        compiler_params=params(16),
        name="finish",
    )(*slabs)


def unpack_kernel(late_ref, up_ref, down_ref, out_ref, sum_s):
    sum_s[...] = jnp.sum(late_ref[...].astype(F32), axis=0)
    for block in range(BLOCKS):
        lanes = slice(block * 128, block * 128 + 128)
        row = block * 48
        up_ref[0:16, lanes] = sum_s[row : row + 16, :]
        down_ref[0:16, lanes] = sum_s[row + 16 : row + 32, :]
        up_ref[16:24, lanes] = sum_s[row + 32 : row + 40, :]
        down_ref[16:24, lanes] = sum_s[row + 40 : row + 48, :]
        row = BLOCKS * 48 + block * 8
        out_ref[:, lanes] = sum_s[row : row + OWN, :]


def unpack(late):
    shard = jax.ShapeDtypeStruct((24, D), F32)
    return pl.pallas_call(
        unpack_kernel,
        out_shape=(shard, shard, jax.ShapeDtypeStruct((OWN, D), F32)),
        in_specs=[VM],
        out_specs=(VM, VM, VM),
        scratch_shapes=[pltpu.VMEM((WHOLE, 128), F32)],
        compiler_params=params(16),
        name="unpack",
    )(late)


def fold_kernel(slabs_ref, *sums):
    for back, target in enumerate(sums):
        rows = slice(back * TAIL, back * TAIL + TAIL)
        target[...] = jnp.sum(slabs_ref[:, rows, :].astype(F32), axis=0).astype(BF)


def fold(slabs):
    piece = jax.ShapeDtypeStruct((TAIL, 128), BF)
    return pl.pallas_call(
        fold_kernel,
        out_shape=(piece,) * 4,
        in_specs=[VM],
        out_specs=(VM,) * 4,
        compiler_params=params(16),
        name="fold",
    )(slabs)


def exchange(slabs, dims):
    return lax.all_to_all(slabs, AXES, 0, 0, axis_index_groups=peer_groups(dims), tiled=True)


def shift(values, dim, ahead):
    pairs = []
    for x, y, z, c in itertools.product(range(4), range(4), range(4), range(2)):
        to = dict(x=x, y=y, z=z)
        to[dim] = (to[dim] + ahead) % 4
        pairs.append((device_number(x, y, z, c), device_number(to["x"], to["y"], to["z"], c)))
    return lax.ppermute(values, AXES, pairs)


def ring(own, dim):
    return jnp.concatenate([own] + [shift(own, dim, ahead) for ahead in (1, 2, 3)], axis=0)


def wide_ring(own, dim):
    half = own.shape[0] // 2
    near, last = shift(own, dim, 1), shift(own, dim, -1)
    far = [shift(near[:half], dim, 1), shift(last[half:], dim, -1)]
    return jnp.concatenate([own, near, *far, last], axis=0)


def copies_of_peers(own):
    return wide_ring(ring(ring(own, "z"), "x"), "y").reshape(PEERS, *own.shape)


def sum_over_peers(own, other):
    received = lax.ppermute(other, AXES, core_pairs())
    slab = (own.astype(F32) + received.astype(F32)).astype(BF)
    pieces = fold(exchange(slab.reshape(16, 4 * TAIL, 128), "zx"))
    return [pieces[0]] + [
        shift(piece, "y", -back) for back, piece in enumerate(pieces) if back
    ]


def on_device(
    tokens,
    seq_lengths,
    ln1_gain,
    ln1_bias,
    qkv_weight,
    out_weight,
    ln2_gain,
    ln2_bias,
    up_weight,
    down_weight,
    cotangent,
):
    wide, narrow = lax.axis_index("wide"), lax.axis_index("narrow")
    spot = jnp.stack([wide & 1, narrow & 3, (narrow >> 2) * 2 + (wide >> 3), (wide >> 1) & 3])
    spot = spot.astype(I32).reshape(1, 4)
    early, late = pack(
        ln1_gain, ln1_bias, qkv_weight, out_weight, ln2_gain, ln2_bias, up_weight.T, down_weight
    )
    late = lax.all_gather(late, AXES, axis_index_groups=peer_groups("yczx"))
    early_own = copies_of_peers(early)
    early_oth = lax.ppermute(early_own, AXES, core_pairs())
    ht, qkv, weights, norms, mixed, middle, h_two, penalty, log_totals = front(
        spot, seq_lengths, tokens, early_own, early_oth
    )
    output, late_grad, dx, vectors = feed(
        seq_lengths, middle, h_two, norms, cotangent, mixed, late
    )
    late_grad = lax.psum_scatter(
        late_grad.reshape(128 * WHOLE, 128),
        AXES,
        scatter_dimension=0,
        axis_index_groups=peer_groups("yc"),
        tiled=True,
    )
    oth, own, dh_one = back(
        spot, seq_lengths, dx, vectors, qkv, penalty, log_totals, weights, ht, tokens
    )
    tail = sum_over_peers(own, oth)
    dtokens = norm_back(tokens, dx, dh_one, norms)
    late_grad = exchange(late_grad.reshape(16, WHOLE, 128), "zx")
    qkv_grad, g1_grad, b1_grad, g2_grad, b2_grad = finish(tail)
    up_grad, down_grad, out_grad = unpack(late_grad)
    return (
        output,
        dtokens,
        g1_grad.reshape(OWN),
        b1_grad.reshape(OWN),
        qkv_grad,
        out_grad,
        g2_grad.reshape(OWN),
        b2_grad.reshape(OWN),
        up_grad.T,
        down_grad,
    )


def solution(mesh):
    rows = P(AXES, None)
    flat = P(AXES)
    columns = P(None, AXES)
    return jax.shard_map(
        on_device,
        mesh=mesh,
        in_specs=(rows, rows, flat, flat, rows, rows, flat, flat, columns, rows, rows),
        out_specs=(rows, rows, flat, flat, rows, rows, flat, flat, columns, rows),
        check_vma=False,
    )
```

```python
import functools
import itertools

import jax
import jax.numpy as jnp
from jax import lax
from jax.experimental import pallas as pl
from jax.experimental.pallas import tpu as pltpu
from jax.sharding import PartitionSpec as P

BF = jnp.bfloat16
F32 = jnp.float32
I32 = jnp.int32
AXES = ("wide", "narrow")
D = 768
ROWS = 512
FF = 3072
OWN = 6
PEERS = 64
HALF = PEERS * OWN
BLOCKS = 6
OUTER = 3 * OWN * BLOCKS
GATHERED = OUTER + OWN * BLOCKS
EARLY = 152
LATE = 48
WHOLE = 288
TAIL = 152
STEP = TAIL + 1
EPS = 1e-05
FAR = 1e30
TANH_SCALE = 0.7978845608028654
TANH_CUBE = 0.044715
MIB = 1 << 20


def device_number(x, y, z, core):
    return ((x & 1) * 8 + y * 2 + core) * 8 + (x >> 1) * 4 + z


def peer_groups(dims):
    sizes = dict(x=4, y=4, z=4, c=2)
    rest = [name for name in "xyzc" if name not in dims]
    groups = []
    for fixed in itertools.product(*[range(sizes[name]) for name in rest]):
        members = []
        for moving in itertools.product(*[range(sizes[name]) for name in dims]):
            at = dict(zip(rest, fixed))
            at.update(zip(dims, moving))
            members.append(device_number(at["x"], at["y"], at["z"], at["c"]))
        groups.append(members)
    return groups


def mixed_groups(first, second):
    halves = [peer_groups(dims) for dims in (first, second)]
    return [
        group
        for core, groups in enumerate(halves)
        for group in groups
        if (group[0] >> 3) & 1 == core
    ]


def core_pairs():
    return [
        (device_number(x, y, z, c), device_number(x, y, z, 1 - c))
        for x, y, z, c in itertools.product(range(4), range(4), range(4), range(2))
    ]


def dot_nn(left, right):
    return lax.dot_general(left, right, (((1,), (0,)), ((), ())), preferred_element_type=F32)


def dot_nt(left, right):
    return lax.dot_general(left, right, (((1,), (1,)), ((), ())), preferred_element_type=F32)


def dot_tn(left, right):
    return lax.dot_general(left, right, (((0,), (0,)), ((), ())), preferred_element_type=F32)


def iota(shape, dim):
    return lax.broadcasted_iota(I32, shape, dim)


def one_hot(mask):
    return jnp.where(mask, 1.0, 0.0).astype(BF)


def split_low(values):
    high = values.astype(BF)
    return high, (values - high.astype(F32)).astype(BF)


def owner(group, core, spot):
    far, near = group >> 4, group & 3
    y = (spot[3] - (far + core * (near - far))) & 3
    x = (spot[2] - (group >> 2)) & 3
    z = (spot[1] - (near + core * (far - near))) & 3
    return ((x & 1) << 6) + (y << 4) + (core << 3) + ((x >> 1) << 2) + z


def sixth(number):
    return (number * 43691) >> 18


def place_matrix(spot):
    slot = iota((1, D), 1)
    other = (slot >= HALF).astype(I32)
    inner = slot - HALF * other
    side = spot[0] + other - 2 * spot[0] * other
    feature = owner(inner & (PEERS - 1), side, spot) * OWN + (inner >> 6)
    return one_hot(iota((D, D), 0) == feature)


def place_transposed(spot):
    slot = iota((D, 1), 0)
    other = (slot >= HALF).astype(I32)
    inner = slot - HALF * other
    side = spot[0] + other - 2 * spot[0] * other
    feature = owner(inner & (PEERS - 1), side, spot) * OWN + (inner >> 6)
    return one_hot(iota((D, D), 1) == feature)


def vector_lanes(which):
    feature = iota((1, D), 1)
    lane = which * OWN + feature - OWN * sixth(feature)
    return one_hot(iota((128, D), 0) == lane)


def owned_features(core, spot):
    return owner(iota((PEERS, 1), 0), core, spot) == sixth(iota((1, D), 1))


def unpack_vector(packed, mine, which):
    spread = dot_nn(packed.astype(BF), vector_lanes(which))
    return jnp.sum(jnp.where(mine, spread, 0.0), axis=0, keepdims=True)


def pack_vectors(vectors, core, spot):
    mine = owned_features(core, spot)
    total = jnp.zeros((PEERS, 128), F32)
    for which, vector in enumerate(vectors):
        spread = jnp.where(mine, vector, 0.0).astype(BF)
        total = total + dot_nt(spread, vector_lanes(which))
    return total


def norm_stats(values):
    center = values - jnp.mean(values, axis=-1, keepdims=True)
    inverse = lax.rsqrt(jnp.mean(center * center, axis=-1, keepdims=True) + EPS)
    return center * inverse, inverse


def norm_pull(gradient, unit, inverse, gain):
    scaled = gradient * gain
    return inverse * (
        scaled
        - jnp.mean(scaled, axis=-1, keepdims=True)
        - unit * jnp.mean(scaled * unit, axis=-1, keepdims=True)
    )


def group_ends(lens_ref):
    ends = []
    total = 0
    for slot in range(4):
        total = total + lens_ref[0, slot]
        ends.append(total)
    return ends


def segments(positions, ends):
    return sum((positions >= end).astype(I32) for end in ends)


VM = pl.BlockSpec(memory_space=pltpu.VMEM)
SM = pl.BlockSpec(memory_space=pltpu.SMEM)
ANY = pl.BlockSpec(memory_space=pl.ANY)


def params(limit=60):
    return pltpu.CompilerParams(vmem_limit_bytes=limit * MIB)


def pack_kernel(
    g1_ref, b1_ref, qkv_ref, out_ref, g2_ref, b2_ref, up_ref, down_ref, early_ref, late_ref, es
):
    es[...] = jnp.zeros_like(es)
    qkv = qkv_ref[...].astype(F32)
    out = out_ref[...].astype(F32)
    for pair in range(BLOCKS):
        for part in range(3):
            start = (pair * 3 + part) * OWN
            es[start : start + OWN, :] = qkv[:, part * D + pair * 128 : part * D + pair * 128 + 128]
        start = OUTER + pair * OWN
        es[start : start + OWN, :] = out[:, pair * 128 : pair * 128 + 128]
    for which, ref in enumerate((g1_ref, b1_ref, g2_ref, b2_ref)):
        es[GATHERED : GATHERED + 1, which * OWN : which * OWN + OWN] = ref[...].astype(F32)
    early_ref[...] = es[...].astype(BF)
    up = up_ref[...].astype(F32)
    down = down_ref[...].astype(F32)
    late_ref[...] = jnp.concatenate([up[0:16], down[0:16], up[16:24], down[16:24]], axis=0).astype(BF)


def pack(g1, b1, qkv, out, g2, b2, up, down):
    return pl.pallas_call(
        pack_kernel,
        out_shape=(
            jax.ShapeDtypeStruct((EARLY, 128), BF),
            jax.ShapeDtypeStruct((LATE, D), BF),
        ),
        in_specs=[VM] * 8,
        out_specs=(VM, VM),
        scratch_shapes=[pltpu.VMEM((EARLY, 128), F32)],
        compiler_params=params(),
        name="pack",
    )(g1[None], b1[None], qkv, out, g2[None], b2[None], up, down)


def softplus4(logits):
    sharp = 4.0 * logits
    return 0.25 * (jnp.maximum(sharp, 0.0) + jnp.log(1.0 + jnp.exp(-jnp.abs(sharp))))


def block_masks(block, ends):
    count = (block + 1) * 128
    query = iota((1, 128), 1) + block * 128
    key = iota((count, 1), 0)
    same = segments(key, ends) == segments(query, ends)
    first = key == 0
    for end in ends:
        first = first | (key == end)
    allowed = same & (key <= query)
    chosen = same & (key < query) & jnp.logical_not(first)
    return allowed, chosen


def twice(values):
    return jnp.concatenate([values, values], axis=1)


def side_by_side(values):
    left = iota((1, 128), 1) < 64
    zero = jnp.zeros((), BF)
    return jnp.concatenate([jnp.where(left, values, zero), jnp.where(left, zero, values)], axis=0)


def own_halves(values):
    return jnp.concatenate([values[0:64, 0:128], values[64:128, 128:256]], axis=0)


def lanes_of(pair, part):
    return pl.ds(pl.multiple_of(pair * 384 + part * 128, 128), 128)


def front_kernel(
    spot_ref, lens_ref, x_ref, own_ref, oth_ref,
    ht_ref, qkv_ref, w_ref, ln_ref, mixed_ref, middle_ref, h_ref, soft_ref,
    rows_s, w, h_s, qkv, pen, soft_s, attn_s, carry, sems,
):
    spot = tuple(spot_ref[0, at] for at in range(4))
    core = spot[0]
    vectors = [jnp.zeros((1, D), F32) for _ in range(4)]
    for half, source in enumerate((own_ref, oth_ref)):
        side = core if half == 0 else 1 - core

        @pl.loop(0, 8)
        def _(block):
            for peer in range(8):
                start = (block * 8 + peer) * (EARLY + 1)
                rows_s[pl.ds(start, EARLY), :] = source[block * 8 + peer].astype(F32)

        for block in range(4 * BLOCKS):
            for row in range(OWN):
                to = half * HALF + row * PEERS
                w[to : to + PEERS, block * 128 : block * 128 + 128] = rows_s[
                    pl.ds(block * OWN + row, PEERS, stride=EARLY + 1), :
                ].astype(BF)
        packed = rows_s[pl.ds(GATHERED, PEERS, stride=EARLY + 1), :]
        mine = owned_features(side, spot)
        vectors = [
            vector + unpack_vector(packed, mine, which) for which, vector in enumerate(vectors)
        ]
    store_w = pltpu.make_async_copy(w, w_ref, sems.at[0])
    store_w.start()
    for which, vector in enumerate(vectors):
        ln_ref[which : which + 1, :] = vector
    ln_ref[4:8, :] = jnp.zeros((4, D), F32)

    @pl.loop(0, 4)
    def _(block):
        rows = pl.ds(pl.multiple_of(block * 128, 128), 128)
        unit, _ = norm_stats(x_ref[rows, :].astype(F32))
        h_s[rows, :] = (unit * ln_ref[0:1, :] + ln_ref[1:2, :]).astype(BF)

    place = place_matrix(spot)
    placed = dot_nn(h_s[...], place).astype(BF)
    for part in range(3):
        columns = slice(part * D, part * D + D)
        qkv[:, columns] = dot_nn(placed, w[:, columns]).astype(BF)
    store_qkv = pltpu.make_async_copy(qkv, qkv_ref, sems.at[1])
    store_qkv.start()

    ends = group_ends(lens_ref)
    scale = jnp.asarray(0.125, BF)
    row, column = iota((128, 256), 0), iota((128, 256), 1)
    before = one_hot((row < column) | (column >= 128))
    carry[...] = jnp.zeros_like(carry)
    k0 = qkv[:, 128:256]
    for block in range(4):
        count = (block + 1) * 128
        rows = slice(block * 128, count)
        q0 = side_by_side(qkv[rows, 0:128] * scale)[0:128]
        allowed, chosen = block_masks(block, ends)
        picked = jnp.where(chosen, softplus4(dot_nt(k0[:count], q0)), 0.0)
        high, low = split_low(picked)
        sums = dot_nn(high, before) + dot_nn(low, before)
        pen[:count, rows] = jnp.where(allowed, sums[:, 0:128] + carry[:count, :], FAR)
        carry[:count, :] = carry[:count, :] + sums[:, 128:256]

    def store_soft(pair):
        return pltpu.make_async_copy(soft_s.at[pair], soft_ref.at[pair], sems.at[2])

    @pl.loop(0, 3)
    def _(turn):
        for block in range(4):
            count = (block + 1) * 128
            rows = slice(block * 128, count)
            penalty = twice(pen[:count, rows])
            for pair in (2 * turn, 2 * turn + 1):
                k = qkv[:count, lanes_of(pair, 1)]
                v = qkv[:count, lanes_of(pair, 2)]
                q = side_by_side(qkv[rows, lanes_of(pair, 0)] * scale)
                shifted = dot_nt(k, q) - penalty
                top = jnp.max(shifted, axis=0, keepdims=True)
                exponent = jnp.exp(shifted - top)
                total = jnp.sum(exponent, axis=0, keepdims=True)
                soft = (exponent * (1.0 / total)).astype(BF)
                soft_s[pair, :count, block * 256 : block * 256 + 256] = soft
                lanes = pl.ds(pl.multiple_of(pair * 128, 128), 128)
                attn_s[lanes, rows] = own_halves(dot_tn(v, soft)).astype(BF)
        store_soft(2 * turn).start()
        store_soft(2 * turn + 1).start()

    mixed_ref[...] = dot_tn(attn_s[...], place).astype(BF)
    middle_ref[...] = dot_nn(mixed_ref[...], w[:, 3 * D : 4 * D])

    @pl.loop(0, 4)
    def _(block):
        rows = pl.ds(pl.multiple_of(block * 128, 128), 128)
        middle = x_ref[rows, :].astype(F32) + middle_ref[rows, :]
        middle_ref[rows, :] = middle
        unit, _ = norm_stats(middle)
        h_ref[rows, :] = (unit * ln_ref[2:3, :] + ln_ref[3:4, :]).astype(BF)

    ht_ref[...] = dot_nt(place_transposed(spot), h_s[...]).astype(BF)
    for store in (store_w, store_qkv, *(store_soft(pair) for pair in range(6))):
        store.wait()


def front(spot, lens, x, own, oth):
    return pl.pallas_call(
        front_kernel,
        out_shape=(
            jax.ShapeDtypeStruct((D, ROWS), BF),
            jax.ShapeDtypeStruct((ROWS, 3 * D), BF),
            jax.ShapeDtypeStruct((D, 4 * D), BF),
            jax.ShapeDtypeStruct((8, D), F32),
            jax.ShapeDtypeStruct((ROWS, D), BF),
            jax.ShapeDtypeStruct((ROWS, D), F32),
            jax.ShapeDtypeStruct((ROWS, D), BF),
            jax.ShapeDtypeStruct((6, ROWS, 1024), BF),
        ),
        in_specs=[SM, SM, VM, VM, VM],
        out_specs=(VM, ANY, ANY, VM, VM, VM, VM, ANY),
        scratch_shapes=[
            pltpu.VMEM((PEERS * (EARLY + 1), 128), F32),
            pltpu.VMEM((D, 4 * D), BF),
            pltpu.VMEM((ROWS, D), BF),
            pltpu.VMEM((ROWS, 3 * D), BF),
            pltpu.VMEM((ROWS, ROWS), F32),
            pltpu.VMEM((6, ROWS, 1024), BF),
            pltpu.VMEM((D, ROWS), BF),
            pltpu.VMEM((ROWS, 128), F32),
            pltpu.SemaphoreType.DMA((3,)),
        ],
        compiler_params=params(),
        name="front",
    )(spot, lens, x, own, oth)


def add_blocks(sums, values):
    for at in range(values.shape[0] // 128):
        part = values[at * 128 : at * 128 + 128]
        if at < len(sums):
            sums[at] = sums[at] + part
        else:
            sums.append(part)


def back_pairs(pairs, qkv, up, weights, total, grads, kept):
    scale = jnp.asarray(0.125, BF)
    dk = [[] for _ in pairs]
    dv = [[] for _ in pairs]
    for block in range(4):
        count = (block + 1) * 128
        rows = slice(block * 128, count)
        gathered = total[:count, rows]
        for at, pair in enumerate(pairs):
            k = qkv[:count, lanes_of(pair, 1)]
            v = qkv[:count, lanes_of(pair, 2)]
            q = side_by_side(qkv[rows, lanes_of(pair, 0)] * scale)
            u = side_by_side(up[rows, pl.ds(pl.multiple_of(pair * 128, 128), 128)])
            low_soft = weights[pair, :count, block * 256 : block * 256 + 256]
            soft = low_soft.astype(F32)
            pulled = dot_nt(v, u)
            inner = jnp.sum(pulled * soft, axis=0, keepdims=True)
            dz = soft * (pulled - inner)
            gathered = gathered + (dz[:, 0:128] + dz[:, 128:256])
            add_blocks(dv[at], dot_nn(low_soft, u))
            if kept is not None and at == 0:
                kept[block, :count, :] = dz
            else:
                low = dz.astype(BF)
                add_blocks(dk[at], dot_nn(low, q))
                dq = (own_halves(dot_tn(k, low)) * 0.125).T
                grads[rows, lanes_of(pair, 0)] = dq.astype(BF)
        total[:count, rows] = gathered
    for at, pair in enumerate(pairs):
        grads[:, lanes_of(pair, 2)] = jnp.concatenate(dv[at], axis=0).astype(BF)
        if dk[at]:
            grads[:, lanes_of(pair, 1)] = jnp.concatenate(dk[at], axis=0).astype(BF)


def back_first(ends, qkv, total, grads, kept):
    scale = jnp.asarray(0.125, BF)
    row, column = iota((128, 256), 0), iota((128, 256), 1)
    after = one_hot((row > column) | (column >= 128))
    carry = jnp.zeros((ROWS, 128), F32)
    dk = []
    for block in (3, 2, 1, 0):
        count = (block + 1) * 128
        rows = slice(block * 128, count)
        k = qkv[:count, 128:256]
        q = side_by_side(qkv[rows, 0:128] * scale)
        _, chosen = block_masks(block, ends)
        high, low = split_low(total[:count, rows])
        sums = dot_nn(high, after) + dot_nn(low, after)
        picked = sums[:, 0:128] + carry[:count]
        carry = carry[:count] + sums[:, 128:256]
        slope = 1.0 / (1.0 + jnp.exp(-4.0 * dot_nt(k, q[0:128])))
        first = kept[block, :count, 0:128] - jnp.where(chosen, slope * picked, 0.0)
        low = jnp.concatenate([first, kept[block, :count, 128:256]], axis=1).astype(BF)
        add_blocks(dk, dot_nn(low, q))
        grads[rows, 0:128] = (own_halves(dot_tn(k, low)) * 0.125).T.astype(BF)
    grads[:, 128:256] = jnp.concatenate(dk, axis=0).astype(BF)


def put_rows(rows_s, piece, start):
    for row in range(OWN):
        rows_s[pl.ds(start + row, PEERS, stride=STEP), :] = piece[
            row * PEERS : row * PEERS + PEERS
        ]


def middle_kernel(
    spot_ref, lens_ref, cot_ref, middle_ref, dh_ref, ln_ref, w_hbm,
    dx_ref, low_ref, up_ref, vec_ref, w, sem,
):
    spot = tuple(spot_ref[0, at] for at in range(4))
    load = pltpu.make_async_copy(w_hbm.at[:, 3 * D : 4 * D], w, sem)
    load.start()
    ends = group_ends(lens_ref)
    vec_ref[...] = jnp.zeros_like(vec_ref)
    gain = ln_ref[2:3, :]

    @pl.loop(0, 4)
    def _(block):
        rows = pl.ds(pl.multiple_of(block * 128, 128), 128)
        unit, inverse = norm_stats(middle_ref[rows, :])
        gradient = dh_ref[rows, :]
        vec_ref[2:3, :] = vec_ref[2:3, :] + jnp.sum(gradient * unit, axis=0, keepdims=True)
        vec_ref[3:4, :] = vec_ref[3:4, :] + jnp.sum(gradient, axis=0, keepdims=True)
        live = (iota((128, 1), 0) + block * 128) < ends[3]
        dy = jnp.where(live, cot_ref[rows, :].astype(F32), 0.0)
        moved = dy + norm_pull(gradient, unit, inverse, gain)
        dx_ref[rows, :] = moved
        low_ref[rows, :] = moved.astype(BF)

    load.wait()
    placed = dot_nt(low_ref[...], w[...]).astype(BF)
    up_ref[...] = dot_nt(placed, place_matrix(spot)).astype(BF)


def middle_back(spot, lens, cot, middle, dh, norms, weights):
    low = jax.ShapeDtypeStruct((ROWS, D), BF)
    return pl.pallas_call(
        middle_kernel,
        out_shape=(
            jax.ShapeDtypeStruct((ROWS, D), F32),
            low,
            low,
            jax.ShapeDtypeStruct((8, D), F32),
        ),
        in_specs=[SM, SM] + [VM] * 4 + [ANY],
        out_specs=(VM,) * 4,
        scratch_shapes=[pltpu.VMEM((D, D), BF), pltpu.SemaphoreType.DMA],
        compiler_params=params(),
        name="middle_back",
    )(spot, lens, cot, middle, dh, norms, weights)


def back_kernel(
    spot_ref, lens_ref, vec_ref, up,
    qkv_hbm, soft_hbm, w_hbm, ht_hbm, x_hbm, low_hbm, mixed_hbm,
    oth_ref, own_ref, dh_one_ref,
    qkv, soft, w, ht, x_ref, low, mixed,
    total, kept, grads, dh_s, vec_s, rows_s, slab_s, sems, out_sems,
):
    spot = tuple(spot_ref[0, at] for at in range(4))
    core = spot[0]
    ends = group_ends(lens_ref)
    loads = [
        pltpu.make_async_copy(source, target, sems.at[number])
        for number, (source, target) in enumerate(
            (
                (qkv_hbm, qkv),
                (w_hbm.at[:, 0 : 3 * D], w),
                (ht_hbm, ht),
                (x_hbm, x_ref),
                (low_hbm, low),
                (mixed_hbm, mixed),
            )
        )
    ]

    def load_soft(pair):
        return pltpu.make_async_copy(soft_hbm.at[pair], soft.at[pair], sems.at[6 + pair])

    loads[0].start()
    for pair in (2, 3, 4, 5, 0, 1):
        load_soft(pair).start()
    for load in loads[1:]:
        load.start()
    total[...] = jnp.zeros_like(total)
    vec_s[...] = vec_ref[...]
    loads[0].wait()

    @pl.loop(0, 2)
    def _(turn):
        load_soft(2 * turn + 2).wait()
        load_soft(2 * turn + 3).wait()
        back_pairs((2 * turn + 2, 2 * turn + 3), qkv, up, soft, total, grads, None)

    load_soft(0).wait()
    load_soft(1).wait()
    back_pairs((0, 1), qkv, up, soft, total, grads, kept)
    back_first(ends, qkv, total, grads, kept)
    for load in loads[1:]:
        load.wait()
    placed = dot_nt(grads[...], w[...]).astype(BF)
    dh_s[...] = dot_nt(placed, place_matrix(spot))

    @pl.loop(0, 4)
    def _(block):
        rows = pl.ds(pl.multiple_of(block * 128, 128), 128)
        unit, _ = norm_stats(x_ref[rows, :].astype(F32))
        gradient = dh_s[rows, :]
        vec_s[0:1, :] = vec_s[0:1, :] + jnp.sum(gradient * unit, axis=0, keepdims=True)
        vec_s[1:2, :] = vec_s[1:2, :] + jnp.sum(gradient, axis=0, keepdims=True)

    stores = [pltpu.make_async_copy(dh_s, dh_one_ref, out_sems.at[2])]
    stores[0].start()
    vectors = [vec_s[which : which + 1, :] for which in range(4)]
    outer = dot_tn(mixed[...], low[...])
    for half, target in ((1, oth_ref), (0, own_ref)):
        side = core if half == 0 else 1 - core
        slots = slice(half * HALF, half * HALF + HALF)
        for part in range(4):
            if part < 3:
                piece = dot_nn(ht[slots, :], grads[:, part * D : part * D + D])
            else:
                piece = outer[slots]
            for block in range(BLOCKS):
                start = (part * BLOCKS + block) * OWN
                put_rows(rows_s, piece[:, block * 128 : block * 128 + 128], start)
        rows_s[pl.ds(GATHERED, PEERS, stride=STEP), :] = pack_vectors(vectors, side, spot)
        for spare in range(GATHERED + 1, TAIL):
            rows_s[pl.ds(spare, PEERS, stride=STEP), :] = jnp.zeros((PEERS, 128), F32)

        @pl.loop(0, 8)
        def _(block):
            for peer in range(8):
                group = block * 8 + peer
                first = (spot[3] + side * (spot[1] - spot[3]) - (group >> 4)) & 3
                second = (spot[1] + side * (spot[3] - spot[1]) - group) & 3
                to = first * 16 + second * 4 + ((spot[2] - (group >> 2)) & 3)
                slab_s[half, to] = rows_s[pl.ds(group * STEP, TAIL), :].astype(BF)

        store = pltpu.make_async_copy(slab_s.at[half], target, out_sems.at[half])
        store.start()
        stores.append(store)
    for store in stores:
        store.wait()


def back(spot, lens, vec, up, qkv, soft, weights, ht, x, low, mixed):
    slab = jax.ShapeDtypeStruct((PEERS, TAIL, 128), BF)
    return pl.pallas_call(
        back_kernel,
        out_shape=(slab, slab, jax.ShapeDtypeStruct((ROWS, D), F32)),
        in_specs=[SM, SM, VM, VM] + [ANY] * 7,
        out_specs=(ANY,) * 3,
        scratch_shapes=[
            pltpu.VMEM((ROWS, 3 * D), BF),
            pltpu.VMEM((6, ROWS, 1024), BF),
            pltpu.VMEM((D, 3 * D), BF),
            pltpu.VMEM((D, ROWS), BF),
            pltpu.VMEM((ROWS, D), BF),
            pltpu.VMEM((ROWS, D), BF),
            pltpu.VMEM((ROWS, D), BF),
            pltpu.VMEM((ROWS, ROWS), F32),
            pltpu.VMEM((4, ROWS, 256), F32),
            pltpu.VMEM((ROWS, 3 * D), BF),
            pltpu.VMEM((ROWS, D), F32),
            pltpu.VMEM((8, D), F32),
            pltpu.VMEM((PEERS * STEP, 128), F32),
            pltpu.VMEM((2, PEERS, TAIL, 128), BF),
            pltpu.SemaphoreType.DMA((12,)),
            pltpu.SemaphoreType.DMA((3,)),
        ],
        compiler_params=params(),
        name="back",
    )(spot, lens, vec, up, qkv, soft, weights, ht, x, low, mixed)


def feed_kernel(
    spot_ref, lens_ref, middle_ref, h_ref, cot_ref, late_ref, y_ref, own_ref, oth_ref, dh_ref,
    up_s, down_s, mid_in, mid_s, gup_s, gdown_s, dy_s, acc_s, sems, out_sems,
):
    def load_up(chunk):
        devices = pl.ds(chunk * 32, 32)
        return pltpu.make_async_copy(late_ref.at[devices, 0:16, :], up_s.at[chunk], sems.at[chunk])

    def load_down(chunk):
        devices = pl.ds(chunk * 32, 32)
        return pltpu.make_async_copy(
            late_ref.at[devices, 16:32, :], down_s.at[chunk], sems.at[4 + chunk]
        )

    def load_mid(half):
        devices = pl.ds(half * 64, 64)
        return pltpu.make_async_copy(
            late_ref.at[devices, 32:48, :], mid_in.at[half], sems.at[8 + half]
        )

    def both_cores(source, y, rows, sem, first, second):
        return [
            pltpu.make_async_copy(source.at[0], first.at[y, :, :, rows, :], sem),
            pltpu.make_async_copy(source.at[1], second.at[:, y, :, rows, :], sem),
        ]

    def big_stores(chunk, first, second):
        copies = []
        for block in range(BLOCKS):
            lanes = slice(block * 128, block * 128 + 128)
            for grads, offset in ((gup_s, 0), (gdown_s, 16)):
                rows = slice(block * 48 + offset, block * 48 + offset + 16)
                source = grads.at[chunk, :, :, :, :, lanes]
                copies += both_cores(source, chunk, rows, out_sems.at[chunk], first, second)
        return copies

    def mid_stores(half, first, second):
        copies = []
        for block in range(BLOCKS):
            lanes = slice(block * 128, block * 128 + 128)
            rows = slice(block * 48 + 32, block * 48 + 48)
            for y in range(2):
                source = mid_s.at[half, y, :, :, :, :, lanes]
                copies += both_cores(
                    source, half * 2 + y, rows, out_sems.at[4 + half], first, second
                )
        return copies

    def send(stores, number):
        @pl.when(spot_ref[0, 0] == 0)
        def _():
            for copy in stores(number, own_ref, oth_ref):
                copy.start()

        @pl.when(spot_ref[0, 0] == 1)
        def _():
            for copy in stores(number, oth_ref, own_ref):
                copy.start()

    for chunk in range(4):
        load_up(chunk).start()
        load_down(chunk).start()
    for half in range(2):
        load_mid(half).start()
    ends = group_ends(lens_ref)

    @pl.loop(0, 4)
    def _(block):
        rows = pl.ds(pl.multiple_of(block * 128, 128), 128)
        acc_s[rows, :] = middle_ref[rows, :]
        live = (iota((128, 1), 0) + block * 128) < ends[3]
        dy_s[rows, :] = jnp.where(live, cot_ref[rows, :].astype(F32), 0.0).astype(BF)
        dh_ref[rows, :] = jnp.zeros((128, D), F32)

    def both_ways(up, down):
        value = dot_nt(h_ref[...], up)
        square = value * value
        bend = jnp.tanh(TANH_SCALE * (value + TANH_CUBE * (value * square)))
        act = (0.5 * value * (1.0 + bend)).astype(BF)
        slope = 0.5 * (1.0 + bend) + (0.5 * TANH_SCALE) * value * (1.0 - bend * bend) * (
            1.0 + 3.0 * TANH_CUBE * square
        )
        pulled = (dot_nt(dy_s[...], down) * slope).astype(BF)
        acc_s[...] = acc_s[...] + dot_nn(act, down)
        dh_ref[...] = dh_ref[...] + dot_nn(pulled, up)
        return dot_tn(pulled, h_ref[...]), dot_tn(act, dy_s[...])

    @pl.loop(0, 4)
    def _(chunk):
        load_up(chunk).wait()
        load_down(chunk).wait()
        up_grad, down_grad = both_ways(
            up_s[chunk].reshape(ROWS, D), down_s[chunk].reshape(ROWS, D)
        )
        gup_s[chunk] = up_grad.astype(BF).reshape(2, 4, 4, 16, D)
        gdown_s[chunk] = down_grad.astype(BF).reshape(2, 4, 4, 16, D)
        send(big_stores, chunk)

    @pl.loop(0, 2)
    def _(half):
        load_mid(half).wait()
        mid = mid_in[half].astype(F32)
        up_grad, down_grad = both_ways(
            mid[:, 0:8, :].reshape(ROWS, D).astype(BF), mid[:, 8:16, :].reshape(ROWS, D).astype(BF)
        )
        joined = jnp.concatenate(
            [up_grad.reshape(PEERS, 8, D), down_grad.reshape(PEERS, 8, D)], axis=1
        )
        mid_s[half] = joined.astype(BF).reshape(2, 2, 4, 4, 16, D)
        send(mid_stores, half)

    y_ref[...] = acc_s[...].astype(BF)
    for chunk in range(4):
        for copy in big_stores(chunk, own_ref, oth_ref):
            copy.wait()
    for half in range(2):
        for copy in mid_stores(half, own_ref, oth_ref):
            copy.wait()


def feed(spot, lens, middle, h, cot, late):
    slab = jax.ShapeDtypeStruct((4, 4, 4, WHOLE, 128), BF)
    return pl.pallas_call(
        feed_kernel,
        out_shape=(
            jax.ShapeDtypeStruct((ROWS, D), BF),
            slab,
            slab,
            jax.ShapeDtypeStruct((ROWS, D), F32),
        ),
        in_specs=[SM, SM, VM, VM, VM, ANY],
        out_specs=(VM, ANY, ANY, VM),
        scratch_shapes=[
            pltpu.VMEM((4, 32, 16, D), BF),
            pltpu.VMEM((4, 32, 16, D), BF),
            pltpu.VMEM((2, PEERS, 16, D), BF),
            pltpu.VMEM((2, 2, 2, 4, 4, 16, D), BF),
            pltpu.VMEM((4, 2, 4, 4, 16, D), BF),
            pltpu.VMEM((4, 2, 4, 4, 16, D), BF),
            pltpu.VMEM((ROWS, D), BF),
            pltpu.VMEM((ROWS, D), F32),
            pltpu.SemaphoreType.DMA((10,)),
            pltpu.SemaphoreType.DMA((6,)),
        ],
        compiler_params=params(),
        name="feed",
    )(spot, lens, middle, h, cot, late)


def norm_back_kernel(x_ref, dx_ref, dh_ref, ln_ref, dtok_ref):
    @pl.loop(0, 4)
    def _(block):
        rows = pl.ds(pl.multiple_of(block * 128, 128), 128)
        unit, inverse = norm_stats(x_ref[rows, :].astype(F32))
        moved = dx_ref[rows, :] + norm_pull(dh_ref[rows, :], unit, inverse, ln_ref[0:1, :])
        dtok_ref[rows, :] = moved.astype(BF)


def norm_back(x, dx, dh, ln):
    return pl.pallas_call(
        norm_back_kernel,
        out_shape=jax.ShapeDtypeStruct((ROWS, D), BF),
        in_specs=[VM] * 4,
        out_specs=VM,
        compiler_params=params(),
        name="norm_back",
    )(x, dx, dh, ln)


def finish_kernel(slabs_ref, qkv_ref, out_ref, g1_ref, b1_ref, g2_ref, b2_ref, sum_s):
    sum_s[...] = jnp.sum(slabs_ref[...].astype(F32), axis=0)
    for pair in range(BLOCKS):
        for part in range(3):
            start = (pair * 3 + part) * OWN
            at = part * D + pair * 128
            qkv_ref[:, at : at + 128] = sum_s[start : start + OWN, :]
        start = OUTER + pair * OWN
        out_ref[:, pair * 128 : pair * 128 + 128] = sum_s[start : start + OWN, :]
    for which, target in enumerate((g1_ref, b1_ref, g2_ref, b2_ref)):
        target[...] = sum_s[GATHERED : GATHERED + 1, which * OWN : which * OWN + OWN]


def finish(slabs):
    vector = jax.ShapeDtypeStruct((1, OWN), F32)
    return pl.pallas_call(
        finish_kernel,
        out_shape=(
            jax.ShapeDtypeStruct((OWN, 3 * D), F32),
            jax.ShapeDtypeStruct((OWN, D), F32),
            vector, vector, vector, vector,
        ),
        in_specs=[VM],
        out_specs=(VM,) * 6,
        scratch_shapes=[pltpu.VMEM((TAIL, 128), F32)],
        compiler_params=params(16),
        name="finish",
    )(slabs)


def unpack_kernel(late_ref, up_ref, down_ref, sum_s):
    sum_s[...] = jnp.sum(late_ref[...].astype(F32), axis=0)
    for block in range(BLOCKS):
        lanes = slice(block * 128, block * 128 + 128)
        row = block * 48
        up_ref[0:16, lanes] = sum_s[row : row + 16, :]
        down_ref[0:16, lanes] = sum_s[row + 16 : row + 32, :]
        up_ref[16:24, lanes] = sum_s[row + 32 : row + 40, :]
        down_ref[16:24, lanes] = sum_s[row + 40 : row + 48, :]


def unpack(late):
    shard = jax.ShapeDtypeStruct((24, D), F32)
    return pl.pallas_call(
        unpack_kernel,
        out_shape=(shard, shard),
        in_specs=[VM],
        out_specs=(VM, VM),
        scratch_shapes=[pltpu.VMEM((WHOLE, 128), F32)],
        compiler_params=params(16),
        name="unpack",
    )(late)


def add_pair(own, other):
    received = lax.ppermute(other, AXES, core_pairs())
    return (own.astype(F32) + received.astype(F32)).astype(BF)


def add_kernel(left_ref, right_ref, sum_ref, left, right, total, sems):
    def copies(source, target, column):
        return [
            pltpu.make_async_copy(
                source.at[pl.ds(part * 8, 8)], target.at[pl.ds(part * 8, 8)], sems.at[part, column]
            )
            for part in range(8)
        ]

    lefts, rights = copies(left_ref, left, 0), copies(right_ref, right, 1)
    stores = copies(total, sum_ref, 2)
    for load in itertools.chain(*zip(lefts, rights)):
        load.start()
    for part in range(8):
        lefts[part].wait()
        rights[part].wait()
        at = slice(part * 8, part * 8 + 8)
        total[at] = (left[at].astype(F32) + right[at].astype(F32)).astype(BF)
        stores[part].start()
    for store in stores:
        store.wait()


def add_large_pair(own, other):
    received = lax.ppermute(other, AXES, core_pairs())
    return pl.pallas_call(
        add_kernel,
        out_shape=jax.ShapeDtypeStruct(own.shape, BF),
        in_specs=[ANY, ANY],
        out_specs=ANY,
        scratch_shapes=[pltpu.VMEM(own.shape, BF)] * 3 + [pltpu.SemaphoreType.DMA((8, 3))],
        compiler_params=params(),
        name="add_large_pair",
    )(own, received)


def scatter(slabs, rows):
    return lax.psum_scatter(
        slabs.reshape(PEERS * rows, 128),
        AXES,
        scatter_dimension=0,
        axis_index_groups=mixed_groups("y", "z"),
        tiled=True,
    )


def exchange(slabs, rows):
    return lax.all_to_all(
        slabs.reshape(16, rows, 128),
        AXES,
        0,
        0,
        axis_index_groups=mixed_groups("zx", "yx"),
        tiled=True,
    )


def shift(values, dims, ahead):
    pairs = []
    for x, y, z, c in itertools.product(range(4), range(4), range(4), range(2)):
        to = dict(x=x, y=y, z=z)
        to[dims[c]] = (to[dims[c]] + ahead) % 4
        pairs.append((device_number(x, y, z, c), device_number(to["x"], to["y"], to["z"], c)))
    return lax.ppermute(values, AXES, pairs)


def ring(own, dims):
    return jnp.concatenate([own] + [shift(own, dims, ahead) for ahead in (1, 2, 3)], axis=0)


def wide_ring(own, dims):
    half = own.shape[0] // 2
    near, last = shift(own, dims, 1), shift(own, dims, -1)
    far = [shift(near[:half], dims, 1), shift(last[half:], dims, -1)]
    return jnp.concatenate([own, near, *far, last], axis=0)


def copies_of_peers(own):
    return wide_ring(ring(ring(own, "zy"), "xx"), "yz").reshape(PEERS, *own.shape)


def on_device(
    tokens,
    seq_lengths,
    ln1_gain,
    ln1_bias,
    qkv_weight,
    out_weight,
    ln2_gain,
    ln2_bias,
    up_weight,
    down_weight,
    cotangent,
):
    wide, narrow = lax.axis_index("wide"), lax.axis_index("narrow")
    spot = jnp.stack([wide & 1, narrow & 3, (narrow >> 2) * 2 + (wide >> 3), (wide >> 1) & 3])
    spot = spot.astype(I32).reshape(1, 4)
    early, late = pack(
        ln1_gain, ln1_bias, qkv_weight, out_weight, ln2_gain, ln2_bias, up_weight.T, down_weight
    )
    late = lax.all_gather(late, AXES, axis_index_groups=peer_groups("yczx"))
    early_own = copies_of_peers(early)
    early_oth = lax.ppermute(early_own, AXES, core_pairs())
    ht, qkv, weights, norms, mixed, middle, h_two, soft = front(
        spot, seq_lengths, tokens, early_own, early_oth
    )
    output, own, oth, dh_two = feed(spot, seq_lengths, middle, h_two, cotangent, late)
    late_grad = add_large_pair(own.reshape(PEERS, WHOLE, 128), oth.reshape(PEERS, WHOLE, 128))
    dx, low, upstream, vectors = middle_back(
        spot, seq_lengths, cotangent, middle, dh_two, norms, weights
    )
    late_grad, upstream = lax.optimization_barrier((late_grad, upstream))
    late_grad = scatter(late_grad, WHOLE)
    oth, own, dh_one = back(
        spot, seq_lengths, vectors, upstream, qkv, soft, weights, ht, tokens, low, mixed
    )
    tail = scatter(add_pair(own, oth), TAIL)
    late_grad = exchange(late_grad, WHOLE)
    dtokens = norm_back(tokens, dx, dh_one, norms)
    tail, late_grad = lax.optimization_barrier((tail, late_grad))
    tail = exchange(tail, TAIL)
    up_grad, down_grad = unpack(late_grad)
    qkv_grad, out_grad, g1_grad, b1_grad, g2_grad, b2_grad = finish(tail)
    return (
        output,
        dtokens,
        g1_grad.reshape(OWN),
        b1_grad.reshape(OWN),
        qkv_grad,
        out_grad,
        g2_grad.reshape(OWN),
        b2_grad.reshape(OWN),
        up_grad.T,
        down_grad,
    )


def solution(mesh):
    rows = P(AXES, None)
    flat = P(AXES)
    columns = P(None, AXES)
    return jax.shard_map(
        on_device,
        mesh=mesh,
        in_specs=(rows, rows, flat, flat, rows, rows, flat, flat, columns, rows, rows),
        out_specs=(rows, rows, flat, flat, rows, rows, flat, flat, columns, rows),
        check_vma=False,
    )
```

```python
import functools
import itertools

import jax
import jax.numpy as jnp
from jax import lax
from jax.experimental import pallas as pl
from jax.experimental.pallas import tpu as pltpu
from jax.sharding import PartitionSpec as P

BF = jnp.bfloat16
F32 = jnp.float32
I32 = jnp.int32
AXES = ("wide", "narrow")
D = 768
ROWS = 512
FF = 3072
OWN = 6
PEERS = 64
HALF = PEERS * OWN
BLOCKS = 6
OUTER = 3 * OWN * BLOCKS
GATHERED = OUTER + OWN * BLOCKS
EARLY = 152
LATE = 48
WHOLE = 288
TAIL = 152
STEP = TAIL + 1
EPS = 1e-05
FAR = 1e30
TANH_SCALE = 0.7978845608028654
TANH_CUBE = 0.044715
MIB = 1 << 20


def device_number(x, y, z, core):
    return ((x & 1) * 8 + y * 2 + core) * 8 + (x >> 1) * 4 + z


def peer_groups(dims):
    sizes = dict(x=4, y=4, z=4, c=2)
    rest = [name for name in "xyzc" if name not in dims]
    groups = []
    for fixed in itertools.product(*[range(sizes[name]) for name in rest]):
        members = []
        for moving in itertools.product(*[range(sizes[name]) for name in dims]):
            at = dict(zip(rest, fixed))
            at.update(zip(dims, moving))
            members.append(device_number(at["x"], at["y"], at["z"], at["c"]))
        groups.append(members)
    return groups


def mixed_groups(first, second):
    halves = [peer_groups(dims) for dims in (first, second)]
    return [
        group
        for core, groups in enumerate(halves)
        for group in groups
        if (group[0] >> 3) & 1 == core
    ]


def core_pairs():
    return [
        (device_number(x, y, z, c), device_number(x, y, z, 1 - c))
        for x, y, z, c in itertools.product(range(4), range(4), range(4), range(2))
    ]


def dot_nn(left, right):
    return lax.dot_general(left, right, (((1,), (0,)), ((), ())), preferred_element_type=F32)


def dot_nt(left, right):
    return lax.dot_general(left, right, (((1,), (1,)), ((), ())), preferred_element_type=F32)


def dot_tn(left, right):
    return lax.dot_general(left, right, (((0,), (0,)), ((), ())), preferred_element_type=F32)


def iota(shape, dim):
    return lax.broadcasted_iota(I32, shape, dim)


def one_hot(mask):
    return jnp.where(mask, 1.0, 0.0).astype(BF)


def split_low(values):
    high = values.astype(BF)
    return high, (values - high.astype(F32)).astype(BF)


def owner(group, core, spot):
    far, near = group >> 4, group & 3
    y = (spot[3] - (far + core * (near - far))) & 3
    x = (spot[2] - (group >> 2)) & 3
    z = (spot[1] - (near + core * (far - near))) & 3
    return ((x & 1) << 6) + (y << 4) + (core << 3) + ((x >> 1) << 2) + z


def sixth(number):
    return (number * 43691) >> 18


def place_matrix(spot):
    slot = iota((1, D), 1)
    other = (slot >= HALF).astype(I32)
    inner = slot - HALF * other
    side = spot[0] + other - 2 * spot[0] * other
    feature = owner(inner & (PEERS - 1), side, spot) * OWN + (inner >> 6)
    return one_hot(iota((D, D), 0) == feature)


def place_transposed(spot):
    slot = iota((D, 1), 0)
    other = (slot >= HALF).astype(I32)
    inner = slot - HALF * other
    side = spot[0] + other - 2 * spot[0] * other
    feature = owner(inner & (PEERS - 1), side, spot) * OWN + (inner >> 6)
    return one_hot(iota((D, D), 1) == feature)


def vector_lanes(which):
    feature = iota((1, D), 1)
    lane = which * OWN + feature - OWN * sixth(feature)
    return one_hot(iota((128, D), 0) == lane)


def owned_features(core, spot):
    return owner(iota((PEERS, 1), 0), core, spot) == sixth(iota((1, D), 1))


def unpack_vector(packed, mine, which):
    spread = dot_nn(packed.astype(BF), vector_lanes(which))
    return jnp.sum(jnp.where(mine, spread, 0.0), axis=0, keepdims=True)


def pack_vectors(vectors, core, spot):
    mine = owned_features(core, spot)
    total = jnp.zeros((PEERS, 128), F32)
    for which, vector in enumerate(vectors):
        spread = jnp.where(mine, vector, 0.0).astype(BF)
        total = total + dot_nt(spread, vector_lanes(which))
    return total


def norm_stats(values):
    center = values - jnp.mean(values, axis=-1, keepdims=True)
    inverse = lax.rsqrt(jnp.mean(center * center, axis=-1, keepdims=True) + EPS)
    return center * inverse, inverse


def norm_pull(gradient, unit, inverse, gain):
    scaled = gradient * gain
    return inverse * (
        scaled
        - jnp.mean(scaled, axis=-1, keepdims=True)
        - unit * jnp.mean(scaled * unit, axis=-1, keepdims=True)
    )


def group_ends(lens_ref):
    ends = []
    total = 0
    for slot in range(4):
        total = total + lens_ref[0, slot]
        ends.append(total)
    return ends


def segments(positions, ends):
    return sum((positions >= end).astype(I32) for end in ends)


VM = pl.BlockSpec(memory_space=pltpu.VMEM)
SM = pl.BlockSpec(memory_space=pltpu.SMEM)
ANY = pl.BlockSpec(memory_space=pl.ANY)


def params(limit=60):
    return pltpu.CompilerParams(vmem_limit_bytes=limit * MIB)


def pack_kernel(
    g1_ref, b1_ref, qkv_ref, out_ref, g2_ref, b2_ref, up_ref, down_ref, early_ref, late_ref, es
):
    es[...] = jnp.zeros_like(es)
    qkv = qkv_ref[...].astype(F32)
    out = out_ref[...].astype(F32)
    for pair in range(BLOCKS):
        for part in range(3):
            start = (pair * 3 + part) * OWN
            es[start : start + OWN, :] = qkv[:, part * D + pair * 128 : part * D + pair * 128 + 128]
        start = OUTER + pair * OWN
        es[start : start + OWN, :] = out[:, pair * 128 : pair * 128 + 128]
    for which, ref in enumerate((g1_ref, b1_ref, g2_ref, b2_ref)):
        es[GATHERED : GATHERED + 1, which * OWN : which * OWN + OWN] = ref[...].astype(F32)
    early_ref[...] = es[...].astype(BF)
    up = up_ref[...].astype(F32)
    down = down_ref[...].astype(F32)
    late_ref[...] = jnp.concatenate([up[0:16], down[0:16], up[16:24], down[16:24]], axis=0).astype(BF)


def pack(g1, b1, qkv, out, g2, b2, up, down):
    return pl.pallas_call(
        pack_kernel,
        out_shape=(
            jax.ShapeDtypeStruct((EARLY, 128), BF),
            jax.ShapeDtypeStruct((LATE, D), BF),
        ),
        in_specs=[VM] * 8,
        out_specs=(VM, VM),
        scratch_shapes=[pltpu.VMEM((EARLY, 128), F32)],
        compiler_params=params(),
        name="pack",
    )(g1[None], b1[None], qkv, out, g2[None], b2[None], up, down)


def softplus4(logits):
    sharp = 4.0 * logits
    return 0.25 * (jnp.maximum(sharp, 0.0) + jnp.log(1.0 + jnp.exp(-jnp.abs(sharp))))


def block_masks(block, ends):
    count = (block + 1) * 128
    query = iota((1, 128), 1) + block * 128
    key = iota((count, 1), 0)
    same = segments(key, ends) == segments(query, ends)
    first = key == 0
    for end in ends:
        first = first | (key == end)
    allowed = same & (key <= query)
    chosen = same & (key < query) & jnp.logical_not(first)
    return allowed, chosen


def twice(values):
    return jnp.concatenate([values, values], axis=1)


def side_by_side(values):
    left = iota((1, 128), 1) < 64
    zero = jnp.zeros((), BF)
    return jnp.concatenate([jnp.where(left, values, zero), jnp.where(left, zero, values)], axis=0)


def own_halves(values):
    return jnp.concatenate([values[0:64, 0:128], values[64:128, 128:256]], axis=0)


def lanes_of(pair, part):
    return pl.ds(pl.multiple_of(pair * 384 + part * 128, 128), 128)


def front_kernel(
    spot_ref, lens_ref, x_ref, own_ref, oth_ref,
    ht_ref, qkv_ref, w_ref, ln_ref, mixed_ref, middle_ref, h_ref, soft_ref,
    rows_s, w, h_s, qkv, pen, soft_s, attn_s, carry, sems,
):
    spot = tuple(spot_ref[0, at] for at in range(4))
    core = spot[0]
    vectors = [jnp.zeros((1, D), F32) for _ in range(4)]
    for half, source in enumerate((own_ref, oth_ref)):
        side = core if half == 0 else 1 - core

        @pl.loop(0, 8)
        def _(block):
            for peer in range(8):
                start = (block * 8 + peer) * (EARLY + 1)
                rows_s[pl.ds(start, EARLY), :] = source[block * 8 + peer].astype(F32)

        for block in range(4 * BLOCKS):
            for row in range(OWN):
                to = half * HALF + row * PEERS
                w[to : to + PEERS, block * 128 : block * 128 + 128] = rows_s[
                    pl.ds(block * OWN + row, PEERS, stride=EARLY + 1), :
                ].astype(BF)
        packed = rows_s[pl.ds(GATHERED, PEERS, stride=EARLY + 1), :]
        mine = owned_features(side, spot)
        vectors = [
            vector + unpack_vector(packed, mine, which) for which, vector in enumerate(vectors)
        ]
    store_w = pltpu.make_async_copy(w, w_ref, sems.at[0])
    store_w.start()
    for which, vector in enumerate(vectors):
        ln_ref[which : which + 1, :] = vector
    ln_ref[4:8, :] = jnp.zeros((4, D), F32)

    @pl.loop(0, 4)
    def _(block):
        rows = pl.ds(pl.multiple_of(block * 128, 128), 128)
        unit, _ = norm_stats(x_ref[rows, :].astype(F32))
        h_s[rows, :] = (unit * ln_ref[0:1, :] + ln_ref[1:2, :]).astype(BF)

    place = place_matrix(spot)
    placed = dot_nn(h_s[...], place).astype(BF)
    for part in range(3):
        columns = slice(part * D, part * D + D)
        qkv[:, columns] = dot_nn(placed, w[:, columns]).astype(BF)
    store_qkv = pltpu.make_async_copy(qkv, qkv_ref, sems.at[1])
    store_qkv.start()

    ends = group_ends(lens_ref)
    scale = jnp.asarray(0.125, BF)
    row, column = iota((128, 256), 0), iota((128, 256), 1)
    before = one_hot((row < column) | (column >= 128))
    carry[...] = jnp.zeros_like(carry)
    k0 = qkv[:, 128:256]
    for block in range(4):
        count = (block + 1) * 128
        rows = slice(block * 128, count)
        q0 = side_by_side(qkv[rows, 0:128] * scale)[0:128]
        allowed, chosen = block_masks(block, ends)
        picked = jnp.where(chosen, softplus4(dot_nt(k0[:count], q0)), 0.0)
        high, low = split_low(picked)
        sums = dot_nn(high, before) + dot_nn(low, before)
        pen[:count, rows] = jnp.where(allowed, sums[:, 0:128] + carry[:count, :], FAR)
        carry[:count, :] = carry[:count, :] + sums[:, 128:256]

    def store_soft(pair):
        return pltpu.make_async_copy(soft_s.at[pair], soft_ref.at[pair], sems.at[2])

    @pl.loop(0, 3)
    def _(turn):
        for block in range(4):
            count = (block + 1) * 128
            rows = slice(block * 128, count)
            penalty = twice(pen[:count, rows])
            for pair in (2 * turn, 2 * turn + 1):
                k = qkv[:count, lanes_of(pair, 1)]
                v = qkv[:count, lanes_of(pair, 2)]
                q = side_by_side(qkv[rows, lanes_of(pair, 0)] * scale)
                shifted = dot_nt(k, q) - penalty
                top = jnp.max(shifted, axis=0, keepdims=True)
                exponent = jnp.exp(shifted - top)
                total = jnp.sum(exponent, axis=0, keepdims=True)
                soft = (exponent * (1.0 / total)).astype(BF)
                soft_s[pair, :count, block * 256 : block * 256 + 256] = soft
                lanes = pl.ds(pl.multiple_of(pair * 128, 128), 128)
                attn_s[lanes, rows] = own_halves(dot_tn(v, soft)).astype(BF)
        store_soft(2 * turn).start()
        store_soft(2 * turn + 1).start()

    mixed_ref[...] = dot_tn(attn_s[...], place).astype(BF)
    middle_ref[...] = dot_nn(mixed_ref[...], w[:, 3 * D : 4 * D])

    @pl.loop(0, 4)
    def _(block):
        rows = pl.ds(pl.multiple_of(block * 128, 128), 128)
        middle = x_ref[rows, :].astype(F32) + middle_ref[rows, :]
        middle_ref[rows, :] = middle
        unit, _ = norm_stats(middle)
        h_ref[rows, :] = (unit * ln_ref[2:3, :] + ln_ref[3:4, :]).astype(BF)

    ht_ref[...] = dot_nt(place_transposed(spot), h_s[...]).astype(BF)
    for store in (store_w, store_qkv, *(store_soft(pair) for pair in range(6))):
        store.wait()


def front(spot, lens, x, own, oth):
    return pl.pallas_call(
        front_kernel,
        out_shape=(
            jax.ShapeDtypeStruct((D, ROWS), BF),
            jax.ShapeDtypeStruct((ROWS, 3 * D), BF),
            jax.ShapeDtypeStruct((D, 4 * D), BF),
            jax.ShapeDtypeStruct((8, D), F32),
            jax.ShapeDtypeStruct((ROWS, D), BF),
            jax.ShapeDtypeStruct((ROWS, D), F32),
            jax.ShapeDtypeStruct((ROWS, D), BF),
            jax.ShapeDtypeStruct((6, ROWS, 1024), BF),
        ),
        in_specs=[SM, SM, VM, VM, VM],
        out_specs=(VM, ANY, ANY, VM, VM, VM, VM, ANY),
        scratch_shapes=[
            pltpu.VMEM((PEERS * (EARLY + 1), 128), F32),
            pltpu.VMEM((D, 4 * D), BF),
            pltpu.VMEM((ROWS, D), BF),
            pltpu.VMEM((ROWS, 3 * D), BF),
            pltpu.VMEM((ROWS, ROWS), F32),
            pltpu.VMEM((6, ROWS, 1024), BF),
            pltpu.VMEM((D, ROWS), BF),
            pltpu.VMEM((ROWS, 128), F32),
            pltpu.SemaphoreType.DMA((3,)),
        ],
        compiler_params=params(),
        name="front",
    )(spot, lens, x, own, oth)


def add_blocks(sums, values):
    for at in range(values.shape[0] // 128):
        part = values[at * 128 : at * 128 + 128]
        if at < len(sums):
            sums[at] = sums[at] + part
        else:
            sums.append(part)


def back_pairs(pairs, qkv, up, weights, total, grads, kept):
    scale = jnp.asarray(0.125, BF)
    dk = [[] for _ in pairs]
    dv = [[] for _ in pairs]
    for block in range(4):
        count = (block + 1) * 128
        rows = slice(block * 128, count)
        gathered = total[:count, rows]
        for at, pair in enumerate(pairs):
            k = qkv[:count, lanes_of(pair, 1)]
            v = qkv[:count, lanes_of(pair, 2)]
            q = side_by_side(qkv[rows, lanes_of(pair, 0)] * scale)
            u = side_by_side(up[rows, pl.ds(pl.multiple_of(pair * 128, 128), 128)])
            low_soft = weights[pair, :count, block * 256 : block * 256 + 256]
            soft = low_soft.astype(F32)
            pulled = dot_nt(v, u)
            inner = jnp.sum(pulled * soft, axis=0, keepdims=True)
            dz = soft * (pulled - inner)
            gathered = gathered + (dz[:, 0:128] + dz[:, 128:256])
            add_blocks(dv[at], dot_nn(low_soft, u))
            if kept is not None and at == 0:
                kept[block, :count, :] = dz
            else:
                low = dz.astype(BF)
                add_blocks(dk[at], dot_nn(low, q))
                dq = (own_halves(dot_tn(k, low)) * 0.125).T
                grads[rows, lanes_of(pair, 0)] = dq.astype(BF)
        total[:count, rows] = gathered
    for at, pair in enumerate(pairs):
        grads[:, lanes_of(pair, 2)] = jnp.concatenate(dv[at], axis=0).astype(BF)
        if dk[at]:
            grads[:, lanes_of(pair, 1)] = jnp.concatenate(dk[at], axis=0).astype(BF)


def back_first(ends, qkv, total, grads, kept):
    scale = jnp.asarray(0.125, BF)
    row, column = iota((128, 256), 0), iota((128, 256), 1)
    after = one_hot((row > column) | (column >= 128))
    carry = jnp.zeros((ROWS, 128), F32)
    dk = []
    for block in (3, 2, 1, 0):
        count = (block + 1) * 128
        rows = slice(block * 128, count)
        k = qkv[:count, 128:256]
        q = side_by_side(qkv[rows, 0:128] * scale)
        _, chosen = block_masks(block, ends)
        high, low = split_low(total[:count, rows])
        sums = dot_nn(high, after) + dot_nn(low, after)
        picked = sums[:, 0:128] + carry[:count]
        carry = carry[:count] + sums[:, 128:256]
        slope = 1.0 / (1.0 + jnp.exp(-4.0 * dot_nt(k, q[0:128])))
        first = kept[block, :count, 0:128] - jnp.where(chosen, slope * picked, 0.0)
        low = jnp.concatenate([first, kept[block, :count, 128:256]], axis=1).astype(BF)
        add_blocks(dk, dot_nn(low, q))
        grads[rows, 0:128] = (own_halves(dot_tn(k, low)) * 0.125).T.astype(BF)
    grads[:, 128:256] = jnp.concatenate(dk, axis=0).astype(BF)


def put_rows(rows_s, piece, start):
    for row in range(OWN):
        rows_s[pl.ds(start + row, PEERS, stride=STEP), :] = piece[
            row * PEERS : row * PEERS + PEERS
        ]


def middle_kernel(
    spot_ref, lens_ref, cot_ref, middle_ref, dh_ref, ln_ref, w_hbm,
    dx_ref, low_ref, up_ref, vec_ref, w, sem,
):
    spot = tuple(spot_ref[0, at] for at in range(4))
    load = pltpu.make_async_copy(w_hbm.at[:, 3 * D : 4 * D], w, sem)
    load.start()
    ends = group_ends(lens_ref)
    vec_ref[...] = jnp.zeros_like(vec_ref)
    gain = ln_ref[2:3, :]

    @pl.loop(0, 4)
    def _(block):
        rows = pl.ds(pl.multiple_of(block * 128, 128), 128)
        unit, inverse = norm_stats(middle_ref[rows, :])
        gradient = dh_ref[rows, :]
        vec_ref[2:3, :] = vec_ref[2:3, :] + jnp.sum(gradient * unit, axis=0, keepdims=True)
        vec_ref[3:4, :] = vec_ref[3:4, :] + jnp.sum(gradient, axis=0, keepdims=True)
        live = (iota((128, 1), 0) + block * 128) < ends[3]
        dy = jnp.where(live, cot_ref[rows, :].astype(F32), 0.0)
        moved = dy + norm_pull(gradient, unit, inverse, gain)
        dx_ref[rows, :] = moved
        low_ref[rows, :] = moved.astype(BF)

    load.wait()
    placed = dot_nt(low_ref[...], w[...]).astype(BF)
    up_ref[...] = dot_nt(placed, place_matrix(spot)).astype(BF)


def middle_back(spot, lens, cot, middle, dh, norms, weights):
    low = jax.ShapeDtypeStruct((ROWS, D), BF)
    return pl.pallas_call(
        middle_kernel,
        out_shape=(
            jax.ShapeDtypeStruct((ROWS, D), F32),
            low,
            low,
            jax.ShapeDtypeStruct((8, D), F32),
        ),
        in_specs=[SM, SM] + [VM] * 4 + [ANY],
        out_specs=(VM,) * 4,
        scratch_shapes=[pltpu.VMEM((D, D), BF), pltpu.SemaphoreType.DMA],
        compiler_params=params(),
        name="middle_back",
    )(spot, lens, cot, middle, dh, norms, weights)


def back_kernel(
    spot_ref, lens_ref, vec_ref, up,
    qkv_hbm, soft_hbm, w_hbm, ht_hbm, x_hbm, low_hbm, mixed_hbm,
    oth_ref, own_ref, dh_one_ref,
    qkv, soft, w, ht, x_ref, low, mixed,
    total, kept, grads, dh_s, vec_s, rows_s, slab_s, sems, out_sems,
):
    spot = tuple(spot_ref[0, at] for at in range(4))
    core = spot[0]
    ends = group_ends(lens_ref)
    loads = [
        pltpu.make_async_copy(source, target, sems.at[number])
        for number, (source, target) in enumerate(
            (
                (qkv_hbm, qkv),
                (w_hbm.at[:, 0 : 3 * D], w),
                (ht_hbm, ht),
                (x_hbm, x_ref),
                (low_hbm, low),
                (mixed_hbm, mixed),
            )
        )
    ]

    def load_soft(pair):
        return pltpu.make_async_copy(soft_hbm.at[pair], soft.at[pair], sems.at[6 + pair])

    loads[0].start()
    for pair in (2, 3, 4, 5, 0, 1):
        load_soft(pair).start()
    for load in loads[1:]:
        load.start()
    total[...] = jnp.zeros_like(total)
    vec_s[...] = vec_ref[...]
    loads[0].wait()

    @pl.loop(0, 2)
    def _(turn):
        load_soft(2 * turn + 2).wait()
        load_soft(2 * turn + 3).wait()
        back_pairs((2 * turn + 2, 2 * turn + 3), qkv, up, soft, total, grads, None)

    load_soft(0).wait()
    load_soft(1).wait()
    back_pairs((0, 1), qkv, up, soft, total, grads, kept)
    back_first(ends, qkv, total, grads, kept)
    for load in loads[1:]:
        load.wait()
    placed = dot_nt(grads[...], w[...]).astype(BF)
    dh_s[...] = dot_nt(placed, place_matrix(spot))

    @pl.loop(0, 4)
    def _(block):
        rows = pl.ds(pl.multiple_of(block * 128, 128), 128)
        unit, _ = norm_stats(x_ref[rows, :].astype(F32))
        gradient = dh_s[rows, :]
        vec_s[0:1, :] = vec_s[0:1, :] + jnp.sum(gradient * unit, axis=0, keepdims=True)
        vec_s[1:2, :] = vec_s[1:2, :] + jnp.sum(gradient, axis=0, keepdims=True)

    stores = [pltpu.make_async_copy(dh_s, dh_one_ref, out_sems.at[2])]
    stores[0].start()
    vectors = [vec_s[which : which + 1, :] for which in range(4)]
    outer = dot_tn(mixed[...], low[...])
    for half, target in ((1, oth_ref), (0, own_ref)):
        side = core if half == 0 else 1 - core
        slots = slice(half * HALF, half * HALF + HALF)
        for part in range(4):
            if part < 3:
                piece = dot_nn(ht[slots, :], grads[:, part * D : part * D + D])
            else:
                piece = outer[slots]
            for block in range(BLOCKS):
                start = (part * BLOCKS + block) * OWN
                put_rows(rows_s, piece[:, block * 128 : block * 128 + 128], start)
        rows_s[pl.ds(GATHERED, PEERS, stride=STEP), :] = pack_vectors(vectors, side, spot)
        for spare in range(GATHERED + 1, TAIL):
            rows_s[pl.ds(spare, PEERS, stride=STEP), :] = jnp.zeros((PEERS, 128), F32)

        @pl.loop(0, 8)
        def _(block):
            for peer in range(8):
                group = block * 8 + peer
                first = (spot[3] + side * (spot[1] - spot[3]) - (group >> 4)) & 3
                second = (spot[1] + side * (spot[3] - spot[1]) - group) & 3
                to = first * 16 + second * 4 + ((spot[2] - (group >> 2)) & 3)
                slab_s[half, to] = rows_s[pl.ds(group * STEP, TAIL), :].astype(BF)

        store = pltpu.make_async_copy(slab_s.at[half], target, out_sems.at[half])
        store.start()
        stores.append(store)
    for store in stores:
        store.wait()


def back(spot, lens, vec, up, qkv, soft, weights, ht, x, low, mixed):
    slab = jax.ShapeDtypeStruct((PEERS, TAIL, 128), BF)
    return pl.pallas_call(
        back_kernel,
        out_shape=(slab, slab, jax.ShapeDtypeStruct((ROWS, D), F32)),
        in_specs=[SM, SM, VM, VM] + [ANY] * 7,
        out_specs=(ANY,) * 3,
        scratch_shapes=[
            pltpu.VMEM((ROWS, 3 * D), BF),
            pltpu.VMEM((6, ROWS, 1024), BF),
            pltpu.VMEM((D, 3 * D), BF),
            pltpu.VMEM((D, ROWS), BF),
            pltpu.VMEM((ROWS, D), BF),
            pltpu.VMEM((ROWS, D), BF),
            pltpu.VMEM((ROWS, D), BF),
            pltpu.VMEM((ROWS, ROWS), F32),
            pltpu.VMEM((4, ROWS, 256), F32),
            pltpu.VMEM((ROWS, 3 * D), BF),
            pltpu.VMEM((ROWS, D), F32),
            pltpu.VMEM((8, D), F32),
            pltpu.VMEM((PEERS * STEP, 128), F32),
            pltpu.VMEM((2, PEERS, TAIL, 128), BF),
            pltpu.SemaphoreType.DMA((12,)),
            pltpu.SemaphoreType.DMA((3,)),
        ],
        compiler_params=params(),
        name="back",
    )(spot, lens, vec, up, qkv, soft, weights, ht, x, low, mixed)


def feed_kernel(
    spot_ref, lens_ref, h_ref, cot_ref, late_ref, act_ref, own_ref, oth_ref, dh_ref,
    up_s, down_s, mid_in, mid_s, gup_s, gdown_s, dy_s, act_s, sems, out_sems,
):
    def load_up(chunk):
        devices = pl.ds(chunk * 32, 32)
        return pltpu.make_async_copy(late_ref.at[devices, 0:16, :], up_s.at[chunk], sems.at[chunk])

    def load_down(chunk):
        devices = pl.ds(chunk * 32, 32)
        return pltpu.make_async_copy(
            late_ref.at[devices, 16:32, :], down_s.at[chunk], sems.at[4 + chunk]
        )

    def load_mid(half):
        devices = pl.ds(half * 64, 64)
        return pltpu.make_async_copy(
            late_ref.at[devices, 32:48, :], mid_in.at[half], sems.at[8 + half]
        )

    def both_cores(source, y, rows, sem, first, second):
        return [
            pltpu.make_async_copy(source.at[0], first.at[y, :, :, rows, :], sem),
            pltpu.make_async_copy(source.at[1], second.at[:, y, :, rows, :], sem),
        ]

    def big_stores(chunk, first, second):
        copies = []
        for block in range(BLOCKS):
            lanes = slice(block * 128, block * 128 + 128)
            for grads, offset in ((gup_s, 0), (gdown_s, 16)):
                rows = slice(block * 48 + offset, block * 48 + offset + 16)
                source = grads.at[chunk, :, :, :, :, lanes]
                copies += both_cores(source, chunk, rows, out_sems.at[chunk], first, second)
        return copies

    def mid_stores(half, first, second):
        copies = []
        for block in range(BLOCKS):
            lanes = slice(block * 128, block * 128 + 128)
            rows = slice(block * 48 + 32, block * 48 + 48)
            for y in range(2):
                source = mid_s.at[half, y, :, :, :, :, lanes]
                copies += both_cores(
                    source, half * 2 + y, rows, out_sems.at[4 + half], first, second
                )
        return copies

    def send(stores, number):
        @pl.when(spot_ref[0, 0] == 0)
        def _():
            for copy in stores(number, own_ref, oth_ref):
                copy.start()

        @pl.when(spot_ref[0, 0] == 1)
        def _():
            for copy in stores(number, oth_ref, own_ref):
                copy.start()

    for chunk in range(4):
        load_up(chunk).start()
        load_down(chunk).start()
    for half in range(2):
        load_mid(half).start()
    ends = group_ends(lens_ref)

    @pl.loop(0, 4)
    def _(block):
        rows = pl.ds(pl.multiple_of(block * 128, 128), 128)
        live = (iota((128, 1), 0) + block * 128) < ends[3]
        dy_s[rows, :] = jnp.where(live, cot_ref[rows, :].astype(F32), 0.0).astype(BF)
        dh_ref[rows, :] = jnp.zeros((128, D), F32)

    def store_act(chunk):
        return pltpu.make_async_copy(act_s.at[chunk], act_ref.at[chunk], out_sems.at[6 + chunk])

    def both_ways(chunk, up, down):
        value = dot_nt(h_ref[...], up)
        square = value * value
        bend = jnp.tanh(TANH_SCALE * (value + TANH_CUBE * (value * square)))
        act = (0.5 * value * (1.0 + bend)).astype(BF)
        slope = 0.5 * (1.0 + bend) + (0.5 * TANH_SCALE) * value * (1.0 - bend * bend) * (
            1.0 + 3.0 * TANH_CUBE * square
        )
        pulled = (dot_nt(dy_s[...], down) * slope).astype(BF)
        act_s[chunk] = act
        dh_ref[...] = dh_ref[...] + dot_nn(pulled, up)
        return dot_tn(pulled, h_ref[...]), dot_tn(act, dy_s[...])

    @pl.loop(0, 4)
    def _(chunk):
        load_up(chunk).wait()
        load_down(chunk).wait()
        up_grad, down_grad = both_ways(
            chunk, up_s[chunk].reshape(ROWS, D), down_s[chunk].reshape(ROWS, D)
        )
        gup_s[chunk] = up_grad.astype(BF).reshape(2, 4, 4, 16, D)
        gdown_s[chunk] = down_grad.astype(BF).reshape(2, 4, 4, 16, D)
        send(big_stores, chunk)
        store_act(chunk).start()

    @pl.loop(0, 2)
    def _(half):
        load_mid(half).wait()
        mid = mid_in[half].astype(F32)
        up_grad, down_grad = both_ways(
            4 + half,
            mid[:, 0:8, :].reshape(ROWS, D).astype(BF),
            mid[:, 8:16, :].reshape(ROWS, D).astype(BF),
        )
        joined = jnp.concatenate(
            [up_grad.reshape(PEERS, 8, D), down_grad.reshape(PEERS, 8, D)], axis=1
        )
        mid_s[half] = joined.astype(BF).reshape(2, 2, 4, 4, 16, D)
        send(mid_stores, half)
        store_act(4 + half).start()

    for chunk in range(6):
        store_act(chunk).wait()
    for chunk in range(4):
        for copy in big_stores(chunk, own_ref, oth_ref):
            copy.wait()
    for half in range(2):
        for copy in mid_stores(half, own_ref, oth_ref):
            copy.wait()


def feed(spot, lens, h, cot, late):
    slab = jax.ShapeDtypeStruct((4, 4, 4, WHOLE, 128), BF)
    return pl.pallas_call(
        feed_kernel,
        out_shape=(
            jax.ShapeDtypeStruct((6, ROWS, ROWS), BF),
            slab,
            slab,
            jax.ShapeDtypeStruct((ROWS, D), F32),
        ),
        in_specs=[SM, SM, VM, VM, ANY],
        out_specs=(ANY, ANY, ANY, VM),
        scratch_shapes=[
            pltpu.VMEM((4, 32, 16, D), BF),
            pltpu.VMEM((4, 32, 16, D), BF),
            pltpu.VMEM((2, PEERS, 16, D), BF),
            pltpu.VMEM((2, 2, 2, 4, 4, 16, D), BF),
            pltpu.VMEM((4, 2, 4, 4, 16, D), BF),
            pltpu.VMEM((4, 2, 4, 4, 16, D), BF),
            pltpu.VMEM((ROWS, D), BF),
            pltpu.VMEM((6, ROWS, ROWS), BF),
            pltpu.SemaphoreType.DMA((10,)),
            pltpu.SemaphoreType.DMA((12,)),
        ],
        compiler_params=params(),
        name="feed",
    )(spot, lens, h, cot, late)


def output_kernel(middle_ref, act_ref, late_ref, y_ref, down_s, mid_s, acc_s, sems):
    loads = [
        pltpu.make_async_copy(
            late_ref.at[pl.ds(chunk * 32, 32), 16:32, :], down_s.at[chunk], sems.at[chunk]
        )
        for chunk in range(4)
    ] + [
        pltpu.make_async_copy(
            late_ref.at[pl.ds(half * 64, 64), 32:48, :], mid_s.at[half], sems.at[4 + half]
        )
        for half in range(2)
    ]
    for load in loads:
        load.start()
    acc_s[...] = middle_ref[...]
    for load in loads:
        load.wait()

    @pl.loop(0, 4)
    def _(chunk):
        acc_s[...] = acc_s[...] + dot_nn(act_ref[chunk], down_s[chunk].reshape(ROWS, D))

    @pl.loop(0, 2)
    def _(half):
        down = mid_s[half].astype(F32)[:, 8:16, :].reshape(ROWS, D).astype(BF)
        acc_s[...] = acc_s[...] + dot_nn(act_ref[4 + half], down)

    y_ref[...] = acc_s[...].astype(BF)


def layer_output(middle, act, late):
    return pl.pallas_call(
        output_kernel,
        out_shape=jax.ShapeDtypeStruct((ROWS, D), BF),
        in_specs=[VM, VM, ANY],
        out_specs=VM,
        scratch_shapes=[
            pltpu.VMEM((4, 32, 16, D), BF),
            pltpu.VMEM((2, PEERS, 16, D), BF),
            pltpu.VMEM((ROWS, D), F32),
            pltpu.SemaphoreType.DMA((6,)),
        ],
        compiler_params=params(),
        name="layer_output",
    )(middle, act, late)


def norm_back_kernel(x_ref, dx_ref, dh_ref, ln_ref, dtok_ref):
    @pl.loop(0, 4)
    def _(block):
        rows = pl.ds(pl.multiple_of(block * 128, 128), 128)
        unit, inverse = norm_stats(x_ref[rows, :].astype(F32))
        moved = dx_ref[rows, :] + norm_pull(dh_ref[rows, :], unit, inverse, ln_ref[0:1, :])
        dtok_ref[rows, :] = moved.astype(BF)


def norm_back(x, dx, dh, ln):
    return pl.pallas_call(
        norm_back_kernel,
        out_shape=jax.ShapeDtypeStruct((ROWS, D), BF),
        in_specs=[VM] * 4,
        out_specs=VM,
        compiler_params=params(),
        name="norm_back",
    )(x, dx, dh, ln)


def finish_kernel(slabs_ref, qkv_ref, out_ref, g1_ref, b1_ref, g2_ref, b2_ref, sum_s):
    sum_s[...] = jnp.sum(slabs_ref[...].astype(F32), axis=0)
    for pair in range(BLOCKS):
        for part in range(3):
            start = (pair * 3 + part) * OWN
            at = part * D + pair * 128
            qkv_ref[:, at : at + 128] = sum_s[start : start + OWN, :]
        start = OUTER + pair * OWN
        out_ref[:, pair * 128 : pair * 128 + 128] = sum_s[start : start + OWN, :]
    for which, target in enumerate((g1_ref, b1_ref, g2_ref, b2_ref)):
        target[...] = sum_s[GATHERED : GATHERED + 1, which * OWN : which * OWN + OWN]


def finish(slabs):
    vector = jax.ShapeDtypeStruct((1, OWN), F32)
    return pl.pallas_call(
        finish_kernel,
        out_shape=(
            jax.ShapeDtypeStruct((OWN, 3 * D), F32),
            jax.ShapeDtypeStruct((OWN, D), F32),
            vector, vector, vector, vector,
        ),
        in_specs=[VM],
        out_specs=(VM,) * 6,
        scratch_shapes=[pltpu.VMEM((TAIL, 128), F32)],
        compiler_params=params(16),
        name="finish",
    )(slabs)


def unpack_kernel(late_ref, up_ref, down_ref, sum_s):
    sum_s[...] = jnp.sum(late_ref[...].astype(F32), axis=0)
    for block in range(BLOCKS):
        lanes = slice(block * 128, block * 128 + 128)
        row = block * 48
        up_ref[0:16, lanes] = sum_s[row : row + 16, :]
        down_ref[0:16, lanes] = sum_s[row + 16 : row + 32, :]
        up_ref[16:24, lanes] = sum_s[row + 32 : row + 40, :]
        down_ref[16:24, lanes] = sum_s[row + 40 : row + 48, :]


def unpack(late):
    shard = jax.ShapeDtypeStruct((24, D), F32)
    return pl.pallas_call(
        unpack_kernel,
        out_shape=(shard, shard),
        in_specs=[VM],
        out_specs=(VM, VM),
        scratch_shapes=[pltpu.VMEM((WHOLE, 128), F32)],
        compiler_params=params(16),
        name="unpack",
    )(late)


def add_pair(own, other):
    received = lax.ppermute(other, AXES, core_pairs())
    return (own.astype(F32) + received.astype(F32)).astype(BF)


def add_kernel(left_ref, right_ref, sum_ref, left, right, total, sems):
    def copies(source, target, column):
        return [
            pltpu.make_async_copy(
                source.at[pl.ds(part * 8, 8)], target.at[pl.ds(part * 8, 8)], sems.at[part, column]
            )
            for part in range(8)
        ]

    lefts, rights = copies(left_ref, left, 0), copies(right_ref, right, 1)
    stores = copies(total, sum_ref, 2)
    for load in itertools.chain(*zip(lefts, rights)):
        load.start()
    for part in range(8):
        lefts[part].wait()
        rights[part].wait()
        at = slice(part * 8, part * 8 + 8)
        total[at] = (left[at].astype(F32) + right[at].astype(F32)).astype(BF)
        stores[part].start()
    for store in stores:
        store.wait()


def add_large_pair(own, other):
    received = lax.ppermute(other, AXES, core_pairs())
    return pl.pallas_call(
        add_kernel,
        out_shape=jax.ShapeDtypeStruct(own.shape, BF),
        in_specs=[ANY, ANY],
        out_specs=ANY,
        scratch_shapes=[pltpu.VMEM(own.shape, BF)] * 3 + [pltpu.SemaphoreType.DMA((8, 3))],
        compiler_params=params(),
        name="add_large_pair",
    )(own, received)


def scatter(slabs, rows):
    return lax.psum_scatter(
        slabs.reshape(PEERS * rows, 128),
        AXES,
        scatter_dimension=0,
        axis_index_groups=mixed_groups("y", "z"),
        tiled=True,
    )


def exchange(slabs, rows):
    return lax.all_to_all(
        slabs.reshape(16, rows, 128),
        AXES,
        0,
        0,
        axis_index_groups=mixed_groups("zx", "yx"),
        tiled=True,
    )


def shift(values, dims, ahead):
    pairs = []
    for x, y, z, c in itertools.product(range(4), range(4), range(4), range(2)):
        to = dict(x=x, y=y, z=z)
        to[dims[c]] = (to[dims[c]] + ahead) % 4
        pairs.append((device_number(x, y, z, c), device_number(to["x"], to["y"], to["z"], c)))
    return lax.ppermute(values, AXES, pairs)


def ring(own, dims):
    return jnp.concatenate([own] + [shift(own, dims, ahead) for ahead in (1, 2, 3)], axis=0)


def wide_ring(own, dims):
    half = own.shape[0] // 2
    near, last = shift(own, dims, 1), shift(own, dims, -1)
    far = [shift(near[:half], dims, 1), shift(last[half:], dims, -1)]
    return jnp.concatenate([own, near, *far, last], axis=0)


def copies_of_peers(own):
    return wide_ring(ring(ring(own, "zy"), "xx"), "yz").reshape(PEERS, *own.shape)


def on_device(
    tokens,
    seq_lengths,
    ln1_gain,
    ln1_bias,
    qkv_weight,
    out_weight,
    ln2_gain,
    ln2_bias,
    up_weight,
    down_weight,
    cotangent,
):
    wide, narrow = lax.axis_index("wide"), lax.axis_index("narrow")
    spot = jnp.stack([wide & 1, narrow & 3, (narrow >> 2) * 2 + (wide >> 3), (wide >> 1) & 3])
    spot = spot.astype(I32).reshape(1, 4)
    early, late = pack(
        ln1_gain, ln1_bias, qkv_weight, out_weight, ln2_gain, ln2_bias, up_weight.T, down_weight
    )
    late = lax.all_gather(late, AXES, axis_index_groups=peer_groups("yczx"))
    early_own = copies_of_peers(early)
    early_oth = lax.ppermute(early_own, AXES, core_pairs())
    ht, qkv, weights, norms, mixed, middle, h_two, soft = front(
        spot, seq_lengths, tokens, early_own, early_oth
    )
    act, own, oth, dh_two = feed(spot, seq_lengths, h_two, cotangent, late)
    late_grad = add_large_pair(own.reshape(PEERS, WHOLE, 128), oth.reshape(PEERS, WHOLE, 128))
    dx, low, upstream, vectors = middle_back(
        spot, seq_lengths, cotangent, middle, dh_two, norms, weights
    )
    late_grad, upstream = lax.optimization_barrier((late_grad, upstream))
    late_grad = scatter(late_grad, WHOLE)
    oth, own, dh_one = back(
        spot, seq_lengths, vectors, upstream, qkv, soft, weights, ht, tokens, low, mixed
    )
    tail, act = lax.optimization_barrier((add_pair(own, oth), act))
    tail = scatter(tail, TAIL)
    late_grad = exchange(late_grad, WHOLE)
    dtokens = norm_back(tokens, dx, dh_one, norms)
    output = layer_output(middle, act, late)
    tail, late_grad, output = lax.optimization_barrier((tail, late_grad, output))
    tail = exchange(tail, TAIL)
    up_grad, down_grad = unpack(late_grad)
    qkv_grad, out_grad, g1_grad, b1_grad, g2_grad, b2_grad = finish(tail)
    return (
        output,
        dtokens,
        g1_grad.reshape(OWN),
        b1_grad.reshape(OWN),
        qkv_grad,
        out_grad,
        g2_grad.reshape(OWN),
        b2_grad.reshape(OWN),
        up_grad.T,
        down_grad,
    )


def solution(mesh):
    rows = P(AXES, None)
    flat = P(AXES)
    columns = P(None, AXES)
    return jax.shard_map(
        on_device,
        mesh=mesh,
        in_specs=(rows, rows, flat, flat, rows, rows, flat, flat, columns, rows, rows),
        out_specs=(rows, rows, flat, flat, rows, rows, flat, flat, columns, rows),
        check_vma=False,
    )
```
